32 devices in a mesh: section: 2 (over core), mp: 4 (over z), dp: 4 (over y, x).
Axes of the slice: x: 2, y: 2, z: 4, core: 2. Of those that a mesh axis runs over, the one named last changes fastest.
Arguments:
- expression: bfloat16 [3968, 13504], P('dp', 'mp'), may hold values from -19.2 to 19.2
- cell_xy: float32 [2, 3968], P(None, 'dp'), may hold values from 0 to 100
- live_mask: int32 [3968], P('dp'), may hold values from 0 to 1, as said below
- lengths: int32 [8, 3], P('dp'), may hold values from 1 to 434, 496 in all within a row
- ramp_step: int32 [1], replicated, may hold values from 0 to 1999
- latent_noise: float32 [3968, 512], P('dp', 'mp'), may hold values from -7.5 to 7.5
- gene_embed: bfloat16 [13504, 1024], P('mp', ('section', 'dp')), may hold values from -0.0546875 to 0.0546875
- ln1_gain: bfloat16 [1024], P(('section', 'dp')), may hold values from 0.5 to 1.5
- ln1_bias: bfloat16 [1024], P(('section', 'dp')), may hold values from -1.5 to 1.5
- w_query: bfloat16 [1024, 1024], P(('section', 'dp'), 'mp'), may hold values from -0.25 to 0.25
- w_key: bfloat16 [1024, 1024], P(('section', 'dp'), 'mp'), may hold values from -0.25 to 0.25
- w_value: bfloat16 [1024, 1024], P(('section', 'dp'), 'mp'), may hold values from -0.1875 to 0.1875
- w_out: bfloat16 [1024, 1024], P('mp', ('section', 'dp')), may hold values from -0.75 to 0.75
- ln2_gain: bfloat16 [1024], P(('section', 'dp')), may hold values from 0.5 to 1.5
- ln2_bias: bfloat16 [1024], P(('section', 'dp')), may hold values from -1.5 to 1.5
- w_up: bfloat16 [1024, 4096], P(('section', 'dp'), 'mp'), may hold values from -0.1875 to 0.1875
- w_down: bfloat16 [4096, 1024], P('mp', ('section', 'dp')), may hold values from -0.09375 to 0.09375
- w_mean: bfloat16 [1024, 512], P(('section', 'dp'), 'mp'), may hold values from -0.1875 to 0.1875
- w_logvar: bfloat16 [1024, 512], P(('section', 'dp'), 'mp'), may hold values from -0.09375 to 0.09375
- comp_mean: bfloat16 [16, 512], P(None, ('mp', 'section', 'dp')), may hold values from -4 to 4
- comp_logvar: bfloat16 [16, 512], P(None, ('mp', 'section', 'dp')), may hold values from -0.5 to 0.5
- w_dec: bfloat16 [512, 1024], P('mp', ('section', 'dp')), may hold values from -0.25 to 0.25
- w_genes: bfloat16 [1024, 13504], P(('section', 'dp'), 'mp'), may hold values from -0.1875 to 0.1875
Outputs:
- grad_gene_embed: float32 [13504, 1024], P('mp', ('section', 'dp'))
- grad_ln1_gain: float32 [1024], P(('section', 'dp'))
- grad_ln1_bias: float32 [1024], P(('section', 'dp'))
- grad_query: float32 [1024, 1024], P(('section', 'dp'), 'mp')
- grad_key: float32 [1024, 1024], P(('section', 'dp'), 'mp')
- grad_value: float32 [1024, 1024], P(('section', 'dp'), 'mp')
- grad_out: float32 [1024, 1024], P('mp', ('section', 'dp'))
- grad_ln2_gain: float32 [1024], P(('section', 'dp'))
- grad_ln2_bias: float32 [1024], P(('section', 'dp'))
- grad_up: float32 [1024, 4096], P(('section', 'dp'), 'mp')
- grad_down: float32 [4096, 1024], P('mp', ('section', 'dp'))
- grad_mean: float32 [1024, 512], P(('section', 'dp'), 'mp')
- grad_logvar: float32 [1024, 512], P(('section', 'dp'), 'mp')
- grad_comp_mean: float32 [16, 512], P(None, ('mp', 'section', 'dp'))
- grad_comp_logvar: float32 [16, 512], P(None, ('mp', 'section', 'dp'))
- grad_dec: float32 [512, 1024], P('mp', ('section', 'dp'))
- grad_genes: float32 [1024, 13504], P(('section', 'dp'), 'mp')
- grad_expression: bfloat16 [3968, 13504], P('dp', 'mp')
The draws below stay inside these ranges and needn't reach their ends.
Inputs may be any that keep to these rules, and one draw needn't show every extreme that they name: `live_mask`: 1 marks a kept cell; the first cell of each buffer of 496 cells is kept. Row b gives the lengths of the 3 slides of buffer b in order; each row sums to 496.
All inputs are finite; a program needn't handle non-finite values.
Results may differ from the reference program's by a relative error of at most 0.03.
Values may be sent and summed in bfloat16 or wider, within the bound.
A program may use at most 256 MiB of HBM per device.

```python
import math
import jax
import jax.numpy as jnp
import numpy as np
from jax import lax

D = 1024
HEADS = 16
HEAD = 64
FF = 4096
GENES = 13504
LATENT = 512
COMPS = 16
CAP = 496
MICRO = 2
SLIDES = 3
MOST = 434
RAMP = 1000
BUFFERS = 8
CELLS = 3968
N_DP = 4


def draw_expression(key, part):
    key = jax.random.fold_in(key, 5)
    rows = jnp.arange(CELLS, dtype=jnp.float32) / CELLS
    base = jnp.clip(jax.random.normal(key, (CELLS, GENES), jnp.float32), -6.0, 6.0)
    scale = 0.4 * jnp.exp(rows * math.log(8.0))
    return (base * scale[:, None]).astype(jnp.bfloat16)


def draw_latent_noise(key, part):
    key = jax.random.fold_in(key, 17)
    columns = 0.5 + jnp.arange(LATENT, dtype=jnp.float32) / LATENT
    base = jnp.clip(jax.random.normal(key, (CELLS, LATENT), jnp.float32), -5.0, 5.0)
    return (base * columns[None, :]).astype(jnp.float32)


def draw_live_mask(key, part):
    key = jax.random.fold_in(key, 11)
    picks = jax.random.randint(key, (CELLS,), 0, 1000)
    index = jnp.arange(CELLS, dtype=jnp.int32)
    limit = 300 + index * 650 // CELLS
    leading = index % CAP == 0
    return jnp.where(leading, 1, (picks < limit).astype(jnp.int32)).astype(jnp.int32)


def block_scale(stream_key, shape, pieces, low, high):
    level = 1.0
    for dim, shards_of in pieces:
        steps = jax.random.uniform(jax.random.fold_in(jax.random.fold_in(stream_key, 6), dim), (shards_of,), jnp.float32, low / len(pieces), high / len(pieces))
        level = level * jnp.repeat(jnp.exp(steps), shape[dim] // shards_of).reshape((-1,) + (1,) * (len(shape) - 1 - dim))
    return level


def length_profile(count, total, most, slope):
    weights = [(1 << 20) // math.isqrt(standing ** slope) + 1 for standing in range(2, count + 1)]
    spare, holding = total - most - (count - 1), [1] * (count - 1)
    while spare > 0:
        movable = [i for i in range(count - 1) if holding[i] < most]
        mass, left = sum([weights[i] for i in movable]), spare
        for i in movable:
            extra = min(most - holding[i], max(1, left * weights[i] // mass), spare)
            holding[i] = holding[i] + extra
            spare = spare - extra
    return np.array([most] + holding)


def ragged(own_key, number_of, total, bound, lean):
    if number_of == 2:
        one = jax.random.randint(own_key, (), max(1, total - bound), min(bound, total - 1) + 1)
        return jnp.stack([one, total - one])
    sizes = jnp.asarray(length_profile(number_of, total, bound, lean), jnp.int32)
    twos = (number_of - 1) // 2
    source_of, taker = sizes[1:1 + 2 * twos:2], sizes[2:2 + 2 * twos:2]
    slack = jnp.minimum(source_of - 1, bound - taker)
    passed = jax.random.randint(jax.random.fold_in(own_key, 1), (twos,), 0, 1 << 20) % (slack + 1)
    sizes = sizes.at[1:1 + 2 * twos:2].set(source_of - passed).at[2:2 + 2 * twos:2].set(taker + passed)
    return sizes[jax.random.permutation(jax.random.fold_in(own_key, 2), number_of)]


def noise(key, shape, spread, reach, cuts=(), kind=jnp.bfloat16):
    values = jax.random.normal(key, shape, jnp.float32) * spread
    if len(cuts) > 0:
        values = block_scale(key, shape, cuts, -0.22, 0.18) * values
    return jnp.clip(values, min=-reach, max=reach).astype(kind)


def setup_inputs(seed: int = 0) -> dict:
    seeds = jax.random.split(jax.random.key(seed), 24)
    return {
        "expression": draw_expression(jax.random.fold_in(seeds[23], 71), 0),
        "cell_xy": jnp.clip(100.0 * jax.random.uniform(seeds[1], (2, CELLS), jnp.float32) ** block_scale(seeds[1], (2, CELLS), ((1, 4),), -0.2, 0.2), 0.0, 100.0),
        "live_mask": draw_live_mask(jax.random.fold_in(seeds[23], 71), 0),
        "lengths": jax.vmap(lambda own: ragged(own, SLIDES, CAP, MOST, 0))(jax.random.split(seeds[3], BUFFERS)).reshape((BUFFERS, SLIDES)).astype(jnp.int32),
        "ramp_step": jax.random.randint(seeds[4], (1,), 0, 2 * RAMP).astype(jnp.int32),
        "latent_noise": draw_latent_noise(jax.random.fold_in(seeds[23], 71), 0),
        "gene_embed": noise(seeds[6], (GENES, D), GENES ** -0.5, 0.0546875, ((0, 4), (1, 8))),
        "ln1_gain": jnp.clip(1.0 + 0.1 * jax.random.normal(seeds[7], (D,), jnp.float32), 0.5, 1.5).astype(jnp.bfloat16),
        "ln1_bias": noise(seeds[8], (D,), 0.3, 1.5, ((0, 8),)),
        "w_query": noise(seeds[9], (D, D), (D // 2) ** -0.5, 0.25, ((0, 8), (1, 4))),
        "w_key": noise(seeds[10], (D, D), (D // 2) ** -0.5, 0.25, ((0, 8), (1, 4))),
        "w_value": noise(seeds[11], (D, D), D ** -0.5, 0.1875, ((0, 8), (1, 4))),
        "w_out": noise(seeds[12], (D, D), (D // 16) ** -0.5, 0.75, ((0, 4), (1, 8))),
        "ln2_gain": jnp.clip(1.0 + 0.1 * jax.random.normal(seeds[13], (D,), jnp.float32), 0.5, 1.5).astype(jnp.bfloat16),
        "ln2_bias": noise(seeds[14], (D,), 0.3, 1.5, ((0, 8),)),
        "w_up": noise(seeds[15], (D, FF), D ** -0.5, 0.1875, ((0, 8), (1, 4))),
        "w_down": noise(seeds[16], (FF, D), FF ** -0.5, 0.09375, ((0, 4), (1, 8))),
        "w_mean": noise(seeds[17], (D, LATENT), D ** -0.5, 0.1875, ((0, 8), (1, 4))),
        "w_logvar": noise(seeds[18], (D, LATENT), (4 * D) ** -0.5, 0.09375, ((0, 8), (1, 4))),
        "comp_mean": noise(seeds[19], (COMPS, LATENT), 1.0, 4.0, ((1, 32),)),
        "comp_logvar": jnp.clip(jax.random.uniform(seeds[20], (COMPS, LATENT), jnp.float32, -0.5, 0.5) * block_scale(seeds[20], (COMPS, LATENT), ((1, 32),), -0.4, 0.0), -0.5, 0.5).astype(jnp.bfloat16),
        "w_dec": noise(seeds[21], (LATENT, D), LATENT ** -0.5, 0.25, ((0, 4), (1, 8))),
        "w_genes": noise(seeds[22], (D, GENES), D ** -0.5, 0.1875, ((0, 8), (1, 4))),
    }


@jax.custom_vjp
def low(v):
    return lax.optimization_barrier(v.astype(jnp.bfloat16)).astype(jnp.float32)

@jax.custom_vjp
def low_back(v):
    return v

def low_keep(v):
    return (low(v), None)

def low_pass(kept, grad):
    return (grad,)

def back_keep(v):
    return (v, None)

def back_low(kept, grad):
    return (low(grad),)
low.defvjp(low_keep, low_pass)
low_back.defvjp(back_keep, back_low)
LOG_TWO_PI = 1.8378770664093453
NEG_LARGE = -1e+30
FREE_BITS = 1.0

def high_dot(left, right):
    return jnp.dot(left, right, precision=lax.Precision.HIGHEST, preferred_element_type=jnp.float32)

def layer_norm(values, gain, offset):
    center = values - lax.optimization_barrier(jnp.mean(values, axis=-1, keepdims=True))
    scale = lax.rsqrt(lax.optimization_barrier(jnp.mean(center * center, axis=-1, keepdims=True)) + 1e-05)
    return center * scale * gain + offset

def position_code(places, feature_count):
    quarter = feature_count // 4
    frequency = jnp.exp(jnp.arange(quarter, dtype=jnp.float32) * (-math.log(10000.0) / quarter))
    along_x = places[0][:, None] * frequency[None, :]
    along_y = places[1][:, None] * frequency[None, :]
    return jnp.concatenate([jnp.sin(along_x), jnp.cos(along_x), jnp.sin(along_y), jnp.cos(along_y)], axis=1)

def slide_ids(length_row, cell_count):
    bounds = jnp.cumsum(length_row.astype(jnp.int32))[:-1].astype(jnp.int32)
    cell_index = jnp.arange(cell_count, dtype=jnp.int32)
    return lax.optimization_barrier(jnp.sum((cell_index[:, None] >= bounds[None, :]).astype(jnp.int32), axis=1)).astype(jnp.int32)

def first_section(gene_rows, places, slide_now, alive_now, params):
    embed_w, gain_one, bias_one, query_w, key_w, value_w, out_w, gain_two, bias_two, up_w, down_w = params
    embedded = low_back(high_dot(low_back(gene_rows), embed_w))
    start = embedded + position_code(places, D)
    normed = low(layer_norm(start, gain_one, bias_one))
    queries = low(low_back(high_dot(normed, query_w))).reshape(CAP, HEADS, HEAD)
    keys_now = low(low_back(high_dot(normed, key_w))).reshape(CAP, HEADS, HEAD)
    values_now = low(low_back(high_dot(normed, value_w))).reshape(CAP, HEADS, HEAD)
    scores = low_back(jnp.einsum('qhd,khd->hqk', queries, keys_now, precision=lax.Precision.HIGHEST) * HEAD ** (-0.5))
    cell_index = jnp.arange(CAP, dtype=jnp.int32)
    allowed = (slide_now[:, None] == slide_now[None, :]) & ((alive_now[None, :] == 1) | (cell_index[:, None] == cell_index[None, :]))
    scores = jnp.where(allowed[None], scores, NEG_LARGE)
    probs_all = jax.nn.softmax(scores, axis=-1)
    attended = jnp.einsum('hqk,khd->qhd', low(probs_all), values_now, precision=lax.Precision.HIGHEST).reshape(CAP, D)
    attended = low(low_back(attended))
    after_attn = start + low_back(high_dot(attended, out_w))
    normed_two = low(layer_norm(after_attn, gain_two, bias_two))
    upper = low_back(high_dot(normed_two, up_w))
    activated = low(jax.nn.gelu(upper, approximate=False))
    result = after_attn + low_back(high_dot(activated, down_w))
    return low(low_back(result))

def second_section(hidden, gene_rows, noise_rows, alive_float, params):
    mean_w, logvar_w, centers, comp_logs, dec_w, genes_w = params
    means = low_back(high_dot(hidden, mean_w))
    log_vars = low_back(high_dot(hidden, logvar_w))
    latent = means + jnp.exp(0.5 * log_vars) * noise_rows
    log_post = lax.optimization_barrier(jnp.sum(-0.5 * LOG_TWO_PI - 0.5 * log_vars - 0.5 * noise_rows * noise_rows, axis=1))
    offsets = latent[None] - centers[:, None, :]
    terms = lax.optimization_barrier(jnp.sum(-0.5 * LOG_TWO_PI - 0.5 * comp_logs[:, None, :] - 0.5 * offsets * offsets * jnp.exp(-comp_logs)[:, None, :], axis=2)) - math.log(COMPS)
    log_prior = jax.scipy.special.logsumexp(terms, axis=0)
    decoder_pre = low_back(high_dot(low(latent), dec_w))
    decoder_act = low(jax.nn.gelu(decoder_pre, approximate=False))
    rebuilt = low_back(high_dot(decoder_act, genes_w))
    residual = rebuilt - low_back(gene_rows)
    rebuild_loss = 0.5 * jnp.sum(alive_float[:, None] * residual * residual)
    return (rebuild_loss, log_post - log_prior)

def reference(expression, cell_xy, live_mask, lengths, ramp_step, latent_noise, gene_embed, ln1_gain, ln1_bias, w_query, w_key, w_value, w_out, ln2_gain, ln2_bias, w_up, w_down, w_mean, w_logvar, comp_mean, comp_logvar, w_dec, w_genes):
    weight_list = (gene_embed, ln1_gain, ln1_bias, w_query, w_key, w_value, w_out, ln2_gain, ln2_bias, w_up, w_down, w_mean, w_logvar, comp_mean, comp_logvar, w_dec, w_genes)
    params = tuple((item.astype(jnp.float32) for item in weight_list))
    genes_float = expression.astype(jnp.float32)
    buffer_count = N_DP * MICRO
    place_all = cell_xy.reshape(2, buffer_count, CAP).transpose(1, 0, 2)
    alive_all = live_mask.reshape(buffer_count, CAP)
    noise_all = latent_noise.reshape(buffer_count, CAP, LATENT)
    live_total = jnp.sum(live_mask.astype(jnp.float32))
    ramp_weight = jnp.minimum(1.0, (ramp_step[0] + 1).astype(jnp.float32) / RAMP)

    def total_loss(genes_in, params_in):
        genes_all = genes_in.reshape(buffer_count, CAP, GENES)

        def scan_step(running, packed):
            gene_rows, places, length_row, alive_rows, noise_rows = packed
            slide_now = slide_ids(length_row, CAP)
            handed = first_section(gene_rows, places, slide_now, alive_rows, params_in[:11])
            rebuild_loss, divergence = second_section(handed, gene_rows, noise_rows, alive_rows.astype(jnp.float32), params_in[11:])
            return (running + rebuild_loss, divergence)
        rebuild_total, divergence_all = lax.scan(jax.checkpoint(scan_step), jnp.zeros((), jnp.float32), (genes_all, place_all, lengths, alive_all, noise_all))
        mean_kl = jnp.sum(divergence_all * alive_all.astype(jnp.float32)) / (LATENT * live_total)
        soft_part = jax.nn.softplus(mean_kl - FREE_BITS)
        return rebuild_total + ramp_weight * live_total * LATENT * (FREE_BITS + 0.5 * soft_part * soft_part)
    loss_value, pull_back = jax.vjp(total_loss, genes_float, params)
    grad_input, grad_params = pull_back(jnp.ones_like(loss_value))
    return (grad_params[0], grad_params[1], grad_params[2], grad_params[3], grad_params[4], grad_params[5], grad_params[6], grad_params[7], grad_params[8], grad_params[9], grad_params[10], grad_params[11], grad_params[12], grad_params[13], grad_params[14], grad_params[15], grad_params[16], grad_input.astype(jnp.bfloat16))
```

```python
import functools
import math

import jax
import jax.numpy as jnp
from jax import lax
from jax.experimental import pallas as pl
from jax.experimental.pallas import tpu as pltpu
from jax.sharding import PartitionSpec as P

HEAD = 64
LATENT = 512
RAMP = 1000
LOG_TWO_PI = 1.8378770664093453
NEG_LARGE = -1e30
FREE_BITS = 1.0
HOP_LAG = 3
F32 = jnp.float32
BF16 = jnp.bfloat16


def mat_nn(left, right):
    return jnp.dot(left, right, preferred_element_type=F32)


def mat_tn(left, right):
    return lax.dot_general(left, right, (((0,), (0,)), ((), ())), preferred_element_type=F32)


def mat_nt(left, right):
    return lax.dot_general(left, right, (((1,), (1,)), ((), ())), preferred_element_type=F32)


def gelu(values):
    return 0.5 * values * (1.0 + lax.erf(values * 0.7071067811865476))


def gelu_slope(values):
    return (
        0.5 * (1.0 + lax.erf(values * 0.7071067811865476))
        + values * jnp.exp(-0.5 * values * values) * 0.3989422804014327
    )


def normalize(values):
    center = values - jnp.mean(values, axis=-1, keepdims=True)
    scale = lax.rsqrt(jnp.mean(center * center, axis=-1, keepdims=True) + 1e-05)
    return center * scale, scale


def norm_back(grad_in, normed, scale, gain):
    scaled = grad_in * gain
    return scale * (
        scaled
        - jnp.mean(scaled, axis=-1, keepdims=True)
        - normed * jnp.mean(scaled * normed, axis=-1, keepdims=True)
    )


def position_code(places, feature_count):
    quarter = feature_count // 4
    frequency = jnp.exp(jnp.arange(quarter, dtype=F32) * (-math.log(10000.0) / quarter))
    along_x = places[0][:, None] * frequency[None, :]
    along_y = places[1][:, None] * frequency[None, :]
    return jnp.concatenate(
        [jnp.sin(along_x), jnp.cos(along_x), jnp.sin(along_y), jnp.cos(along_y)], axis=1
    )


def allowed_pairs(length_row, alive):
    cell_count = alive.shape[0]
    bounds = jnp.cumsum(length_row)[:-1]
    index = jnp.arange(cell_count, dtype=jnp.int32)
    slide = jnp.sum((index[:, None] >= bounds[None, :]).astype(jnp.int32), axis=1)
    return (slide[:, None] == slide[None, :]) & (
        (alive[None, :] == 1) | (index[:, None] == index[None, :])
    )


def heads_of(array):
    return array.reshape(array.shape[0], -1, HEAD)


def attend(queries, keys, values, allowed):
    factor = HEAD ** (-0.5)
    scores = (
        jnp.einsum("qhd,khd->hqk", heads_of(queries), heads_of(keys), preferred_element_type=F32)
        * factor
    )
    scores = jnp.where(allowed[None], scores, NEG_LARGE)
    largest = jnp.max(scores, axis=2, keepdims=True)
    exponents = jnp.exp(scores - largest)
    sums = jnp.sum(exponents, axis=2, keepdims=True)
    probs = (exponents / sums).astype(BF16)
    out = jnp.einsum("hqk,khd->qhd", probs, heads_of(values), preferred_element_type=F32)
    return out.reshape(queries.shape).astype(BF16), largest + jnp.log(sums)


def attend_back(queries, keys, values, grad_out, log_totals, allowed):
    factor = HEAD ** (-0.5)
    q, k, v, g = heads_of(queries), heads_of(keys), heads_of(values), heads_of(grad_out)
    scores = jnp.einsum("qhd,khd->hqk", q, k, preferred_element_type=F32) * factor
    probs = jnp.where(allowed[None], jnp.exp(jnp.minimum(scores - log_totals, 0.0)), 0.0)
    grad_values = jnp.einsum("hqk,qhd->khd", probs.astype(BF16), g, preferred_element_type=F32)
    grad_probs = jnp.einsum("qhd,khd->hqk", g, v, preferred_element_type=F32)
    inner = jnp.sum(probs * grad_probs, axis=2, keepdims=True)
    grad_scores = (probs * (grad_probs - inner)).astype(BF16)
    grad_query = jnp.einsum("hqk,khd->qhd", grad_scores, k, preferred_element_type=F32) * factor
    grad_keys = jnp.einsum("hqk,qhd->khd", grad_scores, q, preferred_element_type=F32) * factor
    return tuple(
        item.reshape(queries.shape).astype(BF16) for item in (grad_query, grad_keys, grad_values)
    )


def part_of(ref, axis, index, size):
    span = pl.ds(index * size, size)
    if axis == 0:
        return ref.at[span, :]
    return ref.at[:, pl.ds(pl.multiple_of(index * size, 128), size)]


def line_sum(part, out, from_left, from_right, to_right, to_left, got_left, got_right, sent_right, sent_left):
    me, count = lax.axis_index("mp"), lax.axis_size("mp")
    pieces, _, width = from_left.shape
    inner_right, inner_left = me < count - 1, me > 0

    def columns(piece):
        return pl.ds(pl.multiple_of(piece * width, width), width)

    def flow(piece, has_source, has_target, source, target, arrived, left, neighbour):
        copy = pltpu.make_async_remote_copy(
            src_ref=target.at[piece],
            dst_ref=source.at[piece],
            send_sem=left.at[piece],
            recv_sem=arrived.at[piece],
            device_id={"mp": neighbour},
        )

        def advance():
            @pl.when(has_source)
            def _():
                copy.wait_recv()

            @pl.when(has_target)
            def _():
                target[piece] = (
                    part[:, columns(piece)] + source[piece].astype(F32)
                ).astype(BF16)
                copy.start()

        return copy, advance

    def rightward(piece):
        return flow(
            piece, inner_left, inner_right, from_left, to_right, got_left, sent_right, me + 1
        )

    def leftward(piece):
        return flow(
            piece, inner_right, inner_left, from_right, to_left, got_right, sent_left, me - 1
        )

    def start():
        @pl.when(me == 0)
        def _():
            from_left[...] = jnp.zeros_like(from_left)

        @pl.when(me == count - 1)
        def _():
            from_right[...] = jnp.zeros_like(from_right)

        def step(moment, carry):
            right_piece = moment - HOP_LAG * me
            left_piece = moment - HOP_LAG * (count - 1 - me)

            @pl.when((right_piece >= 0) & (right_piece < pieces))
            def _():
                rightward(right_piece)[1]()

            @pl.when((left_piece >= 0) & (left_piece < pieces))
            def _():
                leftward(left_piece)[1]()

            return carry

        lax.fori_loop(0, pieces + HOP_LAG * (count - 1), step, 0)

    def finish():
        def step(piece, carry):
            out[:, columns(piece)] = (
                part[:, columns(piece)]
                + from_left[piece].astype(F32)
                + from_right[piece].astype(F32)
            )

            @pl.when(inner_right)
            def _():
                rightward(piece)[0].wait_send()

            @pl.when(inner_left)
            def _():
                leftward(piece)[0].wait_send()

            return carry

        lax.fori_loop(0, pieces, step, 0)

    return start, finish


def comm_kernel(plan, *refs):
    refs = list(refs)

    def take(number):
        taken = refs[:number]
        del refs[:number]
        return taken

    reduces, gathers, swaps, exchanges, shares, pairs = plan
    sources = [take(n) for n in (reduces, len(gathers), len(swaps), len(exchanges), shares, pairs)]
    results = [take(n) for n in (reduces, len(gathers), len(swaps), len(exchanges), shares, pairs)]
    line = take(8) if reduces else None
    sent, got, local_sem = refs

    section, z, dp = (lax.axis_index(name) for name in ("section", "mp", "dp"))
    count_z, count_dp = lax.axis_size("mp"), lax.axis_size("dp")
    row, col = dp // 2, dp % 2
    peers = [row * 2 + (1 - col), (1 - row) * 2 + col, (1 - row) * 2 + (1 - col)]
    partner = {"section": 1 - section}

    barrier = pltpu.get_barrier_semaphore()
    fixed = 0
    if gathers or swaps or pairs:
        pl.semaphore_signal(barrier, inc=1, device_id=partner)
        fixed += 1
    if gathers or exchanges:
        for peer in peers:
            pl.semaphore_signal(barrier, inc=1, device_id={"dp": peer})
        fixed += len(peers)
    if shares:
        for step in range(1, count_z):
            pl.semaphore_signal(barrier, inc=1, device_id={"mp": (z + step) % count_z})
        fixed += count_z - 1
    elif reduces:
        for exists, neighbour in ((z > 0, z - 1), (z < count_z - 1, z + 1)):

            @pl.when(exists)
            def _(neighbour=neighbour):
                pl.semaphore_signal(barrier, inc=1, device_id={"mp": neighbour})

        at_end = (z == 0) | (z == count_z - 1)

        @pl.when(at_end)
        def _():
            pl.semaphore_wait(barrier, fixed + 1)

        @pl.when(jnp.logical_not(at_end))
        def _():
            pl.semaphore_wait(barrier, fixed + 2)

    if fixed and (shares or not reduces):
        pl.semaphore_wait(barrier, fixed)

    used = [0, 0]

    def remote(src, dst, device):
        index = used[0]
        used[0] += 1
        return pltpu.make_async_remote_copy(
            src_ref=src, dst_ref=dst, send_sem=sent.at[index], recv_sem=got.at[index], device_id=device
        )

    def within(src, dst):
        index = used[1]
        used[1] += 1
        return pltpu.make_async_copy(src, dst, local_sem.at[index])

    first, relays, locals_ = [], [], []
    for item, (axis, size) in enumerate(swaps):
        src, dst = sources[2][item], results[2][item]
        first.append(remote(part_of(src, axis, 1 - section, size), dst, partner))
    for item, (axis, size) in enumerate(gathers):
        src, dst = sources[1][item], results[1][item]
        mine = section * count_dp + dp
        locals_.append(within(src, part_of(dst, axis, mine, size)))
        first.append(remote(src, part_of(dst, axis, mine, size), partner))
    for item in range(shares):
        src, dst = sources[4][item], results[4][item]
        locals_.append(within(src, dst.at[z]))
        for step in range(1, count_z):
            first.append(remote(src, dst.at[z], {"mp": (z + step) % count_z}))
    for item in range(pairs):
        src, dst = sources[5][item], results[5][item]
        rows = src.shape[0]
        locals_.append(within(src, part_of(dst, 0, section, rows)))
        first.append(remote(src, part_of(dst, 0, section, rows), partner))
    for peer in peers:
        for item, (axis, size) in enumerate(gathers):
            src, dst = sources[1][item], results[1][item]
            mine = section * count_dp + dp
            copy = remote(src, part_of(dst, axis, mine, size), {"dp": peer})
            held = part_of(dst, axis, section * count_dp + peer, size)
            first.append(copy)
            relays.append((copy, remote(held, held, partner)))
        for item, (axis, size) in enumerate(exchanges):
            src, dst = sources[3][item], results[3][item]
            first.append(remote(part_of(src, axis, peer, size), dst.at[dp], {"dp": peer}))
    for item, (axis, size) in enumerate(exchanges):
        src, dst = sources[3][item], results[3][item]
        locals_.append(within(part_of(src, axis, dp, size), dst.at[dp]))

    for copy in first + locals_:
        copy.start()
    if reduces:
        start, finish = line_sum(sources[0][0], results[0][0], *line)
        start()
    for copy, relay in relays:
        copy.wait_recv()
        relay.start()
    if reduces:
        finish()
    relayed = [copy for copy, _ in relays]
    for copy in first:
        copy.wait_send()
        if not any(copy is other for other in relayed):
            copy.wait_recv()
    for _, relay in relays:
        relay.wait()
    for copy in locals_:
        copy.wait()


def comm(number, reduce=None, gathers=(), swaps=(), exchanges=(), shares=(), pairs=()):
    count_dp, count_z = lax.axis_size("dp"), lax.axis_size("mp")
    sections = lax.axis_size("section")

    def resized(shape, axis, size):
        return shape[:axis] + (size,) + shape[axis + 1 :]

    inputs, outputs, scratch = [], [], []
    plan_gathers, plan_swaps, plan_exchanges = [], [], []
    remote_count = local_count = 0
    if reduce is not None:
        rows, width = reduce.shape
        inputs.append(reduce)
        outputs.append(jax.ShapeDtypeStruct((rows, width), F32))
        buffer = pltpu.VMEM((width // 128, rows, 128), BF16)
        scratch += [buffer] * 4 + [pltpu.SemaphoreType.DMA((width // 128,))] * 4
    for shard, axis in gathers:
        size = shard.shape[axis]
        inputs.append(shard)
        outputs.append(
            jax.ShapeDtypeStruct(resized(shard.shape, axis, size * sections * count_dp), shard.dtype)
        )
        plan_gathers.append((axis, size))
        remote_count += 1 + 2 * (count_dp - 1)
        local_count += 1
    for array, axis in swaps:
        size = array.shape[axis] // sections
        inputs.append(array)
        outputs.append(jax.ShapeDtypeStruct(resized(array.shape, axis, size), array.dtype))
        plan_swaps.append((axis, size))
        remote_count += 1
    for array, axis in exchanges:
        size = array.shape[axis] // count_dp
        inputs.append(array)
        outputs.append(
            jax.ShapeDtypeStruct((count_dp,) + resized(array.shape, axis, size), array.dtype)
        )
        plan_exchanges.append((axis, size))
        remote_count += count_dp - 1
        local_count += 1
    for array in shares:
        inputs.append(array)
        outputs.append(jax.ShapeDtypeStruct((count_z,) + array.shape, array.dtype))
        remote_count += count_z - 1
        local_count += 1
    for array in pairs:
        inputs.append(array)
        outputs.append(
            jax.ShapeDtypeStruct(resized(array.shape, 0, array.shape[0] * sections), array.dtype)
        )
        remote_count += 1
        local_count += 1
    reduces = 0 if reduce is None else 1
    scratch += [
        pltpu.SemaphoreType.DMA((max(remote_count, 1),)),
        pltpu.SemaphoreType.DMA((max(remote_count, 1),)),
        pltpu.SemaphoreType.DMA((max(local_count, 1),)),
    ]
    plan = (reduces, tuple(plan_gathers), tuple(plan_swaps), tuple(plan_exchanges), len(shares), len(pairs))
    vmem, anywhere = pl.BlockSpec(memory_space=pltpu.VMEM), pl.BlockSpec(memory_space=pl.ANY)
    outs = pl.pallas_call(
        functools.partial(comm_kernel, plan),
        out_shape=outputs,
        in_specs=[vmem] * reduces + [anywhere] * (len(inputs) - reduces),
        out_specs=[vmem] * reduces + [anywhere] * (len(inputs) - reduces),
        scratch_shapes=scratch,
        compiler_params=pltpu.CompilerParams(
            collective_id=number, has_side_effects=True, vmem_limit_bytes=48 * 2**20
        ),
        cost_estimate=pl.CostEstimate(flops=1000000, bytes_accessed=90000000, transcendentals=0),
        name="meet",
    )(*inputs)
    outs = list(outs)
    split = []
    for number_of in (reduces, len(gathers), len(swaps), len(exchanges), len(shares), len(pairs)):
        split.append(outs[:number_of])
        outs = outs[number_of:]
    return split


def meet(tiled, number, reduce=None, gathers=(), swaps=(), exchanges=(), shares=(), pairs=()):
    if tiled:
        return comm(number, reduce, gathers, swaps, exchanges, shares, pairs)
    partner = [(i, 1 - i) for i in range(2)]
    section, count_dp = lax.axis_index("section"), lax.axis_size("dp")
    swapped = []
    for array, axis in swaps:
        size = array.shape[axis] // 2
        half = lax.dynamic_slice_in_dim(array, (1 - section) * size, size, axis)
        swapped.append(lax.ppermute(half, "section", partner))
    exchanged = [
        lax.all_to_all(jnp.stack(jnp.split(array, count_dp, axis)), "dp", 0, 0)
        for array, axis in exchanges
    ]
    return [
        [] if reduce is None else comm(number, reduce)[0][0:1],
        [lax.all_gather(shard, ("section", "dp"), axis=axis, tiled=True) for shard, axis in gathers],
        swapped,
        exchanged,
        [lax.all_gather(array, "mp") for array in shares],
        [lax.all_gather(array, "section", axis=0, tiled=True) for array in pairs],
    ]


def half_sum(array, received, axis):
    size = received.shape[axis]
    own = lax.dynamic_slice_in_dim(array, lax.axis_index("section") * size, size, axis)
    return (own.astype(F32) + received.astype(F32)).astype(array.dtype)


def total(parts):
    return jnp.sum(parts.astype(F32), axis=0)


def local(
    expression,
    cell_xy,
    live_mask,
    lengths,
    ramp_step,
    latent_noise,
    gene_embed,
    ln1_gain,
    ln1_bias,
    w_query,
    w_key,
    w_value,
    w_out,
    ln2_gain,
    ln2_bias,
    w_up,
    w_down,
    w_mean,
    w_logvar,
    comp_mean,
    comp_logvar,
    w_dec,
    w_genes,
):
    micro_count = lengths.shape[0]
    cells = expression.shape[0] // micro_count
    micro = lax.axis_index("section")
    latent_cols = w_mean.shape[1]
    comp_count, comp_width = comp_mean.shape
    width = ln1_gain.shape[0]
    shards = 2 * lax.axis_size("dp")
    features = shards * width
    gene_cols = expression.shape[1]
    tiled = width % 128 == 0 and lax.axis_size("dp") == 4
    meeting = functools.partial(meet, tiled)

    def own(array, axis=0):
        return lax.dynamic_slice_in_dim(array, micro * cells, cells, axis)

    genes_in = own(expression)
    alive = own(live_mask)
    alive_float = alive.astype(F32)
    noise = own(latent_noise)
    allowed = allowed_pairs(lax.dynamic_index_in_dim(lengths, micro, 0, False), alive)
    positions = position_code(own(cell_xy, 1), features)

    norm_block = jnp.pad(jnp.stack([ln1_gain, ln1_bias, ln2_gain, ln2_bias]), ((0, 12), (0, 0)))
    comp_block = jnp.pad(
        jnp.concatenate([comp_mean, comp_logvar], axis=0), ((0, 0), (0, width - comp_width))
    )
    small = jnp.concatenate([norm_block, comp_block], axis=0)
    small_rows = small.shape[0]
    _, (embed, small_all), _, _, _, _ = meeting(0, gathers=((gene_embed, 1), (small, 0)))
    small_all = small_all.reshape(shards, small_rows, width).astype(F32)
    norm_params = small_all[:, :4].transpose(1, 0, 2).reshape(4, features)
    gain_one, bias_one, gain_two, bias_two = (norm_params[i : i + 1] for i in range(4))
    comps = small_all[:, 16:, :comp_width].transpose(1, 0, 2).reshape(2 * comp_count, -1)
    centers, spreads = comps[:comp_count], comps[comp_count:]

    qkv_shard = jnp.concatenate([w_query, w_key, w_value], axis=1)
    (summed,), (qkv, out_w, up_w), _, _, _, _ = meeting(
        1, mat_nn(genes_in, embed), gathers=((qkv_shard, 0), (w_out, 1), (w_up, 0))
    )
    start = summed + positions
    normed_one, scale_one = normalize(start)
    first_low = (normed_one * gain_one + bias_one).astype(BF16)
    projected = mat_nn(first_low, qkv).astype(BF16)
    queries, keys, values = jnp.split(projected, 3, axis=1)
    attended, log_totals = attend(queries, keys, values, allowed)
    latent_shard = jnp.concatenate([w_mean, w_logvar], axis=1)
    (summed,), (down_w, latent_w, dec_w), _, _, _, _ = meeting(
        2, mat_nn(attended, out_w), gathers=((w_down, 1), (latent_shard, 0), (w_dec, 1))
    )
    after_attn = start + summed
    normed_two, scale_two = normalize(after_attn)
    second_low = (normed_two * gain_two + bias_two).astype(BF16)
    upper = mat_nn(second_low, up_w)
    activated = gelu(upper).astype(BF16)
    (summed,), (genes_w,), _, _, _, _ = meeting(
        3, mat_nn(activated, down_w), gathers=((w_genes, 0),)
    )
    hidden = (after_attn + summed).astype(BF16)

    stats = mat_nn(hidden, latent_w)
    means, log_vars = stats[:, :latent_cols], stats[:, latent_cols:]
    spread = jnp.exp(0.5 * log_vars) * noise
    latent = means + spread
    latent_low = latent.astype(BF16)
    post_part = jnp.sum(-0.5 * LOG_TWO_PI - 0.5 * log_vars - 0.5 * noise * noise, axis=1)
    precision = jnp.exp(-spreads)
    offsets = latent[None] - centers[:, None, :]
    pulled = offsets * precision[:, None, :]
    comp_part = jnp.sum(
        -0.5 * LOG_TWO_PI - 0.5 * spreads[:, None, :] - 0.5 * offsets * pulled, axis=2
    )
    density_part = jnp.pad(
        jnp.concatenate([comp_part, post_part[None]], axis=0), ((0, 7), (0, -cells % 128))
    )
    (decoder_pre,), _, _, _, (density_parts,), _ = meeting(
        4, mat_nn(latent_low, dec_w), shares=(density_part,)
    )
    densities = jnp.sum(density_parts, axis=0)[:, :cells]
    logits = densities[:comp_count] - math.log(comp_count)
    log_post = densities[comp_count]
    largest = jnp.max(logits, axis=0, keepdims=True)
    log_prior = largest[0] + jnp.log(jnp.sum(jnp.exp(logits - largest), axis=0))
    respons = jnp.exp(logits - log_prior[None, :])
    divergence = jnp.sum((log_post - log_prior) * alive_float)
    decoder_act = gelu(decoder_pre).astype(BF16)
    residual = (mat_nn(decoder_act, genes_w) - genes_in.astype(F32)) * alive_float[:, None]
    grad_rebuilt = residual.astype(BF16)

    grad_genes = mat_tn(decoder_act, grad_rebuilt).astype(BF16)
    counts = jnp.concatenate(
        [jnp.full((1, 128), divergence), jnp.full((7, 128), jnp.sum(alive_float))], axis=0
    )
    (grad_act,), (count_parts,), (genes_other,), _, _, _ = meeting(
        5, mat_nt(grad_rebuilt, genes_w), gathers=((counts, 0),), swaps=((grad_genes, 0),)
    )
    count_parts = jnp.sum(count_parts.reshape(shards, 8, 128)[:, :, 0], axis=0)
    mean_kl = count_parts[0] / (LATENT * count_parts[1])
    ramp_weight = jnp.minimum(1.0, (ramp_step[0] + 1).astype(F32) / RAMP)
    kl_scale = (
        ramp_weight * jax.nn.softplus(mean_kl - FREE_BITS) * jax.nn.sigmoid(mean_kl - FREE_BITS)
    )
    grad_pre = (grad_act * gelu_slope(decoder_pre)).astype(BF16)
    grad_dec = mat_tn(latent_low, grad_pre).astype(BF16)
    cell_weight = kl_scale * alive_float
    weighted = (respons * cell_weight[None, :])[:, :, None]
    grad_latent = mat_nt(grad_pre, dec_w) + jnp.sum(weighted * pulled, axis=0)
    grad_comps = jnp.concatenate(
        [
            -jnp.sum(weighted * pulled, axis=1),
            -jnp.sum(weighted * (0.5 * offsets * pulled - 0.5), axis=1),
        ],
        axis=0,
    )
    grad_means = grad_latent.astype(BF16)
    grad_logs = (grad_latent * (0.5 * spread) - 0.5 * cell_weight[:, None]).astype(BF16)
    grad_stats = jnp.concatenate([grad_means, grad_logs], axis=1)
    grad_latent_w = mat_tn(hidden, grad_stats).astype(BF16)
    cut = gene_cols // 256 * 128
    genes_sum_a = half_sum(grad_genes[:, :cut], genes_other[:, :cut], 0)
    genes_sum_b = half_sum(grad_genes[:, cut:], genes_other[:, cut:], 0)
    (summed,), _, (latent_other, dec_other), (genes_parts_a,), _, _ = meeting(
        6,
        mat_nt(grad_stats, latent_w),
        swaps=((grad_latent_w, 0), (grad_dec, 1)),
        exchanges=((genes_sum_a, 0),),
    )
    grad_hidden = summed.astype(BF16)

    grad_down = mat_tn(activated, grad_hidden).astype(BF16)
    grad_upper = (mat_nt(grad_hidden, down_w) * gelu_slope(upper)).astype(BF16)
    grad_up = mat_tn(second_low, grad_upper).astype(BF16)
    (grad_norm_two,), _, (down_other, up_other), (genes_parts_b, latent_parts, dec_parts), _, _ = (
        meeting(
            7,
            mat_nt(grad_upper, up_w),
            swaps=((grad_down, 1), (grad_up, 0)),
            exchanges=(
                (genes_sum_b, 0),
                (half_sum(grad_latent_w, latent_other, 0), 0),
                (half_sum(grad_dec, dec_other, 1), 1),
            ),
        )
    )
    grad_middle = grad_hidden.astype(F32) + norm_back(
        grad_norm_two, normed_two, scale_two, gain_two
    )
    middle_low = grad_middle.astype(BF16)
    grad_out = mat_tn(attended, middle_low).astype(BF16)
    grad_attended = mat_nt(middle_low, out_w).astype(BF16)
    grad_qkv_act = jnp.concatenate(
        attend_back(queries, keys, values, grad_attended, log_totals, allowed), axis=1
    )
    grad_qkv = mat_tn(first_low, grad_qkv_act).astype(BF16)
    (grad_norm_one,), _, (qkv_other, out_other), (down_parts, up_parts), _, _ = meeting(
        8,
        mat_nt(grad_qkv_act, qkv),
        swaps=((grad_qkv, 0), (grad_out, 1)),
        exchanges=((half_sum(grad_down, down_other, 1), 1), (half_sum(grad_up, up_other, 0), 0)),
    )
    grad_start = grad_middle + norm_back(grad_norm_one, normed_one, scale_one, gain_one)
    start_low = grad_start.astype(BF16)

    norm_grads = jnp.stack(
        [
            jnp.sum(grad_norm_one * normed_one, axis=0),
            jnp.sum(grad_norm_one, axis=0),
            jnp.sum(grad_norm_two * normed_two, axis=0),
            jnp.sum(grad_norm_two, axis=0),
        ]
    )
    norm_grads = norm_grads.reshape(4, shards, width).transpose(1, 0, 2)
    comp_grads = grad_comps.reshape(2 * comp_count, shards, comp_width).transpose(1, 0, 2)
    small_grads = jnp.concatenate(
        [
            jnp.pad(norm_grads, ((0, 0), (0, 12), (0, 0))),
            jnp.pad(comp_grads, ((0, 0), (0, 0), (0, width - comp_width))),
        ],
        axis=1,
    ).reshape(shards * small_rows, width)
    _, _, (start_other, small_other), _, _, _ = meeting(
        9, swaps=((start_low, 1), (small_grads, 0))
    )
    start_mine = lax.dynamic_slice_in_dim(start_low, micro * (features // 2), features // 2, 1)
    start_half = jnp.concatenate(
        [
            jnp.where(micro == 0, start_mine, start_other),
            jnp.where(micro == 0, start_other, start_mine),
        ],
        axis=0,
    )
    grad_embed = mat_tn(expression, start_half).astype(BF16)
    grad_cells = (
        mat_nt(start_low, embed).astype(BF16).astype(F32) + (-residual).astype(BF16).astype(F32)
    ).astype(BF16)
    _, _, _, (embed_parts, qkv_parts, out_parts, small_parts), _, (grad_expression,) = meeting(
        10,
        exchanges=(
            (grad_embed, 1),
            (half_sum(grad_qkv, qkv_other, 0), 0),
            (half_sum(grad_out, out_other, 1), 1),
            (half_sum(small_grads, small_other, 0), 0),
        ),
        pairs=(grad_cells,),
    )
    small_sum = total(small_parts)
    grad_query, grad_key, grad_value = jnp.split(total(qkv_parts), 3, axis=1)
    grad_mean, grad_logvar = jnp.split(total(latent_parts), 2, axis=1)
    return (
        total(embed_parts),
        small_sum[0],
        small_sum[1],
        grad_query,
        grad_key,
        grad_value,
        total(out_parts),
        small_sum[2],
        small_sum[3],
        total(up_parts),
        total(down_parts),
        grad_mean,
        grad_logvar,
        small_sum[16 : 16 + comp_count, :comp_width],
        small_sum[16 + comp_count :, :comp_width],
        total(dec_parts),
        jnp.concatenate([total(genes_parts_a), total(genes_parts_b)], axis=1),
        grad_expression,
    )


def solution(mesh):
    weight_rows = P(("section", "dp"), "mp")
    weight_cols = P("mp", ("section", "dp"))
    vector = P(("section", "dp"))
    comps = P(None, ("mp", "section", "dp"))
    weights = (
        weight_cols, vector, vector, weight_rows, weight_rows, weight_rows, weight_cols,
        vector, vector, weight_rows, weight_cols, weight_rows, weight_rows, comps, comps,
        weight_cols, weight_rows,
    )
    return jax.shard_map(
        local,
        mesh=mesh,
        in_specs=(P("dp", "mp"), P(None, "dp"), P("dp"), P("dp", None), P(), P("dp", "mp"))
        + weights,
        out_specs=weights + (P("dp", "mp"),),
        check_vma=False,
    )
```

```python
import functools
import math

import jax
import jax.numpy as jnp
from jax import lax
from jax.experimental import pallas as pl
from jax.experimental.pallas import tpu as pltpu
from jax.sharding import PartitionSpec as P

HEAD = 64
LATENT = 512
RAMP = 1000
LOG_TWO_PI = 1.8378770664093453
NEG_LARGE = -1e30
FREE_BITS = 1.0
HOP_LAG = 3
WINDOW = 3
BLOCK_STEP = 4
TILE = 256
LINK_BYTES_PER_US = 92000.0
MOMENT_US = 1.3
SPREAD = 1
SPREAD_FROM = 0
SPREAD_STEP = 1
F32 = jnp.float32
BF16 = jnp.bfloat16


def mat_nn(left, right):
    return jnp.dot(left, right, preferred_element_type=F32)


def mat_tn(left, right):
    return lax.dot_general(left, right, (((0,), (0,)), ((), ())), preferred_element_type=F32)


def mat_nt(left, right):
    return lax.dot_general(left, right, (((1,), (1,)), ((), ())), preferred_element_type=F32)


def gelu(values):
    return 0.5 * values * (1.0 + lax.erf(values * 0.7071067811865476))


def gelu_slope(values):
    return (
        0.5 * (1.0 + lax.erf(values * 0.7071067811865476))
        + values * jnp.exp(-0.5 * values * values) * 0.3989422804014327
    )


def normalize(values):
    center = values - jnp.mean(values, axis=-1, keepdims=True)
    scale = lax.rsqrt(jnp.mean(center * center, axis=-1, keepdims=True) + 1e-05)
    return center * scale, scale


def norm_back(grad_in, normed, scale, gain):
    scaled = grad_in * gain
    return scale * (
        scaled
        - jnp.mean(scaled, axis=-1, keepdims=True)
        - normed * jnp.mean(scaled * normed, axis=-1, keepdims=True)
    )


def position_code(places, feature_count):
    quarter = feature_count // 4
    frequency = jnp.exp(jnp.arange(quarter, dtype=F32) * (-math.log(10000.0) / quarter))
    along_x = places[0][:, None] * frequency[None, :]
    along_y = places[1][:, None] * frequency[None, :]
    return jnp.concatenate(
        [jnp.sin(along_x), jnp.cos(along_x), jnp.sin(along_y), jnp.cos(along_y)], axis=1
    )


def slide_ids(length_row, cell_count):
    bounds = jnp.cumsum(length_row)[:-1]
    index = jnp.arange(cell_count, dtype=jnp.int32)
    return jnp.sum((index[:, None] >= bounds[None, :]).astype(jnp.int32), axis=1)


def allowed_pairs(slide, alive):
    index = jnp.arange(alive.shape[0], dtype=jnp.int32)
    return (slide[:, None] == slide[None, :]) & (
        (alive[None, :] == 1) | (index[:, None] == index[None, :])
    )


def heads_of(array):
    return array.reshape(array.shape[0], -1, HEAD)


def attend(queries, keys, values, allowed):
    factor = HEAD ** (-0.5)
    scores = (
        jnp.einsum("qhd,khd->hqk", heads_of(queries), heads_of(keys), preferred_element_type=F32)
        * factor
    )
    scores = jnp.where(allowed[None], scores, NEG_LARGE)
    largest = jnp.max(scores, axis=2, keepdims=True)
    exponents = jnp.exp(scores - largest)
    sums = jnp.sum(exponents, axis=2, keepdims=True)
    probs = (exponents / sums).astype(BF16)
    out = jnp.einsum("hqk,khd->qhd", probs, heads_of(values), preferred_element_type=F32)
    return out.reshape(queries.shape).astype(BF16), largest + jnp.log(sums)


def attend_back_kernel(middle, out_w, projected, log_totals, slide_keys, slide_queries, alive_keys, out):
    cells, width = out.shape[0], out.shape[1] // 3
    factor = HEAD ** (-0.5)
    shape = (cells, cells)
    own_key = lax.broadcasted_iota(jnp.int32, shape, 0) == lax.broadcasted_iota(jnp.int32, shape, 1)
    allowed = (slide_keys[...] == slide_queries[...]) & ((alive_keys[...] == 1) | own_key)
    grad_out = mat_nt(middle[...], out_w[...]).astype(BF16)
    for head in range(width // HEAD):
        first = head * HEAD
        q = projected[:, first : first + HEAD]
        k = projected[:, width + first : width + first + HEAD]
        v = projected[:, 2 * width + first : 2 * width + first + HEAD]
        g = grad_out[:, first : first + HEAD]
        scores = mat_nt(k, q) * factor - log_totals[head : head + 1, :]
        probs = jnp.where(allowed, jnp.exp(jnp.minimum(scores, 0.0)), 0.0)
        grad_probs = mat_nt(v, g)
        inner = jnp.sum(probs * grad_probs, axis=0, keepdims=True)
        grad_scores = (probs * (grad_probs - inner)).astype(BF16)
        out[:, first : first + HEAD] = (mat_tn(grad_scores, k) * factor).astype(BF16)
        out[:, width + first : width + first + HEAD] = (mat_nn(grad_scores, q) * factor).astype(BF16)
        out[:, 2 * width + first : 2 * width + first + HEAD] = mat_nn(
            probs.astype(BF16), g
        ).astype(BF16)


def attend_back(middle, out_w, projected, log_totals, slide, alive):
    return pl.pallas_call(
        attend_back_kernel,
        out_shape=jax.ShapeDtypeStruct(projected.shape, BF16),
        compiler_params=pltpu.CompilerParams(vmem_limit_bytes=48 * 2**20),
        name="attend_back",
    )(
        middle,
        out_w,
        projected,
        log_totals[:, :, 0],
        slide[:, None],
        slide[None, :],
        alive[:, None],
    )


def part_of(ref, axis, index, size):
    span = pl.ds(index * size, size)
    if axis == 0:
        return ref.at[span, :]
    return ref.at[:, pl.ds(pl.multiple_of(index * size, 128), size)]


def line_sum(produce, hooks, part, out, from_left, from_right, to_right, to_left, got_left, got_right, sent_right, sent_left):
    me, count = lax.axis_index("mp"), lax.axis_size("mp")
    pieces, height, width = from_left.shape
    splits = pieces * width // part.shape[1]
    stride = (part.shape[0] - height) // (splits - 1)
    has_right, has_left = me < count - 1, me > 0

    def place(piece):
        return (
            pl.ds(pl.multiple_of(lax.rem(piece, splits) * stride, 16), height),
            pl.ds(pl.multiple_of(lax.div(piece, splits) * width, width), width),
        )

    def rightward(piece):
        return pltpu.make_async_remote_copy(
            src_ref=to_right.at[piece],
            dst_ref=from_left.at[piece],
            send_sem=sent_right.at[piece],
            recv_sem=got_left.at[piece],
            device_id={"mp": me + 1},
        )

    def leftward(piece):
        return pltpu.make_async_remote_copy(
            src_ref=to_left.at[piece],
            dst_ref=from_right.at[piece],
            send_sem=sent_left.at[piece],
            recv_sem=got_right.at[piece],
            device_id={"mp": me - 1},
        )

    def flow(piece, copy, has_source, has_target, source, target):
        @pl.when((piece >= 0) & (piece < pieces))
        def _():
            @pl.when(has_source)
            def _():
                copy(piece).wait_recv()

            @pl.when(has_target & has_source)
            def _():
                target[piece] = (part[place(piece)] + source[piece].astype(F32)).astype(BF16)

            @pl.when(has_target & jnp.logical_not(has_source))
            def _():
                target[piece] = part[place(piece)].astype(BF16)

            @pl.when(has_target & (piece >= WINDOW))
            def _():
                copy(piece - WINDOW).wait_send()

            @pl.when(has_target)
            def _():
                copy(piece).start()

    moments = pieces + HOP_LAG * (count - 1)
    right_half = lax.div(2 * me + 1, count)
    trail = HOP_LAG * (right_half * me + (1 - right_half) * (count - 1 - me))

    def step(moment, carry):
        produce(moment)
        flow(moment - HOP_LAG * me, rightward, has_left, has_right, from_left, to_right)
        flow(
            moment - HOP_LAG * (count - 1 - me), leftward, has_right, has_left, from_right, to_left
        )
        done = moment - trail
        finished = (done >= 0) & (done < pieces)

        @pl.when(finished & has_left & has_right)
        def _():
            out[place(done)] = (
                part[place(done)] + from_left[done].astype(F32) + from_right[done].astype(F32)
            )

        @pl.when(finished & jnp.logical_not(has_left))
        def _():
            out[place(done)] = part[place(done)] + from_right[done].astype(F32)

        @pl.when(finished & jnp.logical_not(has_right))
        def _():
            out[place(done)] = part[place(done)] + from_left[done].astype(F32)

        return carry

    def finish():
        def step(piece, carry):
            @pl.when(has_right)
            def _():
                rightward(piece).wait_send()

            @pl.when(has_left)
            def _():
                leftward(piece).wait_send()

            return carry

        lax.fori_loop(pieces - WINDOW, pieces, step, 0)

    reached = 0
    for when, hook in hooks:
        if when > reached:
            lax.fori_loop(reached, when, step, 0)
            reached = when
        hook()
    lax.fori_loop(reached, moments, step, 0)
    finish()


PRODUCT_SCRATCH = 5


def start_product(form, left, right, part, left_in, right_in, left_sem, right_sem):
    transposed, sliced = form
    blocks = right_in.shape[0]
    width = part.shape[1] // blocks
    if sliced:
        rows = left_in.shape[0]
        first = pl.multiple_of(lax.axis_index("section") * rows, 16)
        left_copy = pltpu.make_async_copy(left.at[pl.ds(first, rows), :], left_in, left_sem)
        left_copy.start()

    def right_copy(block):
        span = pl.ds(pl.multiple_of(block * width, width), width)
        view = right.at[span, :] if transposed else right.at[:, span]
        return pltpu.make_async_copy(view, right_in.at[block], right_sem.at[block])

    for block in range(blocks):
        right_copy(block).start()
    if sliced:
        left_copy.wait()

    def produce(moment):
        @pl.when((lax.rem(moment, BLOCK_STEP) == 0) & (moment < blocks * BLOCK_STEP))
        def _():
            block = lax.div(moment, BLOCK_STEP)
            right_copy(block).wait()
            contract = (((1,), (1 if transposed else 0,)), ((), ()))
            part[:, pl.ds(pl.multiple_of(block * width, width), width)] = lax.dot_general(
                (left_in if sliced else left)[...],
                right_in[block],
                contract,
                preferred_element_type=F32,
            )

    return produce


def halfway(rows):
    return rows // 32 * 16


def block_of(ref, axis, index, size, start=0, stop=None):
    if axis == 0:
        stop = size if stop is None else stop
        return ref.at[pl.ds(pl.multiple_of(index * size + start, 16), stop - start), :]
    stop = ref.shape[0] if stop is None else stop
    return ref.at[pl.ds(start, stop - start), pl.ds(pl.multiple_of(index * size, 128), size)]


def reaction_moments(travelling):
    third = travelling / LINK_BYTES_PER_US
    last = 2 * len(range(8)) + 3 * HOP_LAG - 1
    return [
        min(last, math.ceil((parts * third + 2.0 + 0.5 * parts) / MOMENT_US)) for parts in (1, 2)
    ]


def comm_kernel(plan, *refs):
    refs = list(refs)

    def take(number):
        taken = refs[:number]
        del refs[:number]
        return taken

    reduces, gathers, swaps, exchanges, shares, pairs, travelling = plan
    groups = (len(gathers), len(swaps), len(exchanges), shares, pairs)
    sources = [take(n) for n in (2 if reduces else 0,) + groups]
    others = [take(1)[0] if paired else None for _, _, paired in exchanges]
    results = [take(n) for n in (1 if reduces else 0,) + groups]
    product = take(PRODUCT_SCRATCH) if reduces else None
    line = take(8) if reduces else None
    staging = [take(4 + paired) for _, _, paired in exchanges]
    sent, got, local_sem = refs

    section, z, dp = (lax.axis_index(name) for name in ("section", "mp", "dp"))
    count_z, count_dp = lax.axis_size("mp"), lax.axis_size("dp")
    row, col = dp // 2, dp % 2
    peer_x, peer_y = row * 2 + (1 - col), (1 - row) * 2 + col
    peer_d = (1 - row) * 2 + (1 - col)
    partner, to_x, to_y = {"section": 1 - section}, {"dp": peer_x}, {"dp": peer_y}

    barrier = pltpu.get_barrier_semaphore()
    fixed = 0
    if gathers or swaps or pairs:
        pl.semaphore_signal(barrier, inc=1, device_id=partner)
        fixed += 1
    if gathers or exchanges:
        pl.semaphore_signal(barrier, inc=1, device_id=to_x)
        pl.semaphore_signal(barrier, inc=1, device_id=to_y)
        fixed += 2
    if shares:
        for step in range(1, count_z):
            pl.semaphore_signal(barrier, inc=1, device_id={"mp": (z + step) % count_z})
        fixed += count_z - 1
    elif reduces:
        for exists, neighbour in ((z > 0, z - 1), (z < count_z - 1, z + 1)):

            @pl.when(exists)
            def _(neighbour=neighbour):
                pl.semaphore_signal(barrier, inc=1, device_id={"mp": neighbour})

        at_end = (z == 0) | (z == count_z - 1)

        @pl.when(at_end)
        def _():
            pl.semaphore_wait(barrier, fixed + 1)

        @pl.when(jnp.logical_not(at_end))
        def _():
            pl.semaphore_wait(barrier, fixed + 2)

    if fixed and (shares or not reduces):
        pl.semaphore_wait(barrier, fixed)

    used = [0, 0]

    def remote(src, dst, device):
        index = used[0]
        used[0] += 1
        return pltpu.make_async_remote_copy(
            src_ref=src, dst_ref=dst, send_sem=sent.at[index], recv_sem=got.at[index], device_id=device
        )

    def within(src, dst):
        index = used[1]
        used[1] += 1
        return pltpu.make_async_copy(src, dst, local_sem.at[index])

    locals_, early, first, second = [], [], [], []
    after_one, after_two, after_three = [], [], []
    receives, loads = [], []
    starts_d, starts_xy, conclusions = [], [], []
    for item, (axis, size) in enumerate(swaps):
        src, dst = sources[2][item], results[2][item]
        copy = remote(part_of(src, axis, 1 - section, size), dst, partner)
        early.append(copy)
        receives.append(copy)
    for item in range(pairs):
        copy = remote(sources[5][item], results[5][item], partner)
        early.append(copy)
        receives.append(copy)
    for item in range(shares):
        src, dst = sources[4][item], results[4][item]
        locals_.append(within(src, dst.at[z]))
        for step in range(1, count_z):
            copy = remote(src, dst.at[z], {"mp": (z + step) % count_z})
            early.append(copy)
            receives.append(copy)
    for item, (axis, size) in enumerate(gathers):
        src, dst = sources[1][item], results[1][item]
        rows = src.shape[0]
        cut = halfway(rows)

        def shard_of(index, start=0, stop=rows, dst=dst, axis=axis, size=size):
            return block_of(dst, axis, section * count_dp + index, size, start, stop)

        upper, lower = src.at[pl.ds(0, cut), :], src.at[pl.ds(cut, rows - cut), :]
        locals_.append(within(src, shard_of(dp)))
        own = remote(src, shard_of(dp), partner)
        x_upper = remote(upper, shard_of(dp, 0, cut), to_x)
        y_lower = remote(lower, shard_of(dp, cut), to_y)
        x_lower = remote(lower, shard_of(dp, cut), to_x)
        y_upper = remote(upper, shard_of(dp, 0, cut), to_y)
        pass_y = remote(shard_of(peer_x, 0, cut), shard_of(peer_x, 0, cut), to_y)
        pass_x = remote(shard_of(peer_y, cut), shard_of(peer_y, cut), to_x)
        relay_x = remote(shard_of(peer_x), shard_of(peer_x), partner)
        relay_y = remote(shard_of(peer_y), shard_of(peer_y), partner)
        relay_upper = remote(shard_of(peer_d, 0, cut), shard_of(peer_d, 0, cut), partner)
        relay_lower = remote(shard_of(peer_d, cut), shard_of(peer_d, cut), partner)
        early.append(own)
        first += [x_upper, y_lower]
        second += [x_lower, y_upper]
        after_one += [([x_upper], None, pass_y), ([y_lower], None, pass_x)]
        after_two += [([x_lower], None, relay_x), ([y_upper], None, relay_y)]
        after_three += [([pass_y], None, relay_upper), ([pass_x], None, relay_lower)]
        receives += [own, relay_x, relay_y, relay_upper, relay_lower]
    for item, (axis, size, paired) in enumerate(exchanges):
        src, dst = sources[3][item], results[3][item]
        mine, from_x, from_y, inbound = staging[item][:4]
        rows, dtype = from_x.shape[0], from_x.dtype
        cut = halfway(rows)
        rest = rows - cut
        half = section * count_dp if paired else 0
        fetched = []
        for role, index in enumerate((peer_d, peer_x, peer_y, dp)):
            copies = [within(block_of(src, axis, half + index, size), mine.at[role])]
            if paired:
                copies.append(
                    within(block_of(others[item], axis, index, size), staging[item][4].at[role])
                )
            fetched.append(copies)
            loads += copies

        def merge(role, mine=mine, other=staging[item][-1] if paired else None):
            def run():
                if other is not None:
                    mine[role] = (mine[role].astype(F32) + other[role].astype(F32)).astype(mine.dtype)

            return run

        top, bottom = pl.ds(0, cut), pl.ds(cut, rest)
        d_upper = remote(mine.at[0, top, :], inbound.at[top, :], to_x)
        d_lower = remote(mine.at[0, bottom, :], inbound.at[bottom, :], to_y)
        x_upper = remote(mine.at[1, top, :], from_x.at[top, :], to_x)
        y_lower = remote(mine.at[2, bottom, :], from_y.at[bottom, :], to_y)
        y_upper = remote(mine.at[2, top, :], from_y.at[top, :], to_y)
        x_lower = remote(mine.at[1, bottom, :], from_x.at[bottom, :], to_x)

        def add(role, span, mine=mine, term=inbound):
            def run():
                mine[role, span, :] = (
                    mine[role, span, :].astype(F32) + term[span, :].astype(F32)
                ).astype(mine.dtype)

            return run

        def conclude(mine=mine, from_x=from_x, from_y=from_y, dst=dst):
            dst[...] = mine[3].astype(F32) + from_x[...].astype(F32) + from_y[...].astype(F32)

        starts_d += [(fetched[0], merge(0), [d_upper, d_lower])]
        starts_xy += [
            (fetched[1], merge(1), [x_upper]),
            (fetched[2], merge(2), [y_lower]),
            (fetched[3], merge(3), []),
        ]
        after_one += [
            ([d_upper], add(2, top), y_upper),
            ([d_lower], add(1, bottom), x_lower),
        ]
        receives += [x_upper, y_lower, y_upper, x_lower]
        conclusions.append(conclude)

    remotes = early + first + second

    def begin():
        for copy in loads + remotes + locals_:
            copy.start()

    def send_parts():
        for copies, compute, targets in starts_d + starts_xy:
            for copy in copies:
                copy.wait()
            compute()
            for copy in targets:
                copy.start()

    def react(items):
        def run():
            for waits, compute, copy in items:
                for wait in waits:
                    wait.wait_recv()
                if compute is not None:
                    compute()
                copy.start()

        return run

    if reduces:
        produce = start_product(reduces, *sources[0], *product)
        moments = reaction_moments(travelling)
        hooks = [(0, begin), (2, send_parts), (moments[0], react(after_one)), (moments[1], react(after_two))]
        line_sum(produce, hooks, product[0], results[0][0], *line)
    else:
        begin()
        send_parts()
        react(after_one)()
        react(after_two)()
    react(after_three)()
    for copy in receives:
        copy.wait_recv()
    for conclude in conclusions:
        conclude()
    started = remotes + [copy for _, _, copies in starts_d + starts_xy for copy in copies]
    started += [copy for _, _, copy in after_one + after_two + after_three]
    for copy in started:
        copy.wait_send()
    for copy in locals_:
        copy.wait()


def comm(number, reduce=None, gathers=(), swaps=(), exchanges=(), shares=(), pairs=(), name="meet"):
    count_dp, count_z = lax.axis_size("dp"), lax.axis_size("mp")
    sections = lax.axis_size("section")

    def resized(shape, axis, size):
        return shape[:axis] + (size,) + shape[axis + 1 :]

    inputs, outputs, scratch = [], [], []
    plan_gathers, plan_swaps, plan_exchanges = [], [], []
    remote_count = local_count = travelling = 0
    reduces = None
    if reduce is not None:
        left, right, transposed, sliced = reduce
        reduces = (transposed, sliced)
        rows, depth = left.shape[0] // (sections if sliced else 1), left.shape[1]
        width = right.shape[0 if transposed else 1]
        blocks = width // 256
        inputs += [left, right]
        outputs.append(jax.ShapeDtypeStruct((rows, width), F32))
        scratch += [
            pltpu.VMEM((rows, width), F32),
            pltpu.VMEM((rows, depth) if sliced else (16, 128), BF16),
            pltpu.VMEM((blocks, 256, depth) if transposed else (blocks, depth, 256), BF16),
            pltpu.SemaphoreType.DMA,
            pltpu.SemaphoreType.DMA((blocks,)),
        ]
        buffer = pltpu.VMEM((width // 64, 256, 128), BF16)
        scratch += [buffer] * 4 + [pltpu.SemaphoreType.DMA((width // 64,))] * 4
    for shard, axis in gathers:
        size = shard.shape[axis]
        inputs.append(shard)
        outputs.append(
            jax.ShapeDtypeStruct(resized(shard.shape, axis, size * sections * count_dp), shard.dtype)
        )
        plan_gathers.append((axis, size))
        travelling += shard.size * shard.dtype.itemsize
        remote_count += 11
        local_count += 1
    for array, axis in swaps:
        size = array.shape[axis] // sections
        inputs.append(array)
        outputs.append(jax.ShapeDtypeStruct(resized(array.shape, axis, size), array.dtype))
        plan_swaps.append((axis, size))
        remote_count += 1
    other_inputs = []
    for array, other, axis in exchanges:
        paired = other is not None
        size = array.shape[axis] // (count_dp * (sections if paired else 1))
        piece = resized(array.shape, axis, size)
        inputs.append(array)
        outputs.append(jax.ShapeDtypeStruct(piece, F32))
        plan_exchanges.append((axis, size, paired))
        roles, one = pltpu.VMEM((4,) + piece, array.dtype), pltpu.VMEM(piece, array.dtype)
        scratch += [roles, one, one, one]
        if paired:
            other_inputs.append(other)
            scratch.append(roles)
        travelling += piece[0] * piece[1] * array.dtype.itemsize
        remote_count += 6
        local_count += 8
    for array in shares:
        inputs.append(array)
        outputs.append(jax.ShapeDtypeStruct((count_z,) + array.shape, array.dtype))
        remote_count += count_z - 1
        local_count += 1
    for array in pairs:
        inputs.append(array)
        outputs.append(jax.ShapeDtypeStruct(array.shape, array.dtype))
        remote_count += 1
    inputs += other_inputs
    scratch += [
        pltpu.SemaphoreType.DMA((max(remote_count, 1),)),
        pltpu.SemaphoreType.DMA((max(remote_count, 1),)),
        pltpu.SemaphoreType.DMA((max(local_count, 1),)),
    ]
    plan = (reduces, tuple(plan_gathers), tuple(plan_swaps), tuple(plan_exchanges), len(shares), len(pairs), travelling)
    placed = [True] * (reduces is not None) + [False] * (len(gathers) + len(swaps))
    placed += [True] * len(exchanges) + [False] * (len(shares) + len(pairs))
    vmem, anywhere = pl.BlockSpec(memory_space=pltpu.VMEM), pl.BlockSpec(memory_space=pl.ANY)
    outs = pl.pallas_call(
        functools.partial(comm_kernel, plan),
        out_shape=outputs,
        in_specs=([] if reduces is None else [anywhere if reduces[1] else vmem])
        + [anywhere] * (len(inputs) - (0 if reduces is None else 1)),
        out_specs=[vmem if in_vmem else anywhere for in_vmem in placed],
        scratch_shapes=scratch,
        compiler_params=pltpu.CompilerParams(
            collective_id=number, has_side_effects=True, vmem_limit_bytes=48 * 2**20
        ),
        cost_estimate=pl.CostEstimate(flops=1000000, bytes_accessed=90000000, transcendentals=0),
        name=name,
    )(*inputs)
    outs = list(outs)
    split = []
    for number_of in (1 if reduces else 0, len(gathers), len(swaps), len(exchanges), len(shares), len(pairs)):
        split.append(outs[:number_of])
        outs = outs[number_of:]
    return split


def trade(remote, mine, indices, from_x, from_y, inbound, to_x, to_y):
    rows = from_x.shape[0]
    cut = halfway(rows)
    top, bottom = pl.ds(0, cut), pl.ds(cut, rows - cut)
    d, x, y, own = indices
    d_upper = remote(mine.at[d, top, :], inbound.at[top, :], to_x)
    d_lower = remote(mine.at[d, bottom, :], inbound.at[bottom, :], to_y)
    x_upper = remote(mine.at[x, top, :], from_x.at[top, :], to_x)
    y_lower = remote(mine.at[y, bottom, :], from_y.at[bottom, :], to_y)
    y_upper = remote(mine.at[y, top, :], from_y.at[top, :], to_y)
    x_lower = remote(mine.at[x, bottom, :], from_x.at[bottom, :], to_x)

    def pass_on():
        for copy, index, span, onward in (
            (d_upper, y, top, y_upper),
            (d_lower, x, bottom, x_lower),
        ):
            copy.wait_recv()
            mine[index, span, :] = (
                mine[index, span, :].astype(F32) + inbound[span, :].astype(F32)
            ).astype(mine.dtype)
            onward.start()

    def conclude():
        for copy in (x_upper, y_lower, y_upper, x_lower):
            copy.wait_recv()
        for copy in (d_upper, d_lower, x_upper, y_lower, y_upper, x_lower):
            copy.wait_send()
        return mine[own].astype(F32) + from_x[...].astype(F32) + from_y[...].astype(F32)

    return (d_upper, d_lower), (x_upper, y_lower), pass_on, conclude


def tail_kernel(
    start, expression, embed, grad_rebuilt, qkv, out, small, qkv_other, out_other,
    embed_sum, qkv_sum, out_sum, small_sum, cells_own, cells_other,
    start_other, start_turned, x_own, x_other, embed_in, cells, embed_parts, embed_x, embed_y, embed_in_d,
    qkv_parts, qkv_x, qkv_y, qkv_in_d, qkv_partner, out_parts, out_x, out_y, out_in_d, out_partner,
    small_parts, small_x, small_y, small_in_d, small_partner, sent, got, local_sem,
):
    section, dp = lax.axis_index("section"), lax.axis_index("dp")
    count_dp = lax.axis_size("dp")
    row, col = dp // 2, dp % 2
    peer_x, peer_y = row * 2 + (1 - col), (1 - row) * 2 + col
    peer_d = (1 - row) * 2 + (1 - col)
    partner, to_x, to_y = {"section": 1 - section}, {"dp": peer_x}, {"dp": peer_y}
    rows, genes = cells.shape
    half = start_other.shape[1]
    width = half // count_dp

    barrier = pltpu.get_barrier_semaphore()
    for device in (partner, to_x, to_y):
        pl.semaphore_signal(barrier, inc=1, device_id=device)
    pl.semaphore_wait(barrier, 3)

    used = [0, 0]

    def remote(src, dst, device):
        index = used[0]
        used[0] += 1
        return pltpu.make_async_remote_copy(
            src_ref=src, dst_ref=dst, send_sem=sent.at[index], recv_sem=got.at[index], device_id=device
        )

    def within(src, dst):
        index = used[1]
        used[1] += 1
        return pltpu.make_async_copy(src, dst, local_sem.at[index])

    def half_of(index):
        return pl.ds(pl.multiple_of(index * half, 128), half)

    def rows_of(index):
        return pl.ds(pl.multiple_of(index * rows, 16), rows)

    swaps = [
        remote(start.at[:, half_of(1 - section)], start_other, partner),
        remote(small.at[1 - section], small_partner, partner),
    ]
    for copy in swaps:
        copy.start()
    roles = (peer_d, peer_x, peer_y, dp)
    fetches = []
    for src, other, axis, parts, parts_other in (
        (qkv, qkv_other, 0, qkv_parts, qkv_partner),
        (out, out_other, 1, out_parts, out_partner),
    ):
        size = src.shape[axis] // (2 * count_dp)
        for role, index in enumerate(roles):
            fetches.append(
                within(block_of(src, axis, section * count_dp + index, size), parts.at[role])
            )
            fetches.append(within(block_of(other, axis, index, size), parts_other.at[role]))
    fetches.append(within(small.at[section], small_parts))
    load_own = within(expression.at[rows_of(section), :], x_own)
    load_other = within(expression.at[rows_of(1 - section), :], x_other)
    load_embed = within(embed, embed_in)
    load_cells = within(grad_rebuilt, cells)
    for copy in fetches + [load_own, load_other, load_embed, load_cells]:
        copy.start()

    trades = [
        trade(remote, parts, indices, *buffers, to_x, to_y)
        for parts, indices, buffers in (
            (qkv_parts, (0, 1, 2, 3), (qkv_x, qkv_y, qkv_in_d)),
            (out_parts, (0, 1, 2, 3), (out_x, out_y, out_in_d)),
            (small_parts, roles, (small_x, small_y, small_in_d)),
            (embed_parts, roles, (embed_x, embed_y, embed_in_d)),
        )
    ]

    for copy in fetches:
        copy.wait()
    swaps[1].wait_recv()
    for parts, other in (
        (qkv_parts, qkv_partner),
        (out_parts, out_partner),
        (small_parts, small_partner),
    ):
        parts[...] = (parts[...].astype(F32) + other[...].astype(F32)).astype(parts.dtype)
    for first, second, _, _ in trades[:3]:
        for copy in first + second:
            copy.start()

    load_own.wait()
    load_other.wait()
    swaps[0].wait_recv()
    start_turned[0] = start[:, half_of(section)].T
    start_turned[1] = start_other[...].T

    def embed_tile(span, size):
        tile = mat_nn(start_turned[0], x_own[:, span]) + mat_nn(start_turned[1], x_other[:, span])
        embed_parts[:, :, span] = tile.reshape(count_dp, width, size).astype(BF16)

    whole = genes // TILE

    def embed_step(index, carry):
        embed_tile(pl.ds(pl.multiple_of(index * TILE, TILE), TILE), TILE)
        return carry

    lax.fori_loop(0, whole, embed_step, 0)
    if genes % TILE:
        embed_tile(pl.ds(whole * TILE, genes % TILE), genes % TILE)
    for copy in trades[3][0] + trades[3][1]:
        copy.start()

    load_embed.wait()
    load_cells.wait()

    def cells_tile(span):
        tile = mat_nt(start[...], embed_in[span, :]).astype(BF16)
        cells[:, span] = (tile.astype(F32) - cells[:, span].astype(F32)).astype(BF16)

    def cells_step(index, carry):
        cells_tile(pl.ds(pl.multiple_of(index * TILE, TILE), TILE))
        return carry

    lax.fori_loop(0, whole, cells_step, 0)
    if genes % TILE:
        cells_tile(pl.ds(whole * TILE, genes % TILE))
    give = remote(cells, cells_other, partner)
    give.start()
    keep = within(cells, cells_own)
    keep.start()

    for _, _, pass_on, _ in trades:
        pass_on()
    qkv_sum[...] = trades[0][3]()
    out_sum[...] = trades[1][3]()
    small_sum[...] = trades[2][3]()
    embed_sum[...] = trades[3][3]().T
    for copy in swaps:
        copy.wait_send()
    give.wait()
    keep.wait()


def assemble_kernel(own, other, whole, held, arrived, left):
    section = lax.axis_index("section")
    rows = own.shape[0]
    spans = [(start, min(128, rows - start)) for start in range(0, rows, 128)]
    loads, stores = [], []
    for place, (src, index) in enumerate(((own, section), (other, 1 - section))):
        for part, (start, size) in enumerate(spans):
            span = pl.ds(start, size)
            target = pl.ds(pl.multiple_of(index * rows + start, 16), size)
            number = place * len(spans) + part
            loads.append(
                pltpu.make_async_copy(src.at[span, :], held.at[place, span, :], arrived.at[number])
            )
            stores.append(
                pltpu.make_async_copy(held.at[place, span, :], whole.at[target, :], left.at[number])
            )
    for load in loads:
        load.start()
    for load, store in zip(loads, stores):
        load.wait()
        store.start()
    for store in stores:
        store.wait()


def tail(number, start, expression, embed, grad_rebuilt, qkv, qkv_other, out, out_other, small):
    rows, features = start.shape
    genes, count_dp = embed.shape[0], lax.axis_size("dp")
    half = features // 2
    width = half // count_dp
    vmem, anywhere = pl.BlockSpec(memory_space=pltpu.VMEM), pl.BlockSpec(memory_space=pl.ANY)

    def buffers(shape, dtype, paired):
        parts, one = pltpu.VMEM((count_dp,) + shape, dtype), pltpu.VMEM(shape, dtype)
        return [parts, one, one, one] + ([parts] if paired else [])

    qkv_piece = (qkv.shape[0] // (2 * count_dp), qkv.shape[1])
    out_piece = (out.shape[0], out.shape[1] // (2 * count_dp))
    small_piece = small.shape[2:]
    cells = jax.ShapeDtypeStruct((rows, genes), BF16)
    results = pl.pallas_call(
        tail_kernel,
        out_shape=[
            jax.ShapeDtypeStruct((genes, width), F32),
            jax.ShapeDtypeStruct(qkv_piece, F32),
            jax.ShapeDtypeStruct(out_piece, F32),
            jax.ShapeDtypeStruct(small_piece, F32),
            cells,
            cells,
        ],
        in_specs=[vmem] + [anywhere] * 8,
        out_specs=[vmem] * 4 + [anywhere] * 2,
        scratch_shapes=[
            pltpu.VMEM((rows, half), BF16),
            pltpu.VMEM((2, half, rows), BF16),
            pltpu.VMEM((rows, genes), BF16),
            pltpu.VMEM((rows, genes), BF16),
            pltpu.VMEM((genes, features), BF16),
            pltpu.VMEM((rows, genes), BF16),
        ]
        + buffers((width, genes), BF16, False)
        + buffers(qkv_piece, BF16, True)
        + buffers(out_piece, BF16, True)
        + buffers(small_piece, F32, True)
        + [
            pltpu.SemaphoreType.DMA((27,)),
            pltpu.SemaphoreType.DMA((27,)),
            pltpu.SemaphoreType.DMA((22,)),
        ],
        compiler_params=pltpu.CompilerParams(
            collective_id=number, has_side_effects=True, vmem_limit_bytes=56 * 2**20
        ),
        name="tail",
    )(start, expression, embed, grad_rebuilt, qkv, out, small, qkv_other, out_other)
    whole = pl.pallas_call(
        assemble_kernel,
        out_shape=jax.ShapeDtypeStruct((2 * rows, genes), BF16),
        in_specs=[anywhere] * 2,
        out_specs=anywhere,
        scratch_shapes=[pltpu.VMEM((2, rows, genes), BF16)]
        + [pltpu.SemaphoreType.DMA((2 * (-(-rows // 128)),))] * 2,
        compiler_params=pltpu.CompilerParams(vmem_limit_bytes=56 * 2**20),
        name="assemble",
    )(results[4], results[5])
    return list(results[:4]) + [whole]


def meet(tiled, number, reduce=None, gathers=(), swaps=(), exchanges=(), shares=(), pairs=()):
    if tiled:
        return comm(number, reduce, gathers, swaps, exchanges, shares, pairs)
    partner = [(i, 1 - i) for i in range(2)]
    section, count_dp = lax.axis_index("section"), lax.axis_size("dp")
    swapped = []
    for array, axis in swaps:
        size = array.shape[axis] // 2
        half = lax.dynamic_slice_in_dim(array, (1 - section) * size, size, axis)
        swapped.append(lax.ppermute(half, "section", partner))
    exchanged = []
    for array, other, axis in exchanges:
        if other is not None:
            array = half_sum(array, other, axis)
        parts = lax.all_to_all(jnp.stack(jnp.split(array, count_dp, axis)), "dp", 0, 0)
        exchanged.append(total(parts))
    return [
        [] if reduce is None else comm(number, reduce)[0][0:1],
        [lax.all_gather(shard, ("section", "dp"), axis=axis, tiled=True) for shard, axis in gathers],
        swapped,
        exchanged,
        [lax.all_gather(array, "mp") for array in shares],
        [lax.ppermute(array, "section", partner) for array in pairs],
    ]


def half_sum(array, received, axis):
    size = received.shape[axis]
    own = lax.dynamic_slice_in_dim(array, lax.axis_index("section") * size, size, axis)
    return (own.astype(F32) + received.astype(F32)).astype(array.dtype)


def total(parts):
    return jnp.sum(parts.astype(F32), axis=0)


def local(
    expression,
    cell_xy,
    live_mask,
    lengths,
    ramp_step,
    latent_noise,
    gene_embed,
    ln1_gain,
    ln1_bias,
    w_query,
    w_key,
    w_value,
    w_out,
    ln2_gain,
    ln2_bias,
    w_up,
    w_down,
    w_mean,
    w_logvar,
    comp_mean,
    comp_logvar,
    w_dec,
    w_genes,
):
    micro_count = lengths.shape[0]
    cells = expression.shape[0] // micro_count
    micro = lax.axis_index("section")
    latent_cols = w_mean.shape[1]
    comp_count, comp_width = comp_mean.shape
    width = ln1_gain.shape[0]
    shards = 2 * lax.axis_size("dp")
    features = shards * width
    tiled = width % 128 == 0 and lax.axis_size("dp") == 4
    meeting = functools.partial(meet, tiled)

    def own(array, axis=0):
        return lax.dynamic_slice_in_dim(array, micro * cells, cells, axis)

    genes_in = own(expression)
    alive = own(live_mask)
    alive_float = alive.astype(F32)
    noise = own(latent_noise)
    slide = slide_ids(lax.dynamic_index_in_dim(lengths, micro, 0, False), cells)
    allowed = allowed_pairs(slide, alive)
    positions = position_code(own(cell_xy, 1), features)

    norm_block = jnp.pad(jnp.stack([ln1_gain, ln1_bias, ln2_gain, ln2_bias]), ((0, 12), (0, 0)))
    comp_block = jnp.pad(
        jnp.concatenate([comp_mean, comp_logvar], axis=0), ((0, 0), (0, width - comp_width))
    )
    small = jnp.concatenate([norm_block, comp_block], axis=0)
    small_rows = small.shape[0]
    _, (embed, small_all), _, _, _, _ = meeting(0, gathers=((gene_embed, 1), (small, 0)))
    small_all = small_all.reshape(shards, small_rows, width).astype(F32)
    norm_params = small_all[:, :4].transpose(1, 0, 2).reshape(4, features)
    gain_one, bias_one, gain_two, bias_two = (norm_params[i : i + 1] for i in range(4))
    comps = small_all[:, 16:, :comp_width].transpose(1, 0, 2).reshape(2 * comp_count, -1)
    centers, spreads = comps[:comp_count], comps[comp_count:]

    qkv_shard = jnp.concatenate([w_query, w_key, w_value], axis=1)
    (summed,), (qkv, out_w, up_w), _, _, _, _ = meeting(
        1, (expression, embed, False, True), gathers=((qkv_shard, 0), (w_out, 1), (w_up, 0))
    )
    start = summed + positions
    normed_one, scale_one = normalize(start)
    first_low = (normed_one * gain_one + bias_one).astype(BF16)
    projected = mat_nn(first_low, qkv).astype(BF16)
    queries, keys, values = jnp.split(projected, 3, axis=1)
    attended, log_totals = attend(queries, keys, values, allowed)
    latent_shard = jnp.concatenate([w_mean, w_logvar], axis=1)
    (summed,), (down_w, latent_w, dec_w), _, _, _, _ = meeting(
        2, (attended, out_w, False, False), gathers=((w_down, 1), (latent_shard, 0), (w_dec, 1))
    )
    after_attn = start + summed
    normed_two, scale_two = normalize(after_attn)
    second_low = (normed_two * gain_two + bias_two).astype(BF16)
    upper = mat_nn(second_low, up_w)
    activated = gelu(upper).astype(BF16)
    (summed,), (genes_w,), _, _, _, _ = meeting(
        3, (activated, down_w, False, False), gathers=((w_genes, 0),)
    )
    hidden = (after_attn + summed).astype(BF16)

    stats = mat_nn(hidden, latent_w)
    means, log_vars = stats[:, :latent_cols], stats[:, latent_cols:]
    spread = jnp.exp(0.5 * log_vars) * noise
    latent = means + spread
    latent_low = latent.astype(BF16)
    post_part = jnp.sum(-0.5 * LOG_TWO_PI - 0.5 * log_vars - 0.5 * noise * noise, axis=1)
    precision = jnp.exp(-spreads)
    offsets = latent[None] - centers[:, None, :]
    pulled = offsets * precision[:, None, :]
    comp_part = jnp.sum(
        -0.5 * LOG_TWO_PI - 0.5 * spreads[:, None, :] - 0.5 * offsets * pulled, axis=2
    )
    density_part = jnp.pad(
        jnp.concatenate([comp_part, post_part[None]], axis=0), ((0, 7), (0, -cells % 128))
    )
    (decoder_pre,), _, _, _, (density_parts,), _ = meeting(
        4, (latent_low, dec_w, False, False), shares=(density_part,)
    )
    densities = jnp.sum(density_parts, axis=0)[:, :cells]
    logits = densities[:comp_count] - math.log(comp_count)
    log_post = densities[comp_count]
    largest = jnp.max(logits, axis=0, keepdims=True)
    log_prior = largest[0] + jnp.log(jnp.sum(jnp.exp(logits - largest), axis=0))
    respons = jnp.exp(logits - log_prior[None, :])
    divergence = jnp.sum((log_post - log_prior) * alive_float)
    decoder_act = lax.optimization_barrier(gelu(decoder_pre).astype(BF16))
    residual = (mat_nn(decoder_act, genes_w) - genes_in.astype(F32)) * alive_float[:, None]
    grad_rebuilt = residual.astype(BF16)

    grad_genes = mat_tn(decoder_act, grad_rebuilt).astype(BF16)
    counts = jnp.concatenate(
        [jnp.full((1, 128), divergence), jnp.full((31, 128), jnp.sum(alive_float))], axis=0
    )
    (grad_act,), (count_parts,), (genes_other,), _, _, _ = meeting(
        5, (grad_rebuilt, genes_w, True, False), gathers=((counts, 0),), swaps=((grad_genes, 0),)
    )
    count_parts = jnp.sum(count_parts.reshape(shards, 32, 128)[:, :, 0], axis=0)
    mean_kl = count_parts[0] / (LATENT * count_parts[1])
    ramp_weight = jnp.minimum(1.0, (ramp_step[0] + 1).astype(F32) / RAMP)
    kl_scale = (
        ramp_weight * jax.nn.softplus(mean_kl - FREE_BITS) * jax.nn.sigmoid(mean_kl - FREE_BITS)
    )
    grad_pre = (grad_act * gelu_slope(decoder_pre)).astype(BF16)
    grad_dec = mat_tn(latent_low, grad_pre).astype(BF16)
    cell_weight = kl_scale * alive_float
    weighted = (respons * cell_weight[None, :])[:, :, None]
    grad_latent = mat_nt(grad_pre, dec_w) + jnp.sum(weighted * pulled, axis=0)
    grad_comps = jnp.concatenate(
        [
            -jnp.sum(weighted * pulled, axis=1),
            -jnp.sum(weighted * (0.5 * offsets * pulled - 0.5), axis=1),
        ],
        axis=0,
    )
    grad_means = grad_latent.astype(BF16)
    grad_logs = (grad_latent * (0.5 * spread) - 0.5 * cell_weight[:, None]).astype(BF16)
    grad_stats = jnp.concatenate([grad_means, grad_logs], axis=1)
    grad_latent_w = mat_tn(hidden, grad_stats).astype(BF16)
    (summed,), _, (latent_other, dec_other), (genes_parts,), _, _ = meeting(
        6,
        (grad_stats, latent_w, True, False),
        swaps=((grad_latent_w, 0), (grad_dec, 1)),
        exchanges=((grad_genes, genes_other, 0),),
    )
    grad_hidden = summed.astype(BF16)

    grad_down = mat_tn(activated, grad_hidden).astype(BF16)
    grad_upper = (mat_nt(grad_hidden, down_w) * gelu_slope(upper)).astype(BF16)
    grad_up = mat_tn(second_low, grad_upper).astype(BF16)
    (grad_norm_two,), _, (down_other, up_other), (latent_parts, dec_parts), _, _ = (
        meeting(
            7,
            (grad_upper, up_w, True, False),
            swaps=((grad_down, 1), (grad_up, 0)),
            exchanges=(
                (grad_latent_w, latent_other, 0),
                (grad_dec, dec_other, 1),
            ),
        )
    )
    grad_middle = grad_hidden.astype(F32) + norm_back(
        grad_norm_two, normed_two, scale_two, gain_two
    )
    middle_low = grad_middle.astype(BF16)
    grad_out = mat_tn(attended, middle_low).astype(BF16)
    grad_qkv_act = attend_back(middle_low, out_w, projected, log_totals, slide, alive)
    grad_qkv = mat_tn(first_low, grad_qkv_act).astype(BF16)
    (grad_norm_one,), _, (qkv_other, out_other), (down_parts, up_parts), _, _ = meeting(
        8,
        (grad_qkv_act, qkv, True, False),
        swaps=((grad_qkv, 0), (grad_out, 1)),
        exchanges=((grad_down, down_other, 1), (grad_up, up_other, 0)),
    )
    grad_start = grad_middle + norm_back(grad_norm_one, normed_one, scale_one, gain_one)
    start_low = grad_start.astype(BF16)

    norm_grads = jnp.stack(
        [
            jnp.sum(grad_norm_one * normed_one, axis=0),
            jnp.sum(grad_norm_one, axis=0),
            jnp.sum(grad_norm_two * normed_two, axis=0),
            jnp.sum(grad_norm_two, axis=0),
        ]
    )
    norm_grads = norm_grads.reshape(4, shards, width).transpose(1, 0, 2)
    comp_grads = grad_comps.reshape(2 * comp_count, shards, comp_width).transpose(1, 0, 2)
    small_grads = jnp.concatenate(
        [
            jnp.pad(norm_grads, ((0, 0), (0, 12), (0, 0))),
            jnp.pad(comp_grads, ((0, 0), (0, 0), (0, width - comp_width))),
        ],
        axis=1,
    ).reshape(shards * small_rows, width)
    if tiled:
        embed_parts, qkv_parts, out_parts, small_sum, grad_expression = tail(
            9,
            start_low,
            expression,
            embed,
            grad_rebuilt,
            grad_qkv,
            qkv_other,
            grad_out,
            out_other,
            small_grads.reshape(2, shards // 2, small_rows, width),
        )
    else:
        start_all = lax.all_gather(start_low, "section", axis=0, tiled=True)
        start_half = lax.dynamic_slice_in_dim(start_all, micro * (features // 2), features // 2, 1)
        grad_embed = mat_tn(expression, start_half).astype(BF16)
        grad_cells = (
            mat_nt(start_low, embed).astype(BF16).astype(F32) - grad_rebuilt.astype(F32)
        ).astype(BF16)
        grad_expression = lax.all_gather(grad_cells, "section", axis=0, tiled=True)
        small_other = lax.ppermute(
            lax.dynamic_slice_in_dim(
                small_grads, (1 - micro) * (shards // 2 * small_rows), shards // 2 * small_rows, 0
            ),
            "section",
            [(0, 1), (1, 0)],
        )
        _, _, _, (embed_parts, qkv_parts, out_parts, small_sum), _, _ = meeting(
            9,
            exchanges=(
                (grad_embed, None, 1),
                (grad_qkv, qkv_other, 0),
                (grad_out, out_other, 1),
                (small_grads, small_other, 0),
            ),
        )
    grad_query, grad_key, grad_value = jnp.split(qkv_parts, 3, axis=1)
    grad_mean, grad_logvar = jnp.split(latent_parts, 2, axis=1)
    return (
        embed_parts,
        small_sum[0],
        small_sum[1],
        grad_query,
        grad_key,
        grad_value,
        out_parts,
        small_sum[2],
        small_sum[3],
        up_parts,
        down_parts,
        grad_mean,
        grad_logvar,
        small_sum[16 : 16 + comp_count, :comp_width],
        small_sum[16 + comp_count :, :comp_width],
        dec_parts,
        genes_parts,
        grad_expression,
    )


def solution(mesh):
    weight_rows = P(("section", "dp"), "mp")
    weight_cols = P("mp", ("section", "dp"))
    vector = P(("section", "dp"))
    comps = P(None, ("mp", "section", "dp"))
    weights = (
        weight_cols, vector, vector, weight_rows, weight_rows, weight_rows, weight_cols,
        vector, vector, weight_rows, weight_cols, weight_rows, weight_rows, comps, comps,
        weight_cols, weight_rows,
    )
    return jax.shard_map(
        local,
        mesh=mesh,
        in_specs=(P("dp", "mp"), P(None, "dp"), P("dp"), P("dp", None), P(), P("dp", "mp"))
        + weights,
        out_specs=weights + (P("dp", "mp"),),
        check_vma=False,
    )
```

```python
import functools
import math

import jax
import jax.numpy as jnp
from jax import lax
from jax.experimental import pallas as pl
from jax.experimental.pallas import tpu as pltpu
from jax.sharding import PartitionSpec as P

HEAD = 64
LATENT = 512
RAMP = 1000
LOG_TWO_PI = 1.8378770664093453
NEG_LARGE = -1e30
FREE_BITS = 1.0
HOP_LAG = 3
WINDOW = 3
BLOCK_STEP = 4
TILE = 256
LINK_BYTES_PER_US = 92000.0
MOMENT_US = 1.3
SPREAD = 1
SPREAD_FROM = 0
SPREAD_STEP = 1
F32 = jnp.float32
BF16 = jnp.bfloat16


def mat_nn(left, right):
    return jnp.dot(left, right, preferred_element_type=F32)


def mat_tn(left, right):
    return lax.dot_general(left, right, (((0,), (0,)), ((), ())), preferred_element_type=F32)


def mat_nt(left, right):
    return lax.dot_general(left, right, (((1,), (1,)), ((), ())), preferred_element_type=F32)


def gelu(values):
    return 0.5 * values * (1.0 + lax.erf(values * 0.7071067811865476))


def gelu_slope(values):
    return (
        0.5 * (1.0 + lax.erf(values * 0.7071067811865476))
        + values * jnp.exp(-0.5 * values * values) * 0.3989422804014327
    )


def normalize(values):
    center = values - jnp.mean(values, axis=-1, keepdims=True)
    scale = lax.rsqrt(jnp.mean(center * center, axis=-1, keepdims=True) + 1e-05)
    return center * scale, scale


def norm_back(grad_in, normed, scale, gain):
    scaled = grad_in * gain
    return scale * (
        scaled
        - jnp.mean(scaled, axis=-1, keepdims=True)
        - normed * jnp.mean(scaled * normed, axis=-1, keepdims=True)
    )


def position_code(places, feature_count):
    quarter = feature_count // 4
    frequency = jnp.exp(jnp.arange(quarter, dtype=F32) * (-math.log(10000.0) / quarter))
    along_x = places[0][:, None] * frequency[None, :]
    along_y = places[1][:, None] * frequency[None, :]
    return jnp.concatenate(
        [jnp.sin(along_x), jnp.cos(along_x), jnp.sin(along_y), jnp.cos(along_y)], axis=1
    )


def slide_ids(length_row, cell_count):
    bounds = jnp.cumsum(length_row)[:-1]
    index = jnp.arange(cell_count, dtype=jnp.int32)
    return jnp.sum((index[:, None] >= bounds[None, :]).astype(jnp.int32), axis=1)


def allowed_pairs(slide, alive):
    index = jnp.arange(alive.shape[0], dtype=jnp.int32)
    return (slide[:, None] == slide[None, :]) & (
        (alive[None, :] == 1) | (index[:, None] == index[None, :])
    )


def heads_of(array):
    return array.reshape(array.shape[0], -1, HEAD)


def attend(queries, keys, values, allowed):
    factor = HEAD ** (-0.5)
    scores = (
        jnp.einsum("qhd,khd->hqk", heads_of(queries), heads_of(keys), preferred_element_type=F32)
        * factor
    )
    scores = jnp.where(allowed[None], scores, NEG_LARGE)
    largest = jnp.max(scores, axis=2, keepdims=True)
    exponents = jnp.exp(scores - largest)
    sums = jnp.sum(exponents, axis=2, keepdims=True)
    probs = (exponents / sums).astype(BF16)
    out = jnp.einsum("hqk,khd->qhd", probs, heads_of(values), preferred_element_type=F32)
    return out.reshape(queries.shape).astype(BF16), largest + jnp.log(sums)


def attend_back_kernel(middle, out_w, projected, log_totals, slide_keys, slide_queries, alive_keys, out):
    cells, width = out.shape[0], out.shape[1] // 3
    factor = HEAD ** (-0.5)
    shape = (cells, cells)
    own_key = lax.broadcasted_iota(jnp.int32, shape, 0) == lax.broadcasted_iota(jnp.int32, shape, 1)
    allowed = (slide_keys[...] == slide_queries[...]) & ((alive_keys[...] == 1) | own_key)
    grad_out = mat_nt(middle[...], out_w[...]).astype(BF16)
    for head in range(width // HEAD):
        first = head * HEAD
        q = projected[:, first : first + HEAD]
        k = projected[:, width + first : width + first + HEAD]
        v = projected[:, 2 * width + first : 2 * width + first + HEAD]
        g = grad_out[:, first : first + HEAD]
        scores = mat_nt(k, q) * factor - log_totals[head : head + 1, :]
        probs = jnp.where(allowed, jnp.exp(jnp.minimum(scores, 0.0)), 0.0)
        grad_probs = mat_nt(v, g)
        inner = jnp.sum(probs * grad_probs, axis=0, keepdims=True)
        grad_scores = (probs * (grad_probs - inner)).astype(BF16)
        out[:, first : first + HEAD] = (mat_tn(grad_scores, k) * factor).astype(BF16)
        out[:, width + first : width + first + HEAD] = (mat_nn(grad_scores, q) * factor).astype(BF16)
        out[:, 2 * width + first : 2 * width + first + HEAD] = mat_nn(
            probs.astype(BF16), g
        ).astype(BF16)


def attend_back(middle, out_w, projected, log_totals, slide, alive):
    return pl.pallas_call(
        attend_back_kernel,
        out_shape=jax.ShapeDtypeStruct(projected.shape, BF16),
        compiler_params=pltpu.CompilerParams(vmem_limit_bytes=48 * 2**20),
        name="attend_back",
    )(
        middle,
        out_w,
        projected,
        log_totals[:, :, 0],
        slide[:, None],
        slide[None, :],
        alive[:, None],
    )


def part_of(ref, axis, index, size):
    span = pl.ds(index * size, size)
    if axis == 0:
        return ref.at[span, :]
    return ref.at[:, pl.ds(pl.multiple_of(index * size, 128), size)]


def settle_plain(out, place, value):
    out[place] = value


def line_sum(produce, hooks, settle, part, out, from_left, from_right, to_right, to_left, got_left, got_right, sent_right, sent_left):
    me, count = lax.axis_index("mp"), lax.axis_size("mp")
    pieces, height, width = from_left.shape
    splits = pieces * width // part.shape[1]
    stride = (part.shape[0] - height) // (splits - 1)
    has_right, has_left = me < count - 1, me > 0

    def place(piece):
        return (
            pl.ds(pl.multiple_of(lax.rem(piece, splits) * stride, 16), height),
            pl.ds(pl.multiple_of(lax.div(piece, splits) * width, width), width),
        )

    def rightward(piece):
        return pltpu.make_async_remote_copy(
            src_ref=to_right.at[piece],
            dst_ref=from_left.at[piece],
            send_sem=sent_right.at[piece],
            recv_sem=got_left.at[piece],
            device_id={"mp": me + 1},
        )

    def leftward(piece):
        return pltpu.make_async_remote_copy(
            src_ref=to_left.at[piece],
            dst_ref=from_right.at[piece],
            send_sem=sent_left.at[piece],
            recv_sem=got_right.at[piece],
            device_id={"mp": me - 1},
        )

    def flow(piece, copy, has_source, has_target, source, target):
        @pl.when((piece >= 0) & (piece < pieces))
        def _():
            @pl.when(has_source)
            def _():
                copy(piece).wait_recv()

            @pl.when(has_target & has_source)
            def _():
                target[piece] = (part[place(piece)] + source[piece].astype(F32)).astype(BF16)

            @pl.when(has_target & jnp.logical_not(has_source))
            def _():
                target[piece] = part[place(piece)].astype(BF16)

            @pl.when(has_target & (piece >= WINDOW))
            def _():
                copy(piece - WINDOW).wait_send()

            @pl.when(has_target)
            def _():
                copy(piece).start()

    moments = pieces + HOP_LAG * (count - 1)
    right_half = lax.div(2 * me + 1, count)
    trail = HOP_LAG * (right_half * me + (1 - right_half) * (count - 1 - me))

    def step(moment, carry):
        produce(moment)
        flow(moment - HOP_LAG * me, rightward, has_left, has_right, from_left, to_right)
        flow(
            moment - HOP_LAG * (count - 1 - me), leftward, has_right, has_left, from_right, to_left
        )
        done = moment - trail
        finished = (done >= 0) & (done < pieces)

        @pl.when(finished & has_left & has_right)
        def _():
            settle(
                out,
                place(done),
                part[place(done)] + from_left[done].astype(F32) + from_right[done].astype(F32),
            )

        @pl.when(finished & jnp.logical_not(has_left))
        def _():
            settle(out, place(done), part[place(done)] + from_right[done].astype(F32))

        @pl.when(finished & jnp.logical_not(has_right))
        def _():
            settle(out, place(done), part[place(done)] + from_left[done].astype(F32))

        return carry

    def finish():
        def step(piece, carry):
            @pl.when(has_right)
            def _():
                rightward(piece).wait_send()

            @pl.when(has_left)
            def _():
                leftward(piece).wait_send()

            return carry

        lax.fori_loop(pieces - WINDOW, pieces, step, 0)

    reached = 0
    for when, hook in hooks:
        if when > reached:
            lax.fori_loop(reached, when, step, 0)
            reached = when
        hook()
    lax.fori_loop(reached, moments, step, 0)
    finish()


PRODUCT_SCRATCH = 5


def start_product(form, left, right, part, left_in, right_in, left_sem, right_sem):
    transposed, sliced = form
    blocks = right_in.shape[0]
    width = part.shape[1] // blocks
    if sliced:
        rows = left_in.shape[0]
        first = pl.multiple_of(lax.axis_index("section") * rows, 16)
        left_copy = pltpu.make_async_copy(left.at[pl.ds(first, rows), :], left_in, left_sem)
        left_copy.start()

    def right_copy(block):
        span = pl.ds(pl.multiple_of(block * width, width), width)
        view = right.at[span, :] if transposed else right.at[:, span]
        return pltpu.make_async_copy(view, right_in.at[block], right_sem.at[block])

    for block in range(blocks):
        right_copy(block).start()
    if sliced:
        left_copy.wait()

    def produce(moment):
        @pl.when((lax.rem(moment, BLOCK_STEP) == 0) & (moment < blocks * BLOCK_STEP))
        def _():
            block = lax.div(moment, BLOCK_STEP)
            right_copy(block).wait()
            contract = (((1,), (1 if transposed else 0,)), ((), ()))
            part[:, pl.ds(pl.multiple_of(block * width, width), width)] = lax.dot_general(
                (left_in if sliced else left)[...],
                right_in[block],
                contract,
                preferred_element_type=F32,
            )

    return produce


def halfway(rows):
    return rows // 32 * 16


def block_of(ref, axis, index, size, start=0, stop=None):
    if axis == 0:
        stop = size if stop is None else stop
        return ref.at[pl.ds(pl.multiple_of(index * size + start, 16), stop - start), :]
    stop = ref.shape[0] if stop is None else stop
    return ref.at[pl.ds(start, stop - start), pl.ds(pl.multiple_of(index * size, 128), size)]


def reaction_moments(travelling):
    third = travelling / LINK_BYTES_PER_US
    last = 2 * len(range(8)) + 3 * HOP_LAG - 1
    return [
        min(last, math.ceil((parts * third + 2.0 + 0.5 * parts) / MOMENT_US)) for parts in (1, 2)
    ]


def comm_kernel(plan, *refs):
    refs = list(refs)

    def take(number):
        taken = refs[:number]
        del refs[:number]
        return taken

    reduces, gathers, swaps, exchanges, shares, pairs, travelling = plan
    groups = (len(gathers), len(swaps), len(exchanges), shares, pairs)
    sources = [take(n) for n in (2 if reduces else 0,) + groups]
    others = [take(1)[0] if paired else None for _, _, paired in exchanges]
    results = [take(n) for n in (1 if reduces else 0,) + groups]
    product = take(PRODUCT_SCRATCH) if reduces else None
    line = take(8) if reduces else None
    staging = [take(4 + paired) for _, _, paired in exchanges]
    sent, got, local_sem = refs

    section, z, dp = (lax.axis_index(name) for name in ("section", "mp", "dp"))
    count_z, count_dp = lax.axis_size("mp"), lax.axis_size("dp")
    row, col = dp // 2, dp % 2
    peer_x, peer_y = row * 2 + (1 - col), (1 - row) * 2 + col
    peer_d = (1 - row) * 2 + (1 - col)
    partner, to_x, to_y = {"section": 1 - section}, {"dp": peer_x}, {"dp": peer_y}

    barrier = pltpu.get_barrier_semaphore()
    fixed = 0
    if gathers or swaps or pairs:
        pl.semaphore_signal(barrier, inc=1, device_id=partner)
        fixed += 1
    if gathers or exchanges:
        pl.semaphore_signal(barrier, inc=1, device_id=to_x)
        pl.semaphore_signal(barrier, inc=1, device_id=to_y)
        fixed += 2
    if shares:
        for step in range(1, count_z):
            pl.semaphore_signal(barrier, inc=1, device_id={"mp": (z + step) % count_z})
        fixed += count_z - 1
    elif reduces:
        for exists, neighbour in ((z > 0, z - 1), (z < count_z - 1, z + 1)):

            @pl.when(exists)
            def _(neighbour=neighbour):
                pl.semaphore_signal(barrier, inc=1, device_id={"mp": neighbour})

        at_end = (z == 0) | (z == count_z - 1)

        @pl.when(at_end)
        def _():
            pl.semaphore_wait(barrier, fixed + 1)

        @pl.when(jnp.logical_not(at_end))
        def _():
            pl.semaphore_wait(barrier, fixed + 2)

    if fixed and (shares or not reduces):
        pl.semaphore_wait(barrier, fixed)

    used = [0, 0]

    def remote(src, dst, device):
        index = used[0]
        used[0] += 1
        return pltpu.make_async_remote_copy(
            src_ref=src, dst_ref=dst, send_sem=sent.at[index], recv_sem=got.at[index], device_id=device
        )

    def within(src, dst):
        index = used[1]
        used[1] += 1
        return pltpu.make_async_copy(src, dst, local_sem.at[index])

    locals_, early, first, second = [], [], [], []
    after_one, after_two, after_three = [], [], []
    receives, loads = [], []
    starts_d, starts_xy, conclusions = [], [], []
    for item, (axis, size) in enumerate(swaps):
        src, dst = sources[2][item], results[2][item]
        copy = remote(part_of(src, axis, 1 - section, size), dst, partner)
        early.append(copy)
        receives.append(copy)
    for item in range(pairs):
        copy = remote(sources[5][item], results[5][item], partner)
        early.append(copy)
        receives.append(copy)
    for item in range(shares):
        src, dst = sources[4][item], results[4][item]
        locals_.append(within(src, dst.at[z]))
        for step in range(1, count_z):
            copy = remote(src, dst.at[z], {"mp": (z + step) % count_z})
            early.append(copy)
            receives.append(copy)
    for item, (axis, size) in enumerate(gathers):
        src, dst = sources[1][item], results[1][item]
        rows = src.shape[0]
        cut = halfway(rows)

        def shard_of(index, start=0, stop=rows, dst=dst, axis=axis, size=size):
            return block_of(dst, axis, section * count_dp + index, size, start, stop)

        upper, lower = src.at[pl.ds(0, cut), :], src.at[pl.ds(cut, rows - cut), :]
        locals_.append(within(src, shard_of(dp)))
        own = remote(src, shard_of(dp), partner)
        x_upper = remote(upper, shard_of(dp, 0, cut), to_x)
        y_lower = remote(lower, shard_of(dp, cut), to_y)
        x_lower = remote(lower, shard_of(dp, cut), to_x)
        y_upper = remote(upper, shard_of(dp, 0, cut), to_y)
        pass_y = remote(shard_of(peer_x, 0, cut), shard_of(peer_x, 0, cut), to_y)
        pass_x = remote(shard_of(peer_y, cut), shard_of(peer_y, cut), to_x)
        relay_x = remote(shard_of(peer_x), shard_of(peer_x), partner)
        relay_y = remote(shard_of(peer_y), shard_of(peer_y), partner)
        relay_upper = remote(shard_of(peer_d, 0, cut), shard_of(peer_d, 0, cut), partner)
        relay_lower = remote(shard_of(peer_d, cut), shard_of(peer_d, cut), partner)
        early.append(own)
        first += [x_upper, y_lower]
        second += [x_lower, y_upper]
        after_one += [([x_upper], None, pass_y), ([y_lower], None, pass_x)]
        after_two += [([x_lower], None, relay_x), ([y_upper], None, relay_y)]
        after_three += [([pass_y], None, relay_upper), ([pass_x], None, relay_lower)]
        receives += [own, relay_x, relay_y, relay_upper, relay_lower]
    for item, (axis, size, paired) in enumerate(exchanges):
        src, dst = sources[3][item], results[3][item]
        mine, from_x, from_y, inbound = staging[item][:4]
        rows, dtype = from_x.shape[0], from_x.dtype
        cut = halfway(rows)
        rest = rows - cut
        half = section * count_dp if paired else 0
        fetched = []
        for role, index in enumerate((peer_d, peer_x, peer_y, dp)):
            copies = [within(block_of(src, axis, half + index, size), mine.at[role])]
            if paired:
                copies.append(
                    within(block_of(others[item], axis, index, size), staging[item][4].at[role])
                )
            fetched.append(copies)
            loads += copies

        def merge(role, mine=mine, other=staging[item][-1] if paired else None):
            def run():
                if other is not None:
                    mine[role] = (mine[role].astype(F32) + other[role].astype(F32)).astype(mine.dtype)

            return run

        top, bottom = pl.ds(0, cut), pl.ds(cut, rest)
        d_upper = remote(mine.at[0, top, :], inbound.at[top, :], to_x)
        d_lower = remote(mine.at[0, bottom, :], inbound.at[bottom, :], to_y)
        x_upper = remote(mine.at[1, top, :], from_x.at[top, :], to_x)
        y_lower = remote(mine.at[2, bottom, :], from_y.at[bottom, :], to_y)
        y_upper = remote(mine.at[2, top, :], from_y.at[top, :], to_y)
        x_lower = remote(mine.at[1, bottom, :], from_x.at[bottom, :], to_x)

        def add(role, span, mine=mine, term=inbound):
            def run():
                mine[role, span, :] = (
                    mine[role, span, :].astype(F32) + term[span, :].astype(F32)
                ).astype(mine.dtype)

            return run

        def conclude(mine=mine, from_x=from_x, from_y=from_y, dst=dst):
            dst[...] = mine[3].astype(F32) + from_x[...].astype(F32) + from_y[...].astype(F32)

        starts_d += [(fetched[0], merge(0), [d_upper, d_lower])]
        starts_xy += [
            (fetched[1], merge(1), [x_upper]),
            (fetched[2], merge(2), [y_lower]),
            (fetched[3], merge(3), []),
        ]
        after_one += [
            ([d_upper], add(2, top), y_upper),
            ([d_lower], add(1, bottom), x_lower),
        ]
        receives += [x_upper, y_lower, y_upper, x_lower]
        conclusions.append(conclude)

    remotes = early + first + second

    def begin():
        for copy in loads + remotes + locals_:
            copy.start()

    def send_parts():
        for copies, compute, targets in starts_d + starts_xy:
            for copy in copies:
                copy.wait()
            compute()
            for copy in targets:
                copy.start()

    def react(items):
        def run():
            for waits, compute, copy in items:
                for wait in waits:
                    wait.wait_recv()
                if compute is not None:
                    compute()
                copy.start()

        return run

    if reduces:
        produce = start_product(reduces, *sources[0], *product)
        moments = reaction_moments(travelling)
        hooks = [(0, begin), (2, send_parts), (moments[0], react(after_one)), (moments[1], react(after_two))]
        line_sum(produce, hooks, settle_plain, product[0], results[0][0], *line)
    else:
        begin()
        send_parts()
        react(after_one)()
        react(after_two)()
    react(after_three)()
    for copy in receives:
        copy.wait_recv()
    for conclude in conclusions:
        conclude()
    started = remotes + [copy for _, _, copies in starts_d + starts_xy for copy in copies]
    started += [copy for _, _, copy in after_one + after_two + after_three]
    for copy in started:
        copy.wait_send()
    for copy in locals_:
        copy.wait()


def comm(number, reduce=None, gathers=(), swaps=(), exchanges=(), shares=(), pairs=(), name="meet"):
    count_dp, count_z = lax.axis_size("dp"), lax.axis_size("mp")
    sections = lax.axis_size("section")

    def resized(shape, axis, size):
        return shape[:axis] + (size,) + shape[axis + 1 :]

    inputs, outputs, scratch = [], [], []
    plan_gathers, plan_swaps, plan_exchanges = [], [], []
    remote_count = local_count = travelling = 0
    reduces = None
    if reduce is not None:
        left, right, transposed, sliced = reduce
        reduces = (transposed, sliced)
        rows, depth = left.shape[0] // (sections if sliced else 1), left.shape[1]
        width = right.shape[0 if transposed else 1]
        blocks = width // 256
        inputs += [left, right]
        outputs.append(jax.ShapeDtypeStruct((rows, width), F32))
        scratch += [
            pltpu.VMEM((rows, width), F32),
            pltpu.VMEM((rows, depth) if sliced else (16, 128), BF16),
            pltpu.VMEM((blocks, 256, depth) if transposed else (blocks, depth, 256), BF16),
            pltpu.SemaphoreType.DMA,
            pltpu.SemaphoreType.DMA((blocks,)),
        ]
        buffer = pltpu.VMEM((width // 64, 256, 128), BF16)
        scratch += [buffer] * 4 + [pltpu.SemaphoreType.DMA((width // 64,))] * 4
    for shard, axis in gathers:
        size = shard.shape[axis]
        inputs.append(shard)
        outputs.append(
            jax.ShapeDtypeStruct(resized(shard.shape, axis, size * sections * count_dp), shard.dtype)
        )
        plan_gathers.append((axis, size))
        travelling += shard.size * shard.dtype.itemsize
        remote_count += 11
        local_count += 1
    for array, axis in swaps:
        size = array.shape[axis] // sections
        inputs.append(array)
        outputs.append(jax.ShapeDtypeStruct(resized(array.shape, axis, size), array.dtype))
        plan_swaps.append((axis, size))
        remote_count += 1
    other_inputs = []
    for array, other, axis in exchanges:
        paired = other is not None
        size = array.shape[axis] // (count_dp * (sections if paired else 1))
        piece = resized(array.shape, axis, size)
        inputs.append(array)
        outputs.append(jax.ShapeDtypeStruct(piece, F32))
        plan_exchanges.append((axis, size, paired))
        roles, one = pltpu.VMEM((4,) + piece, array.dtype), pltpu.VMEM(piece, array.dtype)
        scratch += [roles, one, one, one]
        if paired:
            other_inputs.append(other)
            scratch.append(roles)
        travelling += piece[0] * piece[1] * array.dtype.itemsize
        remote_count += 6
        local_count += 8
    for array in shares:
        inputs.append(array)
        outputs.append(jax.ShapeDtypeStruct((count_z,) + array.shape, array.dtype))
        remote_count += count_z - 1
        local_count += 1
    for array in pairs:
        inputs.append(array)
        outputs.append(jax.ShapeDtypeStruct(array.shape, array.dtype))
        remote_count += 1
    inputs += other_inputs
    scratch += [
        pltpu.SemaphoreType.DMA((max(remote_count, 1),)),
        pltpu.SemaphoreType.DMA((max(remote_count, 1),)),
        pltpu.SemaphoreType.DMA((max(local_count, 1),)),
    ]
    plan = (reduces, tuple(plan_gathers), tuple(plan_swaps), tuple(plan_exchanges), len(shares), len(pairs), travelling)
    placed = [True] * (reduces is not None) + [False] * (len(gathers) + len(swaps))
    placed += [True] * len(exchanges) + [False] * (len(shares) + len(pairs))
    vmem, anywhere = pl.BlockSpec(memory_space=pltpu.VMEM), pl.BlockSpec(memory_space=pl.ANY)
    outs = pl.pallas_call(
        functools.partial(comm_kernel, plan),
        out_shape=outputs,
        in_specs=([] if reduces is None else [anywhere if reduces[1] else vmem])
        + [anywhere] * (len(inputs) - (0 if reduces is None else 1)),
        out_specs=[vmem if in_vmem else anywhere for in_vmem in placed],
        scratch_shapes=scratch,
        compiler_params=pltpu.CompilerParams(
            collective_id=number, has_side_effects=True, vmem_limit_bytes=48 * 2**20
        ),
        cost_estimate=pl.CostEstimate(flops=1000000, bytes_accessed=90000000, transcendentals=0),
        name=name,
    )(*inputs)
    outs = list(outs)
    split = []
    for number_of in (1 if reduces else 0, len(gathers), len(swaps), len(exchanges), len(shares), len(pairs)):
        split.append(outs[:number_of])
        outs = outs[number_of:]
    return split


def spread(remote, src, dst, axis, size, section, dp, peers, partner, to_x, to_y):
    count_dp = lax.axis_size("dp")
    rows = src.shape[0]
    cut = halfway(rows)
    peer_x, peer_y, peer_d = peers

    def shard_of(index, start=0, stop=rows):
        return block_of(dst, axis, section * count_dp + index, size, start, stop)

    def still(*place):
        return (shard_of(*place), shard_of(*place))

    upper, lower = src.at[pl.ds(0, cut), :], src.at[pl.ds(cut, rows - cut), :]
    return {
        "own": remote(src, shard_of(dp), partner),
        "x_upper": remote(upper, shard_of(dp, 0, cut), to_x),
        "y_lower": remote(lower, shard_of(dp, cut), to_y),
        "x_lower": remote(lower, shard_of(dp, cut), to_x),
        "y_upper": remote(upper, shard_of(dp, 0, cut), to_y),
        "pass_y": remote(*still(peer_x, 0, cut), to_y),
        "pass_x": remote(*still(peer_y, cut), to_x),
        "relay_x": remote(*still(peer_x), partner),
        "relay_y": remote(*still(peer_y), partner),
        "relay_upper": remote(*still(peer_d, 0, cut), partner),
        "relay_lower": remote(*still(peer_d, cut), partner),
    }


def spread_steps(copies):
    def begin():
        for name in ("own", "x_upper", "y_lower", "x_lower", "y_upper"):
            copies[name].start()

    def follow(pairs):
        def run():
            for arrived, onward in pairs:
                copies[arrived].wait_recv()
                copies[onward].start()

        return run

    one = follow((("x_upper", "pass_y"), ("y_lower", "pass_x")))
    two = follow((("x_lower", "relay_x"), ("y_upper", "relay_y")))
    three = follow((("pass_y", "relay_upper"), ("pass_x", "relay_lower")))
    return begin, one, two, three


def head_kernel(plan, *refs):
    refs = list(refs)

    def take(number):
        taken = refs[:number]
        del refs[:number]
        return taken

    count = len(plan)
    places, frequency, expression, embed = take(4)
    shards = take(count)
    start, embed_all = take(2)
    gathered = take(count)
    part, codes, cells_in, columns_in, cells_sem, columns_sem = take(6)
    held = take(count)
    line = take(8)
    sent, got, local_sem = refs

    section, z, dp = (lax.axis_index(name) for name in ("section", "mp", "dp"))
    count_z, count_dp = lax.axis_size("mp"), lax.axis_size("dp")
    row, col = dp // 2, dp % 2
    peer_x, peer_y = row * 2 + (1 - col), (1 - row) * 2 + col
    peer_d = (1 - row) * 2 + (1 - col)
    peers = (peer_x, peer_y, peer_d)
    partner, to_x, to_y = {"section": 1 - section}, {"dp": peer_x}, {"dp": peer_y}
    rows, width = cells_in.shape[0], embed.shape[1]

    barrier = pltpu.get_barrier_semaphore()
    for device in (partner, to_x, to_y):
        pl.semaphore_signal(barrier, inc=1, device_id=device)
    for exists, neighbour in ((z > 0, z - 1), (z < count_z - 1, z + 1)):

        @pl.when(exists)
        def _(neighbour=neighbour):
            pl.semaphore_signal(barrier, inc=1, device_id={"mp": neighbour})

    at_end = (z == 0) | (z == count_z - 1)

    @pl.when(at_end)
    def _():
        pl.semaphore_wait(barrier, 4)

    @pl.when(jnp.logical_not(at_end))
    def _():
        pl.semaphore_wait(barrier, 5)

    used = [0, 0]

    def remote(src, dst, device):
        index = used[0]
        used[0] += 1
        return pltpu.make_async_remote_copy(
            src_ref=src, dst_ref=dst, send_sem=sent.at[index], recv_sem=got.at[index], device_id=device
        )

    def within(src, dst):
        index = used[1]
        used[1] += 1
        return pltpu.make_async_copy(src, dst, local_sem.at[index])

    place = (section, dp, peers, partner, to_x, to_y)
    main = spread(remote, embed, embed_all, 1, width, *place)
    begin, one, two, three = spread_steps(main)
    rest = [
        spread(remote, src, dst, axis, size, *place)
        for src, dst, (axis, size) in zip(shards, gathered, plan)
    ]
    rest_steps = [spread_steps(copies) for copies in rest]
    loads = [within(src, room) for src, room in zip(shards, held)]
    kept = [within(columns_in.at[0], block_of(embed_all, 1, section * count_dp + dp, width))]
    kept += [
        within(room, block_of(dst, axis, section * count_dp + dp, size))
        for room, dst, (axis, size) in zip(held, gathered, plan)
    ]

    order = [
        section * count_dp + dp,
        (1 - section) * count_dp + dp,
        section * count_dp + peer_x,
        section * count_dp + peer_y,
        (1 - section) * count_dp + peer_x,
        (1 - section) * count_dp + peer_y,
        section * count_dp + peer_d,
        (1 - section) * count_dp + peer_d,
    ]

    first = pl.multiple_of(section * rows, 16)
    cells_copy = pltpu.make_async_copy(expression.at[pl.ds(first, rows), :], cells_in, cells_sem)

    def fetch(turn):
        src = embed if turn == 0 else block_of(embed_all, 1, order[turn], width)
        return pltpu.make_async_copy(src, columns_in.at[turn], columns_sem.at[turn])

    begin()
    cells_copy.start()
    fetch(0).start()
    for copy in loads:
        copy.start()

    quarter = frequency.shape[1]
    for axis in range(2):
        along = places[:, axis : axis + 1] * frequency[...]
        codes[:, 2 * axis * quarter : (2 * axis + 1) * quarter] = jnp.sin(along)
        codes[:, (2 * axis + 1) * quarter : (2 * axis + 2) * quarter] = jnp.cos(along)
    cells_copy.wait()

    def keep():
        for copy in loads:
            copy.wait()
        for copy in kept:
            copy.start()

    def produce(moment):
        turn = lax.div(moment, 2)

        @pl.when((lax.rem(moment, 2) == 0) & (turn < len(order)))
        def _():
            pltpu.make_async_copy(embed, columns_in.at[turn], columns_sem.at[turn]).wait()
            part[:, pl.ds(pl.multiple_of(turn * width, width), width)] = mat_nn(
                cells_in[...], columns_in[turn]
            )

    def settle(out, where, value):
        span, columns = where
        turn = lax.div(columns.start, width)
        block = sum(jnp.where(turn == index, target, 0) for index, target in enumerate(order))
        columns = pl.ds(pl.multiple_of(block * width, width), width)
        out[span, columns] = value + codes[span, columns]

    def arrived(names, turns):
        def run():
            for name in names:
                main[name].wait_recv()
            for turn in turns:
                fetch(turn).start()

        return run

    def neighbours():
        one()
        for steps in rest_steps:
            steps[0]()
        two()
        for turn in (2, 3):
            fetch(turn).start()

    def diagonal():
        three()
        fetch(6).start()

    def later(number):
        def run():
            for steps in rest_steps:
                steps[number]()

        return run

    hooks = [
        (1, keep),
        (2, arrived(("own",), (1,))),
        (4, neighbours),
        (8, arrived(("relay_x", "relay_y"), (4, 5))),
        (12, diagonal),
        (14, arrived(("relay_upper", "relay_lower"), (7,))),
        (17, later(1)),
        (21, later(2)),
    ]
    line_sum(produce, hooks, settle, part, start, *line)
    for steps in rest_steps:
        steps[3]()
    for copies in rest:
        for name in ("own", "relay_x", "relay_y", "relay_upper", "relay_lower"):
            copies[name].wait_recv()
    for copies in [main] + rest:
        for copy in copies.values():
            copy.wait_send()
    for copy in kept:
        copy.wait()


def head(number, places, expression, embed, gathers):
    sections, count_dp = lax.axis_size("section"), lax.axis_size("dp")
    rows, genes = places.shape[0], expression.shape[1]
    width = embed.shape[1]
    total_parts = sections * count_dp
    features = total_parts * width
    quarter = features // 4
    frequency = jnp.exp(jnp.arange(quarter, dtype=F32) * (-math.log(10000.0) / quarter))[None, :]
    vmem, anywhere = pl.BlockSpec(memory_space=pltpu.VMEM), pl.BlockSpec(memory_space=pl.ANY)
    plan = tuple((axis, shard.shape[axis]) for shard, axis in gathers)
    shapes = [
        shard.shape[:axis] + (shard.shape[axis] * total_parts,) + shard.shape[axis + 1 :]
        for shard, axis in gathers
    ]
    pieces = features // 64
    buffer = pltpu.VMEM((pieces, 256, 128), BF16)
    copies = 11 * (1 + len(gathers))
    results = pl.pallas_call(
        functools.partial(head_kernel, plan),
        out_shape=[
            jax.ShapeDtypeStruct((rows, features), F32),
            jax.ShapeDtypeStruct((genes, features), BF16),
        ]
        + [jax.ShapeDtypeStruct(shape, shard.dtype) for shape, (shard, _) in zip(shapes, gathers)],
        in_specs=[vmem] * 2 + [anywhere] * (2 + len(gathers)),
        out_specs=[vmem] + [anywhere] * (1 + len(gathers)),
        scratch_shapes=[
            pltpu.VMEM((rows, features), F32),
            pltpu.VMEM((rows, features), F32),
            pltpu.VMEM((rows, genes), BF16),
            pltpu.VMEM((total_parts, genes, width), BF16),
            pltpu.SemaphoreType.DMA,
            pltpu.SemaphoreType.DMA((total_parts,)),
        ]
        + [pltpu.VMEM(shard.shape, shard.dtype) for shard, _ in gathers]
        + [buffer] * 4
        + [pltpu.SemaphoreType.DMA((pieces,))] * 4
        + [
            pltpu.SemaphoreType.DMA((copies,)),
            pltpu.SemaphoreType.DMA((copies,)),
            pltpu.SemaphoreType.DMA((1 + 2 * len(gathers),)),
        ],
        compiler_params=pltpu.CompilerParams(
            collective_id=number, has_side_effects=True, vmem_limit_bytes=48 * 2**20
        ),
        name="head",
    )(places, frequency, expression, embed, *[shard for shard, _ in gathers])
    return results[0], results[1], results[2:]


def trade(remote, mine, indices, from_x, from_y, inbound, to_x, to_y):
    rows = from_x.shape[0]
    cut = halfway(rows)
    top, bottom = pl.ds(0, cut), pl.ds(cut, rows - cut)
    d, x, y, own = indices
    d_upper = remote(mine.at[d, top, :], inbound.at[top, :], to_x)
    d_lower = remote(mine.at[d, bottom, :], inbound.at[bottom, :], to_y)
    x_upper = remote(mine.at[x, top, :], from_x.at[top, :], to_x)
    y_lower = remote(mine.at[y, bottom, :], from_y.at[bottom, :], to_y)
    y_upper = remote(mine.at[y, top, :], from_y.at[top, :], to_y)
    x_lower = remote(mine.at[x, bottom, :], from_x.at[bottom, :], to_x)

    def pass_on():
        for copy, index, span, onward in (
            (d_upper, y, top, y_upper),
            (d_lower, x, bottom, x_lower),
        ):
            copy.wait_recv()
            mine[index, span, :] = (
                mine[index, span, :].astype(F32) + inbound[span, :].astype(F32)
            ).astype(mine.dtype)
            onward.start()

    def conclude():
        for copy in (x_upper, y_lower, y_upper, x_lower):
            copy.wait_recv()
        for copy in (d_upper, d_lower, x_upper, y_lower, y_upper, x_lower):
            copy.wait_send()
        return mine[own].astype(F32) + from_x[...].astype(F32) + from_y[...].astype(F32)

    return (d_upper, d_lower), (x_upper, y_lower), pass_on, conclude


def tail_kernel(
    start, expression, embed, grad_rebuilt, qkv, out, small, qkv_other, out_other,
    embed_sum, qkv_sum, out_sum, small_sum, cells_own, cells_other,
    start_other, start_turned, x_own, x_other, embed_in, cells, embed_parts, embed_x, embed_y, embed_in_d,
    qkv_parts, qkv_x, qkv_y, qkv_in_d, qkv_partner, out_parts, out_x, out_y, out_in_d, out_partner,
    small_parts, small_x, small_y, small_in_d, small_partner, sent, got, local_sem,
):
    section, dp = lax.axis_index("section"), lax.axis_index("dp")
    count_dp = lax.axis_size("dp")
    row, col = dp // 2, dp % 2
    peer_x, peer_y = row * 2 + (1 - col), (1 - row) * 2 + col
    peer_d = (1 - row) * 2 + (1 - col)
    partner, to_x, to_y = {"section": 1 - section}, {"dp": peer_x}, {"dp": peer_y}
    rows, genes = cells.shape
    half = start_other.shape[1]
    width = half // count_dp

    barrier = pltpu.get_barrier_semaphore()
    for device in (partner, to_x, to_y):
        pl.semaphore_signal(barrier, inc=1, device_id=device)
    pl.semaphore_wait(barrier, 3)

    used = [0, 0]

    def remote(src, dst, device):
        index = used[0]
        used[0] += 1
        return pltpu.make_async_remote_copy(
            src_ref=src, dst_ref=dst, send_sem=sent.at[index], recv_sem=got.at[index], device_id=device
        )

    def within(src, dst):
        index = used[1]
        used[1] += 1
        return pltpu.make_async_copy(src, dst, local_sem.at[index])

    def half_of(index):
        return pl.ds(pl.multiple_of(index * half, 128), half)

    def rows_of(index):
        return pl.ds(pl.multiple_of(index * rows, 16), rows)

    swaps = [
        remote(start.at[:, half_of(1 - section)], start_other, partner),
        remote(small.at[1 - section], small_partner, partner),
    ]
    for copy in swaps:
        copy.start()
    roles = (peer_d, peer_x, peer_y, dp)
    fetches = []
    for src, other, axis, parts, parts_other in (
        (qkv, qkv_other, 0, qkv_parts, qkv_partner),
        (out, out_other, 1, out_parts, out_partner),
    ):
        size = src.shape[axis] // (2 * count_dp)
        for role, index in enumerate(roles):
            fetches.append(
                within(block_of(src, axis, section * count_dp + index, size), parts.at[role])
            )
            fetches.append(within(block_of(other, axis, index, size), parts_other.at[role]))
    fetches.append(within(small.at[section], small_parts))
    load_own = within(expression.at[rows_of(section), :], x_own)
    load_other = within(expression.at[rows_of(1 - section), :], x_other)
    load_embed = within(embed, embed_in)
    load_cells = within(grad_rebuilt, cells)
    for copy in fetches + [load_own, load_other, load_embed, load_cells]:
        copy.start()

    trades = [
        trade(remote, parts, indices, *buffers, to_x, to_y)
        for parts, indices, buffers in (
            (qkv_parts, (0, 1, 2, 3), (qkv_x, qkv_y, qkv_in_d)),
            (out_parts, (0, 1, 2, 3), (out_x, out_y, out_in_d)),
            (small_parts, roles, (small_x, small_y, small_in_d)),
            (embed_parts, roles, (embed_x, embed_y, embed_in_d)),
        )
    ]

    for copy in fetches:
        copy.wait()
    swaps[1].wait_recv()
    for parts, other in (
        (qkv_parts, qkv_partner),
        (out_parts, out_partner),
        (small_parts, small_partner),
    ):
        parts[...] = (parts[...].astype(F32) + other[...].astype(F32)).astype(parts.dtype)
    for first, second, _, _ in trades[:3]:
        for copy in first + second:
            copy.start()

    load_own.wait()
    load_other.wait()
    swaps[0].wait_recv()
    start_turned[0] = start[:, half_of(section)].T
    start_turned[1] = start_other[...].T

    def embed_tile(span, size):
        tile = mat_nn(start_turned[0], x_own[:, span]) + mat_nn(start_turned[1], x_other[:, span])
        embed_parts[:, :, span] = tile.reshape(count_dp, width, size).astype(BF16)

    whole = genes // TILE

    def embed_step(index, carry):
        embed_tile(pl.ds(pl.multiple_of(index * TILE, TILE), TILE), TILE)
        return carry

    lax.fori_loop(0, whole, embed_step, 0)
    if genes % TILE:
        embed_tile(pl.ds(whole * TILE, genes % TILE), genes % TILE)
    for copy in trades[3][0] + trades[3][1]:
        copy.start()

    load_embed.wait()
    load_cells.wait()

    def cells_tile(span):
        tile = mat_nt(start[...], embed_in[span, :]).astype(BF16)
        cells[:, span] = (tile.astype(F32) - cells[:, span].astype(F32)).astype(BF16)

    def cells_step(index, carry):
        cells_tile(pl.ds(pl.multiple_of(index * TILE, TILE), TILE))
        return carry

    lax.fori_loop(0, whole, cells_step, 0)
    if genes % TILE:
        cells_tile(pl.ds(whole * TILE, genes % TILE))
    give = remote(cells, cells_other, partner)
    give.start()
    keep = within(cells, cells_own)
    keep.start()

    for _, _, pass_on, _ in trades:
        pass_on()
    qkv_sum[...] = trades[0][3]()
    out_sum[...] = trades[1][3]()
    small_sum[...] = trades[2][3]()
    embed_sum[...] = trades[3][3]().T
    for copy in swaps:
        copy.wait_send()
    give.wait()
    keep.wait()


def assemble_kernel(own, other, whole, held, arrived, left):
    section = lax.axis_index("section")
    rows = own.shape[0]
    spans = [(start, min(128, rows - start)) for start in range(0, rows, 128)]
    loads, stores = [], []
    for place, (src, index) in enumerate(((own, section), (other, 1 - section))):
        for part, (start, size) in enumerate(spans):
            span = pl.ds(start, size)
            target = pl.ds(pl.multiple_of(index * rows + start, 16), size)
            number = place * len(spans) + part
            loads.append(
                pltpu.make_async_copy(src.at[span, :], held.at[place, span, :], arrived.at[number])
            )
            stores.append(
                pltpu.make_async_copy(held.at[place, span, :], whole.at[target, :], left.at[number])
            )
    for load in loads:
        load.start()
    for load, store in zip(loads, stores):
        load.wait()
        store.start()
    for store in stores:
        store.wait()


def tail(number, start, expression, embed, grad_rebuilt, qkv, qkv_other, out, out_other, small):
    rows, features = start.shape
    genes, count_dp = embed.shape[0], lax.axis_size("dp")
    half = features // 2
    width = half // count_dp
    vmem, anywhere = pl.BlockSpec(memory_space=pltpu.VMEM), pl.BlockSpec(memory_space=pl.ANY)

    def buffers(shape, dtype, paired):
        parts, one = pltpu.VMEM((count_dp,) + shape, dtype), pltpu.VMEM(shape, dtype)
        return [parts, one, one, one] + ([parts] if paired else [])

    qkv_piece = (qkv.shape[0] // (2 * count_dp), qkv.shape[1])
    out_piece = (out.shape[0], out.shape[1] // (2 * count_dp))
    small_piece = small.shape[2:]
    cells = jax.ShapeDtypeStruct((rows, genes), BF16)
    results = pl.pallas_call(
        tail_kernel,
        out_shape=[
            jax.ShapeDtypeStruct((genes, width), F32),
            jax.ShapeDtypeStruct(qkv_piece, F32),
            jax.ShapeDtypeStruct(out_piece, F32),
            jax.ShapeDtypeStruct(small_piece, F32),
            cells,
            cells,
        ],
        in_specs=[vmem] + [anywhere] * 8,
        out_specs=[vmem] * 4 + [anywhere] * 2,
        scratch_shapes=[
            pltpu.VMEM((rows, half), BF16),
            pltpu.VMEM((2, half, rows), BF16),
            pltpu.VMEM((rows, genes), BF16),
            pltpu.VMEM((rows, genes), BF16),
            pltpu.VMEM((genes, features), BF16),
            pltpu.VMEM((rows, genes), BF16),
        ]
        + buffers((width, genes), BF16, False)
        + buffers(qkv_piece, BF16, True)
        + buffers(out_piece, BF16, True)
        + buffers(small_piece, F32, True)
        + [
            pltpu.SemaphoreType.DMA((27,)),
            pltpu.SemaphoreType.DMA((27,)),
            pltpu.SemaphoreType.DMA((22,)),
        ],
        compiler_params=pltpu.CompilerParams(
            collective_id=number, has_side_effects=True, vmem_limit_bytes=56 * 2**20
        ),
        name="tail",
    )(start, expression, embed, grad_rebuilt, qkv, out, small, qkv_other, out_other)
    whole = pl.pallas_call(
        assemble_kernel,
        out_shape=jax.ShapeDtypeStruct((2 * rows, genes), BF16),
        in_specs=[anywhere] * 2,
        out_specs=anywhere,
        scratch_shapes=[pltpu.VMEM((2, rows, genes), BF16)]
        + [pltpu.SemaphoreType.DMA((2 * (-(-rows // 128)),))] * 2,
        compiler_params=pltpu.CompilerParams(vmem_limit_bytes=56 * 2**20),
        name="assemble",
    )(results[4], results[5])
    return list(results[:4]) + [whole]


def line_pipe(produce, hooks, items, spacing, part, total, from_left, from_right, to_right, to_left, got_left, got_right, sent_right, sent_left):
    me, count = lax.axis_index("mp"), lax.axis_size("mp")
    pieces = part.shape[2] // 128
    has_right, has_left = me < count - 1, me > 0

    def place(slot):
        column = lax.rem(slot, spacing) * 128
        return (lax.rem(lax.div(slot, spacing), 2), slice(None), pl.ds(pl.multiple_of(column, 128), 128))

    def rightward(slot):
        return pltpu.make_async_remote_copy(
            src_ref=to_right.at[slot],
            dst_ref=from_left.at[slot],
            send_sem=sent_right.at[slot],
            recv_sem=got_left.at[slot],
            device_id={"mp": me + 1},
        )

    def leftward(slot):
        return pltpu.make_async_remote_copy(
            src_ref=to_left.at[slot],
            dst_ref=from_right.at[slot],
            send_sem=sent_left.at[slot],
            recv_sem=got_right.at[slot],
            device_id={"mp": me - 1},
        )

    def used(slot):
        return (slot >= 0) & (slot < items * spacing) & (lax.rem(slot, spacing) < pieces)

    def flow(slot, copy, has_source, has_target, source, target):
        @pl.when(used(slot))
        def _():
            @pl.when(has_source)
            def _():
                copy(slot).wait_recv()

            @pl.when(has_target & has_source)
            def _():
                target[slot] = (part[place(slot)] + source[slot].astype(F32)).astype(BF16)

            @pl.when(has_target & jnp.logical_not(has_source))
            def _():
                target[slot] = part[place(slot)].astype(BF16)

            @pl.when(has_target)
            def _():
                copy(slot).start()

    right_half = lax.div(2 * me + 1, count)
    trail = HOP_LAG * (right_half * me + (1 - right_half) * (count - 1 - me))

    def step(moment, carry):
        for when, hook in hooks:
            pl.when(moment == when)(hook)
        produce(moment)
        flow(moment - HOP_LAG * me, rightward, has_left, has_right, from_left, to_right)
        flow(
            moment - HOP_LAG * (count - 1 - me), leftward, has_right, has_left, from_right, to_left
        )
        done = moment - trail

        @pl.when(used(done) & has_left & has_right)
        def _():
            total[place(done)] = (
                part[place(done)] + from_left[done].astype(F32) + from_right[done].astype(F32)
            )

        @pl.when(used(done) & jnp.logical_not(has_left))
        def _():
            total[place(done)] = part[place(done)] + from_right[done].astype(F32)

        @pl.when(used(done) & jnp.logical_not(has_right))
        def _():
            total[place(done)] = part[place(done)] + from_left[done].astype(F32)

        return carry

    lax.fori_loop(0, (items + 1) * spacing, step, 0)

    def finish(slot, carry):
        @pl.when(used(slot) & has_right)
        def _():
            rightward(slot).wait_send()

        @pl.when(used(slot) & has_left)
        def _():
            leftward(slot).wait_send()

        return carry

    lax.fori_loop(0, items * spacing, finish, 0)


def pipe_spacing(pieces, count):
    return max(pieces + 1, (pieces - 1 + HOP_LAG * (count - 1)) // 2 + 1)


def middle_kernel(
    plan, spacing, attended, start, gain, bias, out_w, noise, centers, spreads, *refs
):
    refs = list(refs)

    def take(number):
        taken = refs[:number]
        del refs[:number]
        return taken

    count = len(plan)
    shards = take(count)
    (normed_out, scale_out, second_out, upper_out, active_out, hidden_out, log_vars_out,
     latent_out, spread_out, latent_low_out, decoder_out, density_all) = take(12)
    gathered = take(count)
    part, total, kept_rows, density = take(4)
    up_in, down_in, latent_in, dec_in = take(4)
    held = take(count)
    line = take(8)
    sent, got, local_sem = refs

    section, z, dp = (lax.axis_index(name) for name in ("section", "mp", "dp"))
    count_z, count_dp = lax.axis_size("mp"), lax.axis_size("dp")
    row, col = dp // 2, dp % 2
    peer_x, peer_y = row * 2 + (1 - col), (1 - row) * 2 + col
    peers = (peer_x, peer_y, (1 - row) * 2 + (1 - col))
    partner, to_x, to_y = {"section": 1 - section}, {"dp": peer_x}, {"dp": peer_y}
    cells, latents = noise.shape
    half_rows = part.shape[1]
    comp_count = centers.shape[0]

    barrier = pltpu.get_barrier_semaphore()
    for device in (partner, to_x, to_y):
        pl.semaphore_signal(barrier, inc=1, device_id=device)
    for step in range(1, count_z):
        pl.semaphore_signal(barrier, inc=1, device_id={"mp": (z + step) % count_z})
    pl.semaphore_wait(barrier, 3 + count_z - 1)

    used = [0, 0]

    def remote(src, dst, device):
        index = used[0]
        used[0] += 1
        return pltpu.make_async_remote_copy(
            src_ref=src, dst_ref=dst, send_sem=sent.at[index], recv_sem=got.at[index], device_id=device
        )

    def within(src, dst):
        index = used[1]
        used[1] += 1
        return pltpu.make_async_copy(src, dst, local_sem.at[index])

    around = (section, dp, peers, partner, to_x, to_y)
    spreads_of = [
        spread(remote, src, dst, axis, size, *around)
        for src, dst, (axis, size) in zip(shards, gathered, plan)
    ]
    steps_of = [spread_steps(copies) for copies in spreads_of]
    loads = [within(src, room) for src, room in zip(shards, held)]
    keeps = [
        within(room, block_of(dst, axis, section * count_dp + dp, size))
        for room, dst, (axis, size) in zip(held, gathered, plan)
    ]
    fetches = [
        within(src, dst) for src, dst in zip(gathered, (up_in, down_in, latent_in, dec_in))
    ]
    density_sends = [
        remote(density, density_all.at[z], {"mp": (z + step) % count_z})
        for step in range(1, count_z)
    ]
    density_keep = within(density, density_all.at[z])

    def run_steps(items, number):
        def run():
            for item in items:
                steps_of[item][number]()

        return run

    def keep():
        for load in loads:
            load.wait()
        for copy in keeps:
            copy.start()

    near, far = list(range(count - 1)), [count - 1]

    def fetch():
        for item in near:
            for name in ("own", "relay_x", "relay_y", "relay_upper", "relay_lower"):
                spreads_of[item][name].wait_recv()
            keeps[item].wait()
        for copy in fetches:
            copy.start()
        for copy in fetches:
            copy.wait()

    def share():
        for copy in density_sends + [density_keep]:
            copy.start()

    for load in loads:
        load.start()

    def rows_of(half):
        return pl.ds(pl.multiple_of(half * (cells - half_rows), 16), half_rows)

    def out_product(half):
        part[half] = mat_nn(attended[rows_of(half), :], out_w[...])

    def feed_forward(half):
        rows = rows_of(half)
        values = start[rows, :] + total[half]
        kept_rows[half] = values
        normed, scale = normalize(values)
        second = (normed * gain[...] + bias[...]).astype(BF16)
        upper = mat_nn(second, up_in[...])
        active = gelu(upper).astype(BF16)
        part[half] = mat_nn(active, down_in[...])
        normed_out[rows, :] = normed
        scale_out[rows, :] = scale
        second_out[rows, :] = second
        upper_out[rows, :] = upper
        active_out[rows, :] = active

    def latents_of(half):
        rows = rows_of(half)
        hidden = (kept_rows[half] + total[half]).astype(BF16)
        hidden_out[rows, :] = hidden
        stats = mat_nn(hidden, latent_in[...])
        means, log_vars = stats[:, :latents], stats[:, latents:]
        own_noise = noise[rows, :]
        scaled = jnp.exp(0.5 * log_vars) * own_noise
        latent = means + scaled
        low = latent.astype(BF16)
        part[half] = mat_nn(low, dec_in[...])
        log_vars_out[rows, :] = log_vars
        spread_out[rows, :] = scaled
        latent_out[rows, :] = latent
        latent_low_out[rows, :] = low
        lane = lax.broadcasted_iota(jnp.int32, (half_rows, 128), 1)
        columns = jnp.sum(
            -0.5 * LOG_TWO_PI - 0.5 * log_vars - 0.5 * own_noise * own_noise, axis=1, keepdims=True
        )
        table = jnp.where(lane == comp_count, columns, 0.0)
        for index in range(comp_count):
            log_spread = spreads[index : index + 1, :]
            offset = latent - centers[index : index + 1, :]
            columns = jnp.sum(
                -0.5 * LOG_TWO_PI - 0.5 * log_spread - 0.5 * offset * offset * jnp.exp(-log_spread),
                axis=1,
                keepdims=True,
            )
            table = jnp.where(lane == index, columns, table)
        density[:, pl.ds(pl.multiple_of(half * half_rows, 128), half_rows)] = table.T[
            : density.shape[0], :
        ]

    def conclude(half):
        decoder_out[rows_of(half), :] = total[half]

    def produce(moment):
        item = lax.div(moment, spacing)
        half, stage = lax.rem(item, 2), lax.div(item, 2)
        begins = lax.rem(moment, spacing) == 0
        for number, work in enumerate((out_product, feed_forward, latents_of, conclude)):
            pl.when(begins & (stage == number))(functools.partial(work, half))

    hooks = [
        (0, run_steps(near, 0)),
        (1, keep),
        (7, run_steps(near, 1)),
        (13, run_steps(near, 2)),
        (16, run_steps(near, 3)),
        (2 * spacing, fetch),
        (2 * spacing + 1, run_steps(far, 0)),
        (2 * spacing + 10, run_steps(far, 1)),
        (2 * spacing + 18, run_steps(far, 2)),
        (2 * spacing + 26, run_steps(far, 3)),
        (5 * spacing + 1, share),
    ]
    line_pipe(produce, hooks, 6, spacing, part, total, *line)
    conclude(1)
    for item in far:
        for name in ("own", "relay_x", "relay_y", "relay_upper", "relay_lower"):
            spreads_of[item][name].wait_recv()
        keeps[item].wait()
    for copies in spreads_of:
        for copy in copies.values():
            copy.wait_send()
    for copy in density_sends:
        copy.wait()
    density_keep.wait()


def middle(number, attended, start, gain, bias, out_w, noise, centers, spreads, gathers):
    sections, count_dp, count_z = (lax.axis_size(name) for name in ("section", "dp", "mp"))
    cells, features = start.shape
    latents = noise.shape[1]
    total_parts = sections * count_dp
    pieces = features // 128
    spacing = pipe_spacing(pieces, count_z)
    slots = 6 * spacing
    half_rows = 256
    plan = tuple((axis, shard.shape[axis]) for shard, axis in gathers)
    shapes = [
        shard.shape[:axis] + (shard.shape[axis] * total_parts,) + shard.shape[axis + 1 :]
        for shard, axis in gathers
    ]
    units = shapes[0][1]
    vmem, anywhere = pl.BlockSpec(memory_space=pltpu.VMEM), pl.BlockSpec(memory_space=pl.ANY)
    outputs = [
        ((cells, features), F32),
        ((cells, 1), F32),
        ((cells, features), BF16),
        ((cells, units), F32),
        ((cells, units), BF16),
        ((cells, features), BF16),
        ((cells, latents), F32),
        ((cells, latents), F32),
        ((cells, latents), F32),
        ((cells, latents), BF16),
        ((cells, features), F32),
        ((count_z, 24, 2 * half_rows), F32),
    ] + [(shape, BF16) for shape in shapes]
    buffer = pltpu.VMEM((slots, half_rows, 128), BF16)
    copies = 11 * len(gathers) + count_z - 1
    halves = pltpu.VMEM((2, half_rows, features), F32)
    results = pl.pallas_call(
        functools.partial(middle_kernel, plan, spacing),
        out_shape=[jax.ShapeDtypeStruct(*item) for item in outputs],
        in_specs=[vmem] * 8 + [anywhere] * len(gathers),
        out_specs=[vmem] * 11 + [anywhere] * (1 + len(gathers)),
        scratch_shapes=[halves, halves, halves, pltpu.VMEM((24, 2 * half_rows), F32)]
        + [pltpu.VMEM(shape, BF16) for shape in shapes[:-1]]
        + [pltpu.VMEM(shard.shape, BF16) for shard, _ in gathers]
        + [buffer] * 4
        + [pltpu.SemaphoreType.DMA((slots,))] * 4
        + [
            pltpu.SemaphoreType.DMA((copies,)),
            pltpu.SemaphoreType.DMA((copies,)),
            pltpu.SemaphoreType.DMA((3 * len(gathers),)),
        ],
        compiler_params=pltpu.CompilerParams(
            collective_id=number, has_side_effects=True, vmem_limit_bytes=60 * 2**20
        ),
        name="middle",
    )(attended, start, gain, bias, out_w, noise, centers, spreads, *[shard for shard, _ in gathers])
    return results[:12], results[12:]


def meet(tiled, number, reduce=None, gathers=(), swaps=(), exchanges=(), shares=(), pairs=()):
    if tiled:
        return comm(number, reduce, gathers, swaps, exchanges, shares, pairs)
    partner = [(i, 1 - i) for i in range(2)]
    section, count_dp = lax.axis_index("section"), lax.axis_size("dp")
    swapped = []
    for array, axis in swaps:
        size = array.shape[axis] // 2
        half = lax.dynamic_slice_in_dim(array, (1 - section) * size, size, axis)
        swapped.append(lax.ppermute(half, "section", partner))
    exchanged = []
    for array, other, axis in exchanges:
        if other is not None:
            array = half_sum(array, other, axis)
        parts = lax.all_to_all(jnp.stack(jnp.split(array, count_dp, axis)), "dp", 0, 0)
        exchanged.append(total(parts))
    return [
        [] if reduce is None else comm(number, reduce)[0][0:1],
        [lax.all_gather(shard, ("section", "dp"), axis=axis, tiled=True) for shard, axis in gathers],
        swapped,
        exchanged,
        [lax.all_gather(array, "mp") for array in shares],
        [lax.ppermute(array, "section", partner) for array in pairs],
    ]


def half_sum(array, received, axis):
    size = received.shape[axis]
    own = lax.dynamic_slice_in_dim(array, lax.axis_index("section") * size, size, axis)
    return (own.astype(F32) + received.astype(F32)).astype(array.dtype)


def total(parts):
    return jnp.sum(parts.astype(F32), axis=0)


def local(
    expression,
    cell_xy,
    live_mask,
    lengths,
    ramp_step,
    latent_noise,
    gene_embed,
    ln1_gain,
    ln1_bias,
    w_query,
    w_key,
    w_value,
    w_out,
    ln2_gain,
    ln2_bias,
    w_up,
    w_down,
    w_mean,
    w_logvar,
    comp_mean,
    comp_logvar,
    w_dec,
    w_genes,
):
    micro_count = lengths.shape[0]
    cells = expression.shape[0] // micro_count
    micro = lax.axis_index("section")
    latent_cols = w_mean.shape[1]
    comp_count, comp_width = comp_mean.shape
    width = ln1_gain.shape[0]
    shards = 2 * lax.axis_size("dp")
    features = shards * width
    tiled = width % 128 == 0 and lax.axis_size("dp") == 4
    meeting = functools.partial(meet, tiled)

    def own(array, axis=0):
        return lax.dynamic_slice_in_dim(array, micro * cells, cells, axis)

    genes_in = own(expression)
    alive = own(live_mask)
    alive_float = alive.astype(F32)
    noise = own(latent_noise)
    slide = slide_ids(lax.dynamic_index_in_dim(lengths, micro, 0, False), cells)
    allowed = allowed_pairs(slide, alive)

    norm_block = jnp.pad(jnp.stack([ln1_gain, ln1_bias, ln2_gain, ln2_bias]), ((0, 12), (0, 0)))
    comp_block = jnp.pad(
        jnp.concatenate([comp_mean, comp_logvar], axis=0), ((0, 0), (0, width - comp_width))
    )
    small = jnp.concatenate([norm_block, comp_block], axis=0)
    small_rows = small.shape[0]
    qkv_shard = jnp.concatenate([w_query, w_key, w_value], axis=1)
    places = own(cell_xy, 1)
    weights = ((small, 0), (qkv_shard, 0), (w_out, 1))
    if tiled:
        start, embed, (small_all, qkv, out_w) = head(
            0, places.T, expression, gene_embed, weights
        )
    else:
        _, (embed, small_all, qkv, out_w), _, _, _, _ = meeting(
            0, gathers=((gene_embed, 1),) + weights
        )
        (summed,), _, _, _, _, _ = meeting(1, (expression, embed, False, True))
        start = summed + position_code(places, features)
    small_all = small_all.reshape(shards, small_rows, width).astype(F32)
    norm_params = small_all[:, :4].transpose(1, 0, 2).reshape(4, features)
    gain_one, bias_one, gain_two, bias_two = (norm_params[i : i + 1] for i in range(4))
    comps = small_all[:, 16:, :comp_width].transpose(1, 0, 2).reshape(2 * comp_count, -1)
    centers, spreads = comps[:comp_count], comps[comp_count:]

    normed_one, scale_one = normalize(start)
    first_low = (normed_one * gain_one + bias_one).astype(BF16)
    projected = mat_nn(first_low, qkv).astype(BF16)
    queries, keys, values = jnp.split(projected, 3, axis=1)
    attended, log_totals = attend(queries, keys, values, allowed)
    latent_shard = jnp.concatenate([w_mean, w_logvar], axis=1)
    precision = jnp.exp(-spreads)
    if tiled:
        states, (up_w, down_w, latent_w, dec_w, genes_w) = middle(
            1,
            attended,
            start,
            gain_two,
            bias_two,
            out_w,
            noise,
            centers,
            spreads,
            ((w_up, 0), (w_down, 1), (latent_shard, 0), (w_dec, 1), (w_genes, 0)),
        )
        (normed_two, scale_two, second_low, upper, activated, hidden, log_vars, latent, spread_latent,
         latent_low, decoder_pre, density_parts) = states
        density = jnp.sum(density_parts, axis=0)
        rows = density.shape[1] // 2
        densities = jnp.concatenate([density[:, :rows], density[:, 3 * rows - cells :]], axis=1)
    else:
        (summed,), (up_w, down_w, latent_w, dec_w), _, _, _, _ = meeting(
            2, (attended, out_w, False, False), gathers=((w_up, 0), (w_down, 1), (latent_shard, 0), (w_dec, 1))
        )
        after_attn = start + summed
        normed_two, scale_two = normalize(after_attn)
        second_low = (normed_two * gain_two + bias_two).astype(BF16)
        upper = mat_nn(second_low, up_w)
        activated = gelu(upper).astype(BF16)
        (summed,), (genes_w,), _, _, _, _ = meeting(
            3, (activated, down_w, False, False), gathers=((w_genes, 0),)
        )
        hidden = (after_attn + summed).astype(BF16)

        stats = mat_nn(hidden, latent_w)
        means, log_vars = stats[:, :latent_cols], stats[:, latent_cols:]
        spread_latent = jnp.exp(0.5 * log_vars) * noise
        latent = means + spread_latent
        latent_low = latent.astype(BF16)
        post_part = jnp.sum(-0.5 * LOG_TWO_PI - 0.5 * log_vars - 0.5 * noise * noise, axis=1)
        offsets = latent[None] - centers[:, None, :]
        pulled = offsets * precision[:, None, :]
        comp_part = jnp.sum(
            -0.5 * LOG_TWO_PI - 0.5 * spreads[:, None, :] - 0.5 * offsets * pulled, axis=2
        )
        density_part = jnp.pad(
            jnp.concatenate([comp_part, post_part[None]], axis=0), ((0, 7), (0, -cells % 128))
        )
        (decoder_pre,), _, _, _, (density_parts,), _ = meeting(
            4, (latent_low, dec_w, False, False), shares=(density_part,)
        )
        densities = jnp.sum(density_parts, axis=0)[:, :cells]
    logits = densities[:comp_count] - math.log(comp_count)
    log_post = densities[comp_count]
    largest = jnp.max(logits, axis=0, keepdims=True)
    log_prior = largest[0] + jnp.log(jnp.sum(jnp.exp(logits - largest), axis=0))
    respons = jnp.exp(logits - log_prior[None, :])
    divergence = jnp.sum((log_post - log_prior) * alive_float)
    decoder_act = lax.optimization_barrier(gelu(decoder_pre).astype(BF16))
    residual = (mat_nn(decoder_act, genes_w) - genes_in.astype(F32)) * alive_float[:, None]
    grad_rebuilt = residual.astype(BF16)

    grad_genes = mat_tn(decoder_act, grad_rebuilt).astype(BF16)
    counts = jnp.concatenate(
        [jnp.full((1, 128), divergence), jnp.full((31, 128), jnp.sum(alive_float))], axis=0
    )
    (grad_act,), (count_parts,), (genes_other,), _, _, _ = meeting(
        5, (grad_rebuilt, genes_w, True, False), gathers=((counts, 0),), swaps=((grad_genes, 0),)
    )
    count_parts = jnp.sum(count_parts.reshape(shards, 32, 128)[:, :, 0], axis=0)
    mean_kl = count_parts[0] / (LATENT * count_parts[1])
    ramp_weight = jnp.minimum(1.0, (ramp_step[0] + 1).astype(F32) / RAMP)
    kl_scale = (
        ramp_weight * jax.nn.softplus(mean_kl - FREE_BITS) * jax.nn.sigmoid(mean_kl - FREE_BITS)
    )
    grad_pre = (grad_act * gelu_slope(decoder_pre)).astype(BF16)
    grad_dec = mat_tn(latent_low, grad_pre).astype(BF16)
    cell_weight = kl_scale * alive_float
    offsets = latent[None] - centers[:, None, :]
    pulled = offsets * precision[:, None, :]
    weighted = (respons * cell_weight[None, :])[:, :, None]
    grad_latent = mat_nt(grad_pre, dec_w) + jnp.sum(weighted * pulled, axis=0)
    grad_comps = jnp.concatenate(
        [
            -jnp.sum(weighted * pulled, axis=1),
            -jnp.sum(weighted * (0.5 * offsets * pulled - 0.5), axis=1),
        ],
        axis=0,
    )
    grad_means = grad_latent.astype(BF16)
    grad_logs = (grad_latent * (0.5 * spread_latent) - 0.5 * cell_weight[:, None]).astype(BF16)
    grad_stats = jnp.concatenate([grad_means, grad_logs], axis=1)
    grad_latent_w = mat_tn(hidden, grad_stats).astype(BF16)
    (summed,), _, (latent_other, dec_other), (genes_parts,), _, _ = meeting(
        6,
        (grad_stats, latent_w, True, False),
        swaps=((grad_latent_w, 0), (grad_dec, 1)),
        exchanges=((grad_genes, genes_other, 0),),
    )
    grad_hidden = summed.astype(BF16)

    grad_down = mat_tn(activated, grad_hidden).astype(BF16)
    grad_upper = (mat_nt(grad_hidden, down_w) * gelu_slope(upper)).astype(BF16)
    grad_up = mat_tn(second_low, grad_upper).astype(BF16)
    (grad_norm_two,), _, (down_other, up_other), (latent_parts, dec_parts), _, _ = (
        meeting(
            7,
            (grad_upper, up_w, True, False),
            swaps=((grad_down, 1), (grad_up, 0)),
            exchanges=(
                (grad_latent_w, latent_other, 0),
                (grad_dec, dec_other, 1),
            ),
        )
    )
    grad_middle = grad_hidden.astype(F32) + norm_back(
        grad_norm_two, normed_two, scale_two, gain_two
    )
    middle_low = grad_middle.astype(BF16)
    grad_out = mat_tn(attended, middle_low).astype(BF16)
    grad_qkv_act = attend_back(middle_low, out_w, projected, log_totals, slide, alive)
    grad_qkv = mat_tn(first_low, grad_qkv_act).astype(BF16)
    (grad_norm_one,), _, (qkv_other, out_other), (down_parts, up_parts), _, _ = meeting(
        8,
        (grad_qkv_act, qkv, True, False),
        swaps=((grad_qkv, 0), (grad_out, 1)),
        exchanges=((grad_down, down_other, 1), (grad_up, up_other, 0)),
    )
    grad_start = grad_middle + norm_back(grad_norm_one, normed_one, scale_one, gain_one)
    start_low = grad_start.astype(BF16)

    norm_grads = jnp.stack(
        [
            jnp.sum(grad_norm_one * normed_one, axis=0),
            jnp.sum(grad_norm_one, axis=0),
            jnp.sum(grad_norm_two * normed_two, axis=0),
            jnp.sum(grad_norm_two, axis=0),
        ]
    )
    norm_grads = norm_grads.reshape(4, shards, width).transpose(1, 0, 2)
    comp_grads = grad_comps.reshape(2 * comp_count, shards, comp_width).transpose(1, 0, 2)
    small_grads = jnp.concatenate(
        [
            jnp.pad(norm_grads, ((0, 0), (0, 12), (0, 0))),
            jnp.pad(comp_grads, ((0, 0), (0, 0), (0, width - comp_width))),
        ],
        axis=1,
    ).reshape(shards * small_rows, width)
    if tiled:
        embed_parts, qkv_parts, out_parts, small_sum, grad_expression = tail(
            9,
            start_low,
            expression,
            embed,
            grad_rebuilt,
            grad_qkv,
            qkv_other,
            grad_out,
            out_other,
            small_grads.reshape(2, shards // 2, small_rows, width),
        )
    else:
        start_all = lax.all_gather(start_low, "section", axis=0, tiled=True)
        start_half = lax.dynamic_slice_in_dim(start_all, micro * (features // 2), features // 2, 1)
        grad_embed = mat_tn(expression, start_half).astype(BF16)
        grad_cells = (
            mat_nt(start_low, embed).astype(BF16).astype(F32) - grad_rebuilt.astype(F32)
        ).astype(BF16)
        grad_expression = lax.all_gather(grad_cells, "section", axis=0, tiled=True)
        small_other = lax.ppermute(
            lax.dynamic_slice_in_dim(
                small_grads, (1 - micro) * (shards // 2 * small_rows), shards // 2 * small_rows, 0
            ),
            "section",
            [(0, 1), (1, 0)],
        )
        _, _, _, (embed_parts, qkv_parts, out_parts, small_sum), _, _ = meeting(
            9,
            exchanges=(
                (grad_embed, None, 1),
                (grad_qkv, qkv_other, 0),
                (grad_out, out_other, 1),
                (small_grads, small_other, 0),
            ),
        )
    grad_query, grad_key, grad_value = jnp.split(qkv_parts, 3, axis=1)
    grad_mean, grad_logvar = jnp.split(latent_parts, 2, axis=1)
    return (
        embed_parts,
        small_sum[0],
        small_sum[1],
        grad_query,
        grad_key,
        grad_value,
        out_parts,
        small_sum[2],
        small_sum[3],
        up_parts,
        down_parts,
        grad_mean,
        grad_logvar,
        small_sum[16 : 16 + comp_count, :comp_width],
        small_sum[16 + comp_count :, :comp_width],
        dec_parts,
        genes_parts,
        grad_expression,
    )


def solution(mesh):
    weight_rows = P(("section", "dp"), "mp")
    weight_cols = P("mp", ("section", "dp"))
    vector = P(("section", "dp"))
    comps = P(None, ("mp", "section", "dp"))
    weights = (
        weight_cols, vector, vector, weight_rows, weight_rows, weight_rows, weight_cols,
        vector, vector, weight_rows, weight_cols, weight_rows, weight_rows, comps, comps,
        weight_cols, weight_rows,
    )
    return jax.shard_map(
        local,
        mesh=mesh,
        in_specs=(P("dp", "mp"), P(None, "dp"), P("dp"), P("dp", None), P(), P("dp", "mp"))
        + weights,
        out_specs=weights + (P("dp", "mp"),),
        check_vma=False,
    )
```

```python
import functools
import math

import jax
import jax.numpy as jnp
from jax import lax
from jax.experimental import pallas as pl
from jax.experimental.pallas import tpu as pltpu
from jax.sharding import PartitionSpec as P

HEAD = 64
LATENT = 512
RAMP = 1000
LOG_TWO_PI = 1.8378770664093453
NEG_LARGE = -1e30
FREE_BITS = 1.0
HOP_LAG = 3
WINDOW = 3
BLOCK_STEP = 4
TILE = 256
LINK_BYTES_PER_US = 92000.0
MOMENT_US = 1.3
SPREAD = 1
SPREAD_FROM = 0
SPREAD_STEP = 1
F32 = jnp.float32
BF16 = jnp.bfloat16


def mat_nn(left, right):
    return jnp.dot(left, right, preferred_element_type=F32)


def mat_tn(left, right):
    return lax.dot_general(left, right, (((0,), (0,)), ((), ())), preferred_element_type=F32)


def mat_nt(left, right):
    return lax.dot_general(left, right, (((1,), (1,)), ((), ())), preferred_element_type=F32)


def gelu(values):
    return 0.5 * values * (1.0 + lax.erf(values * 0.7071067811865476))


def gelu_slope(values):
    return (
        0.5 * (1.0 + lax.erf(values * 0.7071067811865476))
        + values * jnp.exp(-0.5 * values * values) * 0.3989422804014327
    )


def normalize(values):
    center = values - jnp.mean(values, axis=-1, keepdims=True)
    scale = lax.rsqrt(jnp.mean(center * center, axis=-1, keepdims=True) + 1e-05)
    return center * scale, scale


def norm_back(grad_in, normed, scale, gain):
    scaled = grad_in * gain
    return scale * (
        scaled
        - jnp.mean(scaled, axis=-1, keepdims=True)
        - normed * jnp.mean(scaled * normed, axis=-1, keepdims=True)
    )


def position_code(places, feature_count):
    quarter = feature_count // 4
    frequency = jnp.exp(jnp.arange(quarter, dtype=F32) * (-math.log(10000.0) / quarter))
    along_x = places[0][:, None] * frequency[None, :]
    along_y = places[1][:, None] * frequency[None, :]
    return jnp.concatenate(
        [jnp.sin(along_x), jnp.cos(along_x), jnp.sin(along_y), jnp.cos(along_y)], axis=1
    )


def slide_ids(length_row, cell_count):
    bounds = jnp.cumsum(length_row)[:-1]
    index = jnp.arange(cell_count, dtype=jnp.int32)
    return jnp.sum((index[:, None] >= bounds[None, :]).astype(jnp.int32), axis=1)


def attend_kernel(start, gain, bias, weights, slide_keys, slide_queries, alive_keys, *outs):
    normed_out, scale_out, low_out, projected_out, attended_out, totals_out = outs
    cells, width = attended_out.shape
    factor = HEAD ** (-0.5)
    normed, scale = normalize(start[...])
    normed_out[...] = normed
    scale_out[...] = scale
    low = (normed * gain[...] + bias[...]).astype(BF16)
    low_out[...] = low
    projected = mat_nn(low, weights[...]).astype(BF16)
    projected_out[...] = projected
    shape = (cells, cells)
    own_key = lax.broadcasted_iota(jnp.int32, shape, 0) == lax.broadcasted_iota(jnp.int32, shape, 1)
    allowed = (slide_keys[...] == slide_queries[...]) & ((alive_keys[...] == 1) | own_key)
    for head_index in range(width // HEAD):
        first = head_index * HEAD
        q = projected[:, first : first + HEAD]
        k = projected[:, width + first : width + first + HEAD]
        v = projected[:, 2 * width + first : 2 * width + first + HEAD]
        scores = jnp.where(allowed, mat_nt(k, q) * factor, NEG_LARGE)
        largest = jnp.max(scores, axis=0, keepdims=True)
        exponents = jnp.exp(scores - largest)
        sums = jnp.sum(exponents, axis=0, keepdims=True)
        probs = (exponents / sums).astype(BF16)
        attended_out[:, first : first + HEAD] = mat_tn(probs, v).astype(BF16)
        totals_out[head_index : head_index + 1, :] = largest + jnp.log(sums)


def attend(start, gain, bias, weights, slide, alive):
    cells, features = start.shape
    width = weights.shape[1] // 3
    return pl.pallas_call(
        attend_kernel,
        out_shape=[
            jax.ShapeDtypeStruct((cells, features), F32),
            jax.ShapeDtypeStruct((cells, 1), F32),
            jax.ShapeDtypeStruct((cells, features), BF16),
            jax.ShapeDtypeStruct((cells, 3 * width), BF16),
            jax.ShapeDtypeStruct((cells, width), BF16),
            jax.ShapeDtypeStruct((width // HEAD, cells), F32),
        ],
        compiler_params=pltpu.CompilerParams(vmem_limit_bytes=48 * 2**20),
        name="attend",
    )(start, gain, bias, weights, slide[:, None], slide[None, :], alive[:, None])


def decode_kernel(section, pre, weights, cells, alive, residual, grad, act, act_turned):
    @pl.when(pl.program_id(0) == 0)
    def _():
        value = gelu(pre[...]).astype(BF16)
        act[...] = value
        act_turned[...] = value.T

    rebuilt = mat_nn(act[...], weights[...])
    difference = ((rebuilt - cells[...].astype(F32)) * alive[...]).astype(BF16)
    residual[...] = difference
    grad[...] = mat_nn(act_turned[...], difference).astype(BF16)


def decode(micro, pre, weights, expression, alive):
    rows, features = pre.shape
    genes = weights.shape[1]
    block = 512
    return pl.pallas_call(
        decode_kernel,
        grid_spec=pltpu.PrefetchScalarGridSpec(
            num_scalar_prefetch=1,
            grid=(pl.cdiv(genes, block),),
            in_specs=[
                pl.BlockSpec((rows, features), lambda step, section: (0, 0)),
                pl.BlockSpec((features, block), lambda step, section: (0, step)),
                pl.BlockSpec((rows, block), lambda step, section: (section[0], step)),
                pl.BlockSpec((rows, 1), lambda step, section: (0, 0)),
            ],
            out_specs=[
                pl.BlockSpec((rows, block), lambda step, section: (0, step)),
                pl.BlockSpec((features, block), lambda step, section: (0, step)),
            ],
            scratch_shapes=[pltpu.VMEM((rows, features), BF16), pltpu.VMEM((features, rows), BF16)],
        ),
        out_shape=[
            jax.ShapeDtypeStruct((rows, genes), BF16),
            jax.ShapeDtypeStruct((features, genes), BF16),
        ],
        compiler_params=pltpu.CompilerParams(vmem_limit_bytes=48 * 2**20),
        name="decode",
    )(micro.astype(jnp.int32).reshape(1), pre, weights, expression, alive[:, None])


def attend_back_kernel(plan, middle, out_w, projected, log_totals, slide_keys, slide_queries, alive_keys, *refs):
    swapped, out, received = refs[: len(plan)], refs[len(plan)], refs[len(plan) + 1 : 2 * len(plan) + 1]
    sent, got = refs[2 * len(plan) + 1 :]
    section = lax.axis_index("section")
    partner = {"section": 1 - section}
    barrier = pltpu.get_barrier_semaphore()
    pl.semaphore_signal(barrier, inc=1, device_id=partner)
    pl.semaphore_wait(barrier, 1)
    copies = [
        pltpu.make_async_remote_copy(
            src_ref=part_of(src, axis, 1 - section, size),
            dst_ref=dst,
            send_sem=sent.at[item],
            recv_sem=got.at[item],
            device_id=partner,
        )
        for item, (src, dst, (axis, size)) in enumerate(zip(swapped, received, plan))
    ]
    for copy in copies:
        copy.start()
    cells, width = out.shape[0], out.shape[1] // 3
    factor = HEAD ** (-0.5)
    shape = (cells, cells)
    own_key = lax.broadcasted_iota(jnp.int32, shape, 0) == lax.broadcasted_iota(jnp.int32, shape, 1)
    allowed = (slide_keys[...] == slide_queries[...]) & ((alive_keys[...] == 1) | own_key)
    grad_out = mat_nt(middle[...], out_w[...]).astype(BF16)
    for head in range(width // HEAD):
        first = head * HEAD
        q = projected[:, first : first + HEAD]
        k = projected[:, width + first : width + first + HEAD]
        v = projected[:, 2 * width + first : 2 * width + first + HEAD]
        g = grad_out[:, first : first + HEAD]
        scores = mat_nt(k, q) * factor - log_totals[head : head + 1, :]
        probs = jnp.where(allowed, jnp.exp(jnp.minimum(scores, 0.0)), 0.0)
        grad_probs = mat_nt(v, g)
        inner = jnp.sum(probs * grad_probs, axis=0, keepdims=True)
        grad_scores = (probs * (grad_probs - inner)).astype(BF16)
        out[:, first : first + HEAD] = (mat_tn(grad_scores, k) * factor).astype(BF16)
        out[:, width + first : width + first + HEAD] = (mat_nn(grad_scores, q) * factor).astype(BF16)
        out[:, 2 * width + first : 2 * width + first + HEAD] = mat_nn(
            probs.astype(BF16), g
        ).astype(BF16)
    for copy in copies:
        copy.wait()


def attend_back(number, middle, out_w, projected, log_totals, slide, alive, swaps):
    plan = tuple((axis, array.shape[axis] // 2) for array, axis in swaps)
    halves = [
        array.shape[:axis] + (array.shape[axis] // 2,) + array.shape[axis + 1 :]
        for array, axis in swaps
    ]
    vmem, anywhere = pl.BlockSpec(memory_space=pltpu.VMEM), pl.BlockSpec(memory_space=pl.ANY)
    count = len(swaps)
    results = pl.pallas_call(
        functools.partial(attend_back_kernel, plan),
        out_shape=[jax.ShapeDtypeStruct(projected.shape, BF16)]
        + [jax.ShapeDtypeStruct(half, BF16) for half in halves],
        in_specs=[vmem] * 7 + [anywhere] * count,
        out_specs=[vmem] + [anywhere] * count,
        scratch_shapes=[pltpu.SemaphoreType.DMA((max(count, 1),))] * 2,
        compiler_params=pltpu.CompilerParams(
            collective_id=number, has_side_effects=True, vmem_limit_bytes=48 * 2**20
        ),
        name="attend_back",
    )(
        middle,
        out_w,
        projected,
        log_totals,
        slide[:, None],
        slide[None, :],
        alive[:, None],
        *[array for array, _ in swaps],
    )
    return results[0], results[1:]


def part_of(ref, axis, index, size):
    span = pl.ds(index * size, size)
    if axis == 0:
        return ref.at[span, :]
    return ref.at[:, pl.ds(pl.multiple_of(index * size, 128), size)]


def settle_plain(out, place, value):
    out[place] = value


def line_sum(produce, hooks, settle, part, out, from_left, from_right, to_right, to_left, got_left, got_right, sent_right, sent_left):
    me, count = lax.axis_index("mp"), lax.axis_size("mp")
    pieces, height, width = from_left.shape
    splits = pieces * width // part.shape[1]
    stride = (part.shape[0] - height) // (splits - 1)
    has_right, has_left = me < count - 1, me > 0

    def place(piece):
        return (
            pl.ds(pl.multiple_of(lax.rem(piece, splits) * stride, 16), height),
            pl.ds(pl.multiple_of(lax.div(piece, splits) * width, width), width),
        )

    def rightward(piece):
        return pltpu.make_async_remote_copy(
            src_ref=to_right.at[piece],
            dst_ref=from_left.at[piece],
            send_sem=sent_right.at[piece],
            recv_sem=got_left.at[piece],
            device_id={"mp": me + 1},
        )

    def leftward(piece):
        return pltpu.make_async_remote_copy(
            src_ref=to_left.at[piece],
            dst_ref=from_right.at[piece],
            send_sem=sent_left.at[piece],
            recv_sem=got_right.at[piece],
            device_id={"mp": me - 1},
        )

    def flow(piece, copy, has_source, has_target, source, target):
        @pl.when((piece >= 0) & (piece < pieces))
        def _():
            @pl.when(has_source)
            def _():
                copy(piece).wait_recv()

            @pl.when(has_target & has_source)
            def _():
                target[piece] = (part[place(piece)] + source[piece].astype(F32)).astype(BF16)

            @pl.when(has_target & jnp.logical_not(has_source))
            def _():
                target[piece] = part[place(piece)].astype(BF16)

            @pl.when(has_target & (piece >= WINDOW))
            def _():
                copy(piece - WINDOW).wait_send()

            @pl.when(has_target)
            def _():
                copy(piece).start()

    moments = pieces + HOP_LAG * (count - 1)
    right_half = lax.div(2 * me + 1, count)
    trail = HOP_LAG * (right_half * me + (1 - right_half) * (count - 1 - me))

    def step(moment, carry):
        produce(moment)
        flow(moment - HOP_LAG * me, rightward, has_left, has_right, from_left, to_right)
        flow(
            moment - HOP_LAG * (count - 1 - me), leftward, has_right, has_left, from_right, to_left
        )
        done = moment - trail
        finished = (done >= 0) & (done < pieces)

        @pl.when(finished & has_left & has_right)
        def _():
            settle(
                out,
                place(done),
                part[place(done)] + from_left[done].astype(F32) + from_right[done].astype(F32),
            )

        @pl.when(finished & jnp.logical_not(has_left))
        def _():
            settle(out, place(done), part[place(done)] + from_right[done].astype(F32))

        @pl.when(finished & jnp.logical_not(has_right))
        def _():
            settle(out, place(done), part[place(done)] + from_left[done].astype(F32))

        return carry

    def finish():
        def step(piece, carry):
            @pl.when(has_right)
            def _():
                rightward(piece).wait_send()

            @pl.when(has_left)
            def _():
                leftward(piece).wait_send()

            return carry

        lax.fori_loop(pieces - WINDOW, pieces, step, 0)

    reached = 0
    for when, hook in hooks:
        if when > reached:
            lax.fori_loop(reached, when, step, 0)
            reached = when
        hook()
    lax.fori_loop(reached, moments, step, 0)
    finish()


PRODUCT_SCRATCH = 5


def start_product(form, left, right, part, left_in, right_in, left_sem, right_sem):
    transposed, sliced = form
    blocks = right_in.shape[0]
    width = part.shape[1] // blocks
    if sliced:
        rows = left_in.shape[0]
        first = pl.multiple_of(lax.axis_index("section") * rows, 16)
        left_copy = pltpu.make_async_copy(left.at[pl.ds(first, rows), :], left_in, left_sem)
        left_copy.start()

    def right_copy(block):
        span = pl.ds(pl.multiple_of(block * width, width), width)
        view = right.at[span, :] if transposed else right.at[:, span]
        return pltpu.make_async_copy(view, right_in.at[block], right_sem.at[block])

    for block in range(blocks):
        right_copy(block).start()
    if sliced:
        left_copy.wait()

    def produce(moment):
        @pl.when((lax.rem(moment, BLOCK_STEP) == 0) & (moment < blocks * BLOCK_STEP))
        def _():
            block = lax.div(moment, BLOCK_STEP)
            right_copy(block).wait()
            contract = (((1,), (1 if transposed else 0,)), ((), ()))
            part[:, pl.ds(pl.multiple_of(block * width, width), width)] = lax.dot_general(
                (left_in if sliced else left)[...],
                right_in[block],
                contract,
                preferred_element_type=F32,
            )

    return produce


def halfway(rows):
    return rows // 32 * 16


def block_of(ref, axis, index, size, start=0, stop=None):
    if axis == 0:
        stop = size if stop is None else stop
        return ref.at[pl.ds(pl.multiple_of(index * size + start, 16), stop - start), :]
    stop = ref.shape[0] if stop is None else stop
    return ref.at[pl.ds(start, stop - start), pl.ds(pl.multiple_of(index * size, 128), size)]


def reaction_moments(travelling):
    third = travelling / LINK_BYTES_PER_US
    last = 2 * len(range(8)) + 3 * HOP_LAG - 1
    return [
        min(last, math.ceil((parts * third + 2.0 + 0.5 * parts) / MOMENT_US)) for parts in (1, 2)
    ]


def comm_kernel(plan, *refs):
    refs = list(refs)

    def take(number):
        taken = refs[:number]
        del refs[:number]
        return taken

    reduces, gathers, swaps, exchanges, shares, pairs, travelling = plan
    groups = (len(gathers), len(swaps), len(exchanges), shares, pairs)
    sources = [take(n) for n in (2 if reduces else 0,) + groups]
    others = [take(1)[0] if paired else None for _, _, paired in exchanges]
    results = [take(n) for n in (1 if reduces else 0,) + groups]
    product = take(PRODUCT_SCRATCH) if reduces else None
    line = take(8) if reduces else None
    staging = [take(4 + paired) for _, _, paired in exchanges]
    sent, got, local_sem = refs

    section, z, dp = (lax.axis_index(name) for name in ("section", "mp", "dp"))
    count_z, count_dp = lax.axis_size("mp"), lax.axis_size("dp")
    row, col = dp // 2, dp % 2
    peer_x, peer_y = row * 2 + (1 - col), (1 - row) * 2 + col
    peer_d = (1 - row) * 2 + (1 - col)
    partner, to_x, to_y = {"section": 1 - section}, {"dp": peer_x}, {"dp": peer_y}

    barrier = pltpu.get_barrier_semaphore()
    fixed = 0
    if gathers or swaps or pairs:
        pl.semaphore_signal(barrier, inc=1, device_id=partner)
        fixed += 1
    if gathers or exchanges:
        pl.semaphore_signal(barrier, inc=1, device_id=to_x)
        pl.semaphore_signal(barrier, inc=1, device_id=to_y)
        fixed += 2
    if shares:
        for step in range(1, count_z):
            pl.semaphore_signal(barrier, inc=1, device_id={"mp": (z + step) % count_z})
        fixed += count_z - 1
    elif reduces:
        for exists, neighbour in ((z > 0, z - 1), (z < count_z - 1, z + 1)):

            @pl.when(exists)
            def _(neighbour=neighbour):
                pl.semaphore_signal(barrier, inc=1, device_id={"mp": neighbour})

        at_end = (z == 0) | (z == count_z - 1)

        @pl.when(at_end)
        def _():
            pl.semaphore_wait(barrier, fixed + 1)

        @pl.when(jnp.logical_not(at_end))
        def _():
            pl.semaphore_wait(barrier, fixed + 2)

    if fixed and (shares or not reduces):
        pl.semaphore_wait(barrier, fixed)

    used = [0, 0]

    def remote(src, dst, device):
        index = used[0]
        used[0] += 1
        return pltpu.make_async_remote_copy(
            src_ref=src, dst_ref=dst, send_sem=sent.at[index], recv_sem=got.at[index], device_id=device
        )

    def within(src, dst):
        index = used[1]
        used[1] += 1
        return pltpu.make_async_copy(src, dst, local_sem.at[index])

    locals_, early, first, second = [], [], [], []
    after_one, after_two, after_three = [], [], []
    receives, loads = [], []
    starts_d, starts_xy, conclusions = [], [], []
    for item, (axis, size) in enumerate(swaps):
        src, dst = sources[2][item], results[2][item]
        copy = remote(part_of(src, axis, 1 - section, size), dst, partner)
        early.append(copy)
        receives.append(copy)
    for item in range(pairs):
        copy = remote(sources[5][item], results[5][item], partner)
        early.append(copy)
        receives.append(copy)
    for item in range(shares):
        src, dst = sources[4][item], results[4][item]
        locals_.append(within(src, dst.at[z]))
        for step in range(1, count_z):
            copy = remote(src, dst.at[z], {"mp": (z + step) % count_z})
            early.append(copy)
            receives.append(copy)
    for item, (axis, size) in enumerate(gathers):
        src, dst = sources[1][item], results[1][item]
        rows = src.shape[0]
        cut = halfway(rows)

        def shard_of(index, start=0, stop=rows, dst=dst, axis=axis, size=size):
            return block_of(dst, axis, section * count_dp + index, size, start, stop)

        upper, lower = src.at[pl.ds(0, cut), :], src.at[pl.ds(cut, rows - cut), :]
        locals_.append(within(src, shard_of(dp)))
        own = remote(src, shard_of(dp), partner)
        x_upper = remote(upper, shard_of(dp, 0, cut), to_x)
        y_lower = remote(lower, shard_of(dp, cut), to_y)
        x_lower = remote(lower, shard_of(dp, cut), to_x)
        y_upper = remote(upper, shard_of(dp, 0, cut), to_y)
        pass_y = remote(shard_of(peer_x, 0, cut), shard_of(peer_x, 0, cut), to_y)
        pass_x = remote(shard_of(peer_y, cut), shard_of(peer_y, cut), to_x)
        relay_x = remote(shard_of(peer_x), shard_of(peer_x), partner)
        relay_y = remote(shard_of(peer_y), shard_of(peer_y), partner)
        relay_upper = remote(shard_of(peer_d, 0, cut), shard_of(peer_d, 0, cut), partner)
        relay_lower = remote(shard_of(peer_d, cut), shard_of(peer_d, cut), partner)
        early.append(own)
        first += [x_upper, y_lower]
        second += [x_lower, y_upper]
        after_one += [([x_upper], None, pass_y), ([y_lower], None, pass_x)]
        after_two += [([x_lower], None, relay_x), ([y_upper], None, relay_y)]
        after_three += [([pass_y], None, relay_upper), ([pass_x], None, relay_lower)]
        receives += [own, relay_x, relay_y, relay_upper, relay_lower]
    for item, (axis, size, paired) in enumerate(exchanges):
        src, dst = sources[3][item], results[3][item]
        mine, from_x, from_y, inbound = staging[item][:4]
        rows, dtype = from_x.shape[0], from_x.dtype
        cut = halfway(rows)
        rest = rows - cut
        half = section * count_dp if paired else 0
        fetched = []
        for role, index in enumerate((peer_d, peer_x, peer_y, dp)):
            copies = [within(block_of(src, axis, half + index, size), mine.at[role])]
            if paired:
                copies.append(
                    within(block_of(others[item], axis, index, size), staging[item][4].at[role])
                )
            fetched.append(copies)
            loads += copies

        def merge(role, mine=mine, other=staging[item][-1] if paired else None):
            def run():
                if other is not None:
                    mine[role] = (mine[role].astype(F32) + other[role].astype(F32)).astype(mine.dtype)

            return run

        top, bottom = pl.ds(0, cut), pl.ds(cut, rest)
        d_upper = remote(mine.at[0, top, :], inbound.at[top, :], to_x)
        d_lower = remote(mine.at[0, bottom, :], inbound.at[bottom, :], to_y)
        x_upper = remote(mine.at[1, top, :], from_x.at[top, :], to_x)
        y_lower = remote(mine.at[2, bottom, :], from_y.at[bottom, :], to_y)
        y_upper = remote(mine.at[2, top, :], from_y.at[top, :], to_y)
        x_lower = remote(mine.at[1, bottom, :], from_x.at[bottom, :], to_x)

        def add(role, span, mine=mine, term=inbound):
            def run():
                mine[role, span, :] = (
                    mine[role, span, :].astype(F32) + term[span, :].astype(F32)
                ).astype(mine.dtype)

            return run

        def conclude(mine=mine, from_x=from_x, from_y=from_y, dst=dst):
            dst[...] = mine[3].astype(F32) + from_x[...].astype(F32) + from_y[...].astype(F32)

        starts_d += [(fetched[0], merge(0), [d_upper, d_lower])]
        starts_xy += [
            (fetched[1], merge(1), [x_upper]),
            (fetched[2], merge(2), [y_lower]),
            (fetched[3], merge(3), []),
        ]
        after_one += [
            ([d_upper], add(2, top), y_upper),
            ([d_lower], add(1, bottom), x_lower),
        ]
        receives += [x_upper, y_lower, y_upper, x_lower]
        conclusions.append(conclude)

    remotes = early + first + second

    def begin():
        for copy in loads + remotes + locals_:
            copy.start()

    def send_parts():
        for copies, compute, targets in starts_d + starts_xy:
            for copy in copies:
                copy.wait()
            compute()
            for copy in targets:
                copy.start()

    def react(items):
        def run():
            for waits, compute, copy in items:
                for wait in waits:
                    wait.wait_recv()
                if compute is not None:
                    compute()
                copy.start()

        return run

    if reduces:
        produce = start_product(reduces, *sources[0], *product)
        moments = reaction_moments(travelling)
        hooks = [(0, begin), (2, send_parts), (moments[0], react(after_one)), (moments[1], react(after_two))]
        line_sum(produce, hooks, settle_plain, product[0], results[0][0], *line)
    else:
        begin()
        send_parts()
        react(after_one)()
        react(after_two)()
    react(after_three)()
    for copy in receives:
        copy.wait_recv()
    for conclude in conclusions:
        conclude()
    started = remotes + [copy for _, _, copies in starts_d + starts_xy for copy in copies]
    started += [copy for _, _, copy in after_one + after_two + after_three]
    for copy in started:
        copy.wait_send()
    for copy in locals_:
        copy.wait()


def comm(number, reduce=None, gathers=(), swaps=(), exchanges=(), shares=(), pairs=(), name="meet"):
    count_dp, count_z = lax.axis_size("dp"), lax.axis_size("mp")
    sections = lax.axis_size("section")

    def resized(shape, axis, size):
        return shape[:axis] + (size,) + shape[axis + 1 :]

    inputs, outputs, scratch = [], [], []
    plan_gathers, plan_swaps, plan_exchanges = [], [], []
    remote_count = local_count = travelling = 0
    reduces = None
    if reduce is not None:
        left, right, transposed, sliced = reduce
        reduces = (transposed, sliced)
        rows, depth = left.shape[0] // (sections if sliced else 1), left.shape[1]
        width = right.shape[0 if transposed else 1]
        blocks = width // 256
        inputs += [left, right]
        outputs.append(jax.ShapeDtypeStruct((rows, width), F32))
        scratch += [
            pltpu.VMEM((rows, width), F32),
            pltpu.VMEM((rows, depth) if sliced else (16, 128), BF16),
            pltpu.VMEM((blocks, 256, depth) if transposed else (blocks, depth, 256), BF16),
            pltpu.SemaphoreType.DMA,
            pltpu.SemaphoreType.DMA((blocks,)),
        ]
        buffer = pltpu.VMEM((width // 64, 256, 128), BF16)
        scratch += [buffer] * 4 + [pltpu.SemaphoreType.DMA((width // 64,))] * 4
    for shard, axis in gathers:
        size = shard.shape[axis]
        inputs.append(shard)
        outputs.append(
            jax.ShapeDtypeStruct(resized(shard.shape, axis, size * sections * count_dp), shard.dtype)
        )
        plan_gathers.append((axis, size))
        travelling += shard.size * shard.dtype.itemsize
        remote_count += 11
        local_count += 1
    for array, axis in swaps:
        size = array.shape[axis] // sections
        inputs.append(array)
        outputs.append(jax.ShapeDtypeStruct(resized(array.shape, axis, size), array.dtype))
        plan_swaps.append((axis, size))
        remote_count += 1
    other_inputs = []
    for array, other, axis in exchanges:
        paired = other is not None
        size = array.shape[axis] // (count_dp * (sections if paired else 1))
        piece = resized(array.shape, axis, size)
        inputs.append(array)
        outputs.append(jax.ShapeDtypeStruct(piece, F32))
        plan_exchanges.append((axis, size, paired))
        roles, one = pltpu.VMEM((4,) + piece, array.dtype), pltpu.VMEM(piece, array.dtype)
        scratch += [roles, one, one, one]
        if paired:
            other_inputs.append(other)
            scratch.append(roles)
        travelling += piece[0] * piece[1] * array.dtype.itemsize
        remote_count += 6
        local_count += 8
    for array in shares:
        inputs.append(array)
        outputs.append(jax.ShapeDtypeStruct((count_z,) + array.shape, array.dtype))
        remote_count += count_z - 1
        local_count += 1
    for array in pairs:
        inputs.append(array)
        outputs.append(jax.ShapeDtypeStruct(array.shape, array.dtype))
        remote_count += 1
    inputs += other_inputs
    scratch += [
        pltpu.SemaphoreType.DMA((max(remote_count, 1),)),
        pltpu.SemaphoreType.DMA((max(remote_count, 1),)),
        pltpu.SemaphoreType.DMA((max(local_count, 1),)),
    ]
    plan = (reduces, tuple(plan_gathers), tuple(plan_swaps), tuple(plan_exchanges), len(shares), len(pairs), travelling)
    placed = [True] * (reduces is not None) + [False] * (len(gathers) + len(swaps))
    placed += [True] * len(exchanges) + [False] * (len(shares) + len(pairs))
    vmem, anywhere = pl.BlockSpec(memory_space=pltpu.VMEM), pl.BlockSpec(memory_space=pl.ANY)
    outs = pl.pallas_call(
        functools.partial(comm_kernel, plan),
        out_shape=outputs,
        in_specs=([] if reduces is None else [anywhere if reduces[1] else vmem])
        + [anywhere] * (len(inputs) - (0 if reduces is None else 1)),
        out_specs=[vmem if in_vmem else anywhere for in_vmem in placed],
        scratch_shapes=scratch,
        compiler_params=pltpu.CompilerParams(
            collective_id=number, has_side_effects=True, vmem_limit_bytes=48 * 2**20
        ),
        cost_estimate=pl.CostEstimate(flops=1000000, bytes_accessed=90000000, transcendentals=0),
        name=name,
    )(*inputs)
    outs = list(outs)
    split = []
    for number_of in (1 if reduces else 0, len(gathers), len(swaps), len(exchanges), len(shares), len(pairs)):
        split.append(outs[:number_of])
        outs = outs[number_of:]
    return split


def spread(remote, src, dst, axis, size, section, dp, peers, partner, to_x, to_y):
    count_dp = lax.axis_size("dp")
    rows = src.shape[0]
    cut = halfway(rows)
    peer_x, peer_y, peer_d = peers

    def shard_of(index, start=0, stop=rows):
        return block_of(dst, axis, section * count_dp + index, size, start, stop)

    def still(*place):
        return (shard_of(*place), shard_of(*place))

    upper, lower = src.at[pl.ds(0, cut), :], src.at[pl.ds(cut, rows - cut), :]
    return {
        "own": remote(src, shard_of(dp), partner),
        "x_upper": remote(upper, shard_of(dp, 0, cut), to_x),
        "y_lower": remote(lower, shard_of(dp, cut), to_y),
        "x_lower": remote(lower, shard_of(dp, cut), to_x),
        "y_upper": remote(upper, shard_of(dp, 0, cut), to_y),
        "pass_y": remote(*still(peer_x, 0, cut), to_y),
        "pass_x": remote(*still(peer_y, cut), to_x),
        "relay_x": remote(*still(peer_x), partner),
        "relay_y": remote(*still(peer_y), partner),
        "relay_upper": remote(*still(peer_d, 0, cut), partner),
        "relay_lower": remote(*still(peer_d, cut), partner),
    }


def spread_steps(copies):
    def begin():
        for name in ("own", "x_upper", "y_lower", "x_lower", "y_upper"):
            copies[name].start()

    def follow(pairs):
        def run():
            for arrived, onward in pairs:
                copies[arrived].wait_recv()
                copies[onward].start()

        return run

    one = follow((("x_upper", "pass_y"), ("y_lower", "pass_x")))
    two = follow((("x_lower", "relay_x"), ("y_upper", "relay_y")))
    three = follow((("pass_y", "relay_upper"), ("pass_x", "relay_lower")))
    return begin, one, two, three


def head_kernel(plan, *refs):
    refs = list(refs)

    def take(number):
        taken = refs[:number]
        del refs[:number]
        return taken

    count = len(plan)
    places, frequency, expression, embed = take(4)
    shards = take(count)
    start, embed_all = take(2)
    gathered = take(count)
    part, codes, cells_in, columns_in, cells_sem, columns_sem = take(6)
    held = take(count)
    line = take(8)
    sent, got, local_sem = refs

    section, z, dp = (lax.axis_index(name) for name in ("section", "mp", "dp"))
    count_z, count_dp = lax.axis_size("mp"), lax.axis_size("dp")
    row, col = dp // 2, dp % 2
    peer_x, peer_y = row * 2 + (1 - col), (1 - row) * 2 + col
    peer_d = (1 - row) * 2 + (1 - col)
    peers = (peer_x, peer_y, peer_d)
    partner, to_x, to_y = {"section": 1 - section}, {"dp": peer_x}, {"dp": peer_y}
    rows, width = cells_in.shape[0], embed.shape[1]

    barrier = pltpu.get_barrier_semaphore()
    for device in (partner, to_x, to_y):
        pl.semaphore_signal(barrier, inc=1, device_id=device)
    for exists, neighbour in ((z > 0, z - 1), (z < count_z - 1, z + 1)):

        @pl.when(exists)
        def _(neighbour=neighbour):
            pl.semaphore_signal(barrier, inc=1, device_id={"mp": neighbour})

    at_end = (z == 0) | (z == count_z - 1)

    @pl.when(at_end)
    def _():
        pl.semaphore_wait(barrier, 4)

    @pl.when(jnp.logical_not(at_end))
    def _():
        pl.semaphore_wait(barrier, 5)

    used = [0, 0]

    def remote(src, dst, device):
        index = used[0]
        used[0] += 1
        return pltpu.make_async_remote_copy(
            src_ref=src, dst_ref=dst, send_sem=sent.at[index], recv_sem=got.at[index], device_id=device
        )

    def within(src, dst):
        index = used[1]
        used[1] += 1
        return pltpu.make_async_copy(src, dst, local_sem.at[index])

    place = (section, dp, peers, partner, to_x, to_y)
    main = spread(remote, embed, embed_all, 1, width, *place)
    begin, one, two, three = spread_steps(main)
    rest = [
        spread(remote, src, dst, axis, size, *place)
        for src, dst, (axis, size) in zip(shards, gathered, plan)
    ]
    rest_steps = [spread_steps(copies) for copies in rest]
    loads = [within(src, room) for src, room in zip(shards, held)]
    kept = [within(columns_in.at[0], block_of(embed_all, 1, section * count_dp + dp, width))]
    kept += [
        within(room, block_of(dst, axis, section * count_dp + dp, size))
        for room, dst, (axis, size) in zip(held, gathered, plan)
    ]

    order = [
        section * count_dp + dp,
        (1 - section) * count_dp + dp,
        section * count_dp + peer_x,
        section * count_dp + peer_y,
        (1 - section) * count_dp + peer_x,
        (1 - section) * count_dp + peer_y,
        section * count_dp + peer_d,
        (1 - section) * count_dp + peer_d,
    ]

    first = pl.multiple_of(section * rows, 16)
    cells_copy = pltpu.make_async_copy(expression.at[pl.ds(first, rows), :], cells_in, cells_sem)

    def fetch(turn):
        src = embed if turn == 0 else block_of(embed_all, 1, order[turn], width)
        return pltpu.make_async_copy(src, columns_in.at[turn], columns_sem.at[turn])

    begin()
    cells_copy.start()
    fetch(0).start()
    for copy in loads:
        copy.start()

    quarter = frequency.shape[1]
    for axis in range(2):
        along = places[:, axis : axis + 1] * frequency[...]
        codes[:, 2 * axis * quarter : (2 * axis + 1) * quarter] = jnp.sin(along)
        codes[:, (2 * axis + 1) * quarter : (2 * axis + 2) * quarter] = jnp.cos(along)
    cells_copy.wait()

    def keep():
        for copy in loads:
            copy.wait()
        for copy in kept:
            copy.start()

    def produce(moment):
        turn = lax.div(moment, 2)

        @pl.when((lax.rem(moment, 2) == 0) & (turn < len(order)))
        def _():
            pltpu.make_async_copy(embed, columns_in.at[turn], columns_sem.at[turn]).wait()
            part[:, pl.ds(pl.multiple_of(turn * width, width), width)] = mat_nn(
                cells_in[...], columns_in[turn]
            )

    def settle(out, where, value):
        span, columns = where
        turn = lax.div(columns.start, width)
        block = sum(jnp.where(turn == index, target, 0) for index, target in enumerate(order))
        columns = pl.ds(pl.multiple_of(block * width, width), width)
        out[span, columns] = value + codes[span, columns]

    def arrived(names, turns):
        def run():
            for name in names:
                main[name].wait_recv()
            for turn in turns:
                fetch(turn).start()

        return run

    def neighbours():
        one()
        for steps in rest_steps:
            steps[0]()
        two()
        for turn in (2, 3):
            fetch(turn).start()

    def diagonal():
        three()
        fetch(6).start()

    def later(number):
        def run():
            for steps in rest_steps:
                steps[number]()

        return run

    hooks = [
        (1, keep),
        (2, arrived(("own",), (1,))),
        (4, neighbours),
        (8, arrived(("relay_x", "relay_y"), (4, 5))),
        (12, diagonal),
        (14, arrived(("relay_upper", "relay_lower"), (7,))),
        (17, later(1)),
        (21, later(2)),
    ]
    line_sum(produce, hooks, settle, part, start, *line)
    for steps in rest_steps:
        steps[3]()
    for copies in rest:
        for name in ("own", "relay_x", "relay_y", "relay_upper", "relay_lower"):
            copies[name].wait_recv()
    for copies in [main] + rest:
        for copy in copies.values():
            copy.wait_send()
    for copy in kept:
        copy.wait()


def head(number, places, expression, embed, gathers):
    sections, count_dp = lax.axis_size("section"), lax.axis_size("dp")
    rows, genes = places.shape[0], expression.shape[1]
    width = embed.shape[1]
    total_parts = sections * count_dp
    features = total_parts * width
    quarter = features // 4
    frequency = jnp.exp(jnp.arange(quarter, dtype=F32) * (-math.log(10000.0) / quarter))[None, :]
    vmem, anywhere = pl.BlockSpec(memory_space=pltpu.VMEM), pl.BlockSpec(memory_space=pl.ANY)
    plan = tuple((axis, shard.shape[axis]) for shard, axis in gathers)
    shapes = [
        shard.shape[:axis] + (shard.shape[axis] * total_parts,) + shard.shape[axis + 1 :]
        for shard, axis in gathers
    ]
    pieces = features // 64
    buffer = pltpu.VMEM((pieces, 256, 128), BF16)
    copies = 11 * (1 + len(gathers))
    results = pl.pallas_call(
        functools.partial(head_kernel, plan),
        out_shape=[
            jax.ShapeDtypeStruct((rows, features), F32),
            jax.ShapeDtypeStruct((genes, features), BF16),
        ]
        + [jax.ShapeDtypeStruct(shape, shard.dtype) for shape, (shard, _) in zip(shapes, gathers)],
        in_specs=[vmem] * 2 + [anywhere] * (2 + len(gathers)),
        out_specs=[vmem] + [anywhere] * (1 + len(gathers)),
        scratch_shapes=[
            pltpu.VMEM((rows, features), F32),
            pltpu.VMEM((rows, features), F32),
            pltpu.VMEM((rows, genes), BF16),
            pltpu.VMEM((total_parts, genes, width), BF16),
            pltpu.SemaphoreType.DMA,
            pltpu.SemaphoreType.DMA((total_parts,)),
        ]
        + [pltpu.VMEM(shard.shape, shard.dtype) for shard, _ in gathers]
        + [buffer] * 4
        + [pltpu.SemaphoreType.DMA((pieces,))] * 4
        + [
            pltpu.SemaphoreType.DMA((copies,)),
            pltpu.SemaphoreType.DMA((copies,)),
            pltpu.SemaphoreType.DMA((1 + 2 * len(gathers),)),
        ],
        compiler_params=pltpu.CompilerParams(
            collective_id=number, has_side_effects=True, vmem_limit_bytes=48 * 2**20
        ),
        name="head",
    )(places, frequency, expression, embed, *[shard for shard, _ in gathers])
    return results[0], results[1], results[2:]


def trade(remote, mine, indices, from_x, from_y, inbound, to_x, to_y):
    rows = from_x.shape[0]
    cut = halfway(rows)
    top, bottom = pl.ds(0, cut), pl.ds(cut, rows - cut)
    d, x, y, own = indices
    d_upper = remote(mine.at[d, top, :], inbound.at[top, :], to_x)
    d_lower = remote(mine.at[d, bottom, :], inbound.at[bottom, :], to_y)
    x_upper = remote(mine.at[x, top, :], from_x.at[top, :], to_x)
    y_lower = remote(mine.at[y, bottom, :], from_y.at[bottom, :], to_y)
    y_upper = remote(mine.at[y, top, :], from_y.at[top, :], to_y)
    x_lower = remote(mine.at[x, bottom, :], from_x.at[bottom, :], to_x)

    def pass_on():
        for copy, index, span, onward in (
            (d_upper, y, top, y_upper),
            (d_lower, x, bottom, x_lower),
        ):
            copy.wait_recv()
            mine[index, span, :] = (
                mine[index, span, :].astype(F32) + inbound[span, :].astype(F32)
            ).astype(mine.dtype)
            onward.start()

    def conclude():
        for copy in (x_upper, y_lower, y_upper, x_lower):
            copy.wait_recv()
        for copy in (d_upper, d_lower, x_upper, y_lower, y_upper, x_lower):
            copy.wait_send()
        return mine[own].astype(F32) + from_x[...].astype(F32) + from_y[...].astype(F32)

    return (d_upper, d_lower), (x_upper, y_lower), pass_on, conclude


def tail_kernel(
    start, expression, embed, grad_rebuilt, qkv, out, small, qkv_other, out_other,
    embed_sum, qkv_sum, out_sum, small_sum, cells_own, cells_other,
    start_other, start_turned, x_own, x_other, embed_in, cells, embed_parts, embed_x, embed_y, embed_in_d,
    qkv_parts, qkv_x, qkv_y, qkv_in_d, qkv_partner, out_parts, out_x, out_y, out_in_d, out_partner,
    small_parts, small_x, small_y, small_in_d, small_partner, sent, got, local_sem,
):
    section, dp = lax.axis_index("section"), lax.axis_index("dp")
    count_dp = lax.axis_size("dp")
    row, col = dp // 2, dp % 2
    peer_x, peer_y = row * 2 + (1 - col), (1 - row) * 2 + col
    peer_d = (1 - row) * 2 + (1 - col)
    partner, to_x, to_y = {"section": 1 - section}, {"dp": peer_x}, {"dp": peer_y}
    rows, genes = cells.shape
    half = start_other.shape[1]
    width = half // count_dp

    barrier = pltpu.get_barrier_semaphore()
    for device in (partner, to_x, to_y):
        pl.semaphore_signal(barrier, inc=1, device_id=device)
    pl.semaphore_wait(barrier, 3)

    used = [0, 0]

    def remote(src, dst, device):
        index = used[0]
        used[0] += 1
        return pltpu.make_async_remote_copy(
            src_ref=src, dst_ref=dst, send_sem=sent.at[index], recv_sem=got.at[index], device_id=device
        )

    def within(src, dst):
        index = used[1]
        used[1] += 1
        return pltpu.make_async_copy(src, dst, local_sem.at[index])

    def half_of(index):
        return pl.ds(pl.multiple_of(index * half, 128), half)

    def rows_of(index):
        return pl.ds(pl.multiple_of(index * rows, 16), rows)

    swaps = [
        remote(start.at[:, half_of(1 - section)], start_other, partner),
        remote(small.at[1 - section], small_partner, partner),
    ]
    for copy in swaps:
        copy.start()
    roles = (peer_d, peer_x, peer_y, dp)
    fetches = []
    for src, other, axis, parts, parts_other in (
        (qkv, qkv_other, 0, qkv_parts, qkv_partner),
        (out, out_other, 1, out_parts, out_partner),
    ):
        size = src.shape[axis] // (2 * count_dp)
        for role, index in enumerate(roles):
            fetches.append(
                within(block_of(src, axis, section * count_dp + index, size), parts.at[role])
            )
            fetches.append(within(block_of(other, axis, index, size), parts_other.at[role]))
    fetches.append(within(small.at[section], small_parts))
    load_own = within(expression.at[rows_of(section), :], x_own)
    load_other = within(expression.at[rows_of(1 - section), :], x_other)
    load_embed = within(embed, embed_in)
    load_cells = within(grad_rebuilt, cells)
    for copy in fetches + [load_own, load_other, load_embed, load_cells]:
        copy.start()

    trades = [
        trade(remote, parts, indices, *buffers, to_x, to_y)
        for parts, indices, buffers in (
            (qkv_parts, (0, 1, 2, 3), (qkv_x, qkv_y, qkv_in_d)),
            (out_parts, (0, 1, 2, 3), (out_x, out_y, out_in_d)),
            (small_parts, roles, (small_x, small_y, small_in_d)),
            (embed_parts, roles, (embed_x, embed_y, embed_in_d)),
        )
    ]

    for copy in fetches:
        copy.wait()
    swaps[1].wait_recv()
    for parts, other in (
        (qkv_parts, qkv_partner),
        (out_parts, out_partner),
        (small_parts, small_partner),
    ):
        parts[...] = (parts[...].astype(F32) + other[...].astype(F32)).astype(parts.dtype)
    for first, second, _, _ in trades[:3]:
        for copy in first + second:
            copy.start()

    load_own.wait()
    load_other.wait()
    swaps[0].wait_recv()
    start_turned[0] = start[:, half_of(section)].T
    start_turned[1] = start_other[...].T

    def embed_tile(span, size):
        tile = mat_nn(start_turned[0], x_own[:, span]) + mat_nn(start_turned[1], x_other[:, span])
        embed_parts[:, :, span] = tile.reshape(count_dp, width, size).astype(BF16)

    whole = genes // TILE

    def embed_step(index, carry):
        embed_tile(pl.ds(pl.multiple_of(index * TILE, TILE), TILE), TILE)
        return carry

    lax.fori_loop(0, whole, embed_step, 0)
    if genes % TILE:
        embed_tile(pl.ds(whole * TILE, genes % TILE), genes % TILE)
    for copy in trades[3][0] + trades[3][1]:
        copy.start()

    load_embed.wait()
    load_cells.wait()

    def cells_tile(span):
        tile = mat_nt(start[...], embed_in[span, :]).astype(BF16)
        cells[:, span] = (tile.astype(F32) - cells[:, span].astype(F32)).astype(BF16)

    def cells_step(index, carry):
        cells_tile(pl.ds(pl.multiple_of(index * TILE, TILE), TILE))
        return carry

    lax.fori_loop(0, whole, cells_step, 0)
    if genes % TILE:
        cells_tile(pl.ds(whole * TILE, genes % TILE))
    give = remote(cells, cells_other, partner)
    give.start()
    keep = within(cells, cells_own)
    keep.start()

    for _, _, pass_on, _ in trades:
        pass_on()
    qkv_sum[...] = trades[0][3]()
    out_sum[...] = trades[1][3]()
    small_sum[...] = trades[2][3]()
    embed_sum[...] = trades[3][3]().T
    for copy in swaps:
        copy.wait_send()
    give.wait()
    keep.wait()


def assemble_kernel(own, other, whole, held, arrived, left):
    section = lax.axis_index("section")
    rows = own.shape[0]
    spans = [(start, min(128, rows - start)) for start in range(0, rows, 128)]
    loads, stores = [], []
    for place, (src, index) in enumerate(((own, section), (other, 1 - section))):
        for part, (start, size) in enumerate(spans):
            span = pl.ds(start, size)
            target = pl.ds(pl.multiple_of(index * rows + start, 16), size)
            number = place * len(spans) + part
            loads.append(
                pltpu.make_async_copy(src.at[span, :], held.at[place, span, :], arrived.at[number])
            )
            stores.append(
                pltpu.make_async_copy(held.at[place, span, :], whole.at[target, :], left.at[number])
            )
    for load in loads:
        load.start()
    for load, store in zip(loads, stores):
        load.wait()
        store.start()
    for store in stores:
        store.wait()


def tail(number, start, expression, embed, grad_rebuilt, qkv, qkv_other, out, out_other, small):
    rows, features = start.shape
    genes, count_dp = embed.shape[0], lax.axis_size("dp")
    half = features // 2
    width = half // count_dp
    vmem, anywhere = pl.BlockSpec(memory_space=pltpu.VMEM), pl.BlockSpec(memory_space=pl.ANY)

    def buffers(shape, dtype, paired):
        parts, one = pltpu.VMEM((count_dp,) + shape, dtype), pltpu.VMEM(shape, dtype)
        return [parts, one, one, one] + ([parts] if paired else [])

    qkv_piece = (qkv.shape[0] // (2 * count_dp), qkv.shape[1])
    out_piece = (out.shape[0], out.shape[1] // (2 * count_dp))
    small_piece = small.shape[2:]
    cells = jax.ShapeDtypeStruct((rows, genes), BF16)
    results = pl.pallas_call(
        tail_kernel,
        out_shape=[
            jax.ShapeDtypeStruct((genes, width), F32),
            jax.ShapeDtypeStruct(qkv_piece, F32),
            jax.ShapeDtypeStruct(out_piece, F32),
            jax.ShapeDtypeStruct(small_piece, F32),
            cells,
            cells,
        ],
        in_specs=[vmem] + [anywhere] * 8,
        out_specs=[vmem] * 4 + [anywhere] * 2,
        scratch_shapes=[
            pltpu.VMEM((rows, half), BF16),
            pltpu.VMEM((2, half, rows), BF16),
            pltpu.VMEM((rows, genes), BF16),
            pltpu.VMEM((rows, genes), BF16),
            pltpu.VMEM((genes, features), BF16),
            pltpu.VMEM((rows, genes), BF16),
        ]
        + buffers((width, genes), BF16, False)
        + buffers(qkv_piece, BF16, True)
        + buffers(out_piece, BF16, True)
        + buffers(small_piece, F32, True)
        + [
            pltpu.SemaphoreType.DMA((27,)),
            pltpu.SemaphoreType.DMA((27,)),
            pltpu.SemaphoreType.DMA((22,)),
        ],
        compiler_params=pltpu.CompilerParams(
            collective_id=number, has_side_effects=True, vmem_limit_bytes=56 * 2**20
        ),
        name="tail",
    )(start, expression, embed, grad_rebuilt, qkv, out, small, qkv_other, out_other)
    whole = pl.pallas_call(
        assemble_kernel,
        out_shape=jax.ShapeDtypeStruct((2 * rows, genes), BF16),
        in_specs=[anywhere] * 2,
        out_specs=anywhere,
        scratch_shapes=[pltpu.VMEM((2, rows, genes), BF16)]
        + [pltpu.SemaphoreType.DMA((2 * (-(-rows // 128)),))] * 2,
        compiler_params=pltpu.CompilerParams(vmem_limit_bytes=56 * 2**20),
        name="assemble",
    )(results[4], results[5])
    return list(results[:4]) + [whole]


def line_pipe(produce, hooks, items, spacing, part, total, from_left, from_right, to_right, to_left, got_left, got_right, sent_right, sent_left):
    me, count = lax.axis_index("mp"), lax.axis_size("mp")
    pieces = part.shape[2] // 128
    has_right, has_left = me < count - 1, me > 0

    def place(slot):
        column = lax.rem(slot, spacing) * 128
        return (lax.rem(lax.div(slot, spacing), 2), slice(None), pl.ds(pl.multiple_of(column, 128), 128))

    rooms = from_left.shape[0]

    def room_of(slot):
        return lax.rem(slot, rooms)

    def rightward(slot):
        room = room_of(slot)
        return pltpu.make_async_remote_copy(
            src_ref=to_right.at[room],
            dst_ref=from_left.at[room],
            send_sem=sent_right.at[room],
            recv_sem=got_left.at[room],
            device_id={"mp": me + 1},
        )

    def leftward(slot):
        room = room_of(slot)
        return pltpu.make_async_remote_copy(
            src_ref=to_left.at[room],
            dst_ref=from_right.at[room],
            send_sem=sent_left.at[room],
            recv_sem=got_right.at[room],
            device_id={"mp": me - 1},
        )

    def used(slot):
        return (slot >= 0) & (slot < items * spacing) & (lax.rem(slot, spacing) < pieces)

    def flow(slot, copy, has_source, has_target, source, target):
        @pl.when(used(slot))
        def _():
            room = room_of(slot)

            @pl.when(has_source)
            def _():
                copy(slot).wait_recv()

            @pl.when(has_target & (slot >= rooms))
            def _():
                copy(slot).wait_send()

            @pl.when(has_target & has_source)
            def _():
                target[room] = (part[place(slot)] + source[room].astype(F32)).astype(BF16)

            @pl.when(has_target & jnp.logical_not(has_source))
            def _():
                target[room] = part[place(slot)].astype(BF16)

            @pl.when(has_target)
            def _():
                copy(slot).start()

    right_half = lax.div(2 * me + 1, count)
    trail = HOP_LAG * (right_half * me + (1 - right_half) * (count - 1 - me))

    def step(moment, carry):
        for when, hook in hooks:
            pl.when(moment == when)(hook)
        produce(moment)
        flow(moment - HOP_LAG * me, rightward, has_left, has_right, from_left, to_right)
        flow(
            moment - HOP_LAG * (count - 1 - me), leftward, has_right, has_left, from_right, to_left
        )
        done = moment - trail

        room = room_of(done)

        @pl.when(used(done) & has_left & has_right)
        def _():
            total[place(done)] = (
                part[place(done)] + from_left[room].astype(F32) + from_right[room].astype(F32)
            )

        @pl.when(used(done) & jnp.logical_not(has_left))
        def _():
            total[place(done)] = part[place(done)] + from_right[room].astype(F32)

        @pl.when(used(done) & jnp.logical_not(has_right))
        def _():
            total[place(done)] = part[place(done)] + from_left[room].astype(F32)

        return carry

    lax.fori_loop(0, (items + 1) * spacing, step, 0)

    def finish(slot, carry):
        @pl.when(used(slot) & has_right)
        def _():
            rightward(slot).wait_send()

        @pl.when(used(slot) & has_left)
        def _():
            leftward(slot).wait_send()

        return carry

    lax.fori_loop(items * spacing - rooms, items * spacing, finish, 0)


def pipe_spacing(pieces, count):
    return max(pieces + 1, (pieces - 1 + HOP_LAG * (count - 1)) // 2 + 1)


def middle_kernel(
    plan, spacing, attended, start, gain, bias, out_w, noise, centers, spreads, *refs
):
    refs = list(refs)

    def take(number):
        taken = refs[:number]
        del refs[:number]
        return taken

    count = len(plan)
    shards = take(count)
    (normed_out, scale_out, second_out, upper_out, active_out, hidden_out, log_vars_out,
     latent_out, spread_out, latent_low_out, decoder_out, density_all) = take(12)
    gathered = take(count)
    part, total, kept_rows, density = take(4)
    up_in, down_in, latent_in, dec_in = take(4)
    held = take(count)
    line = take(8)
    sent, got, local_sem = refs

    section, z, dp = (lax.axis_index(name) for name in ("section", "mp", "dp"))
    count_z, count_dp = lax.axis_size("mp"), lax.axis_size("dp")
    row, col = dp // 2, dp % 2
    peer_x, peer_y = row * 2 + (1 - col), (1 - row) * 2 + col
    peers = (peer_x, peer_y, (1 - row) * 2 + (1 - col))
    partner, to_x, to_y = {"section": 1 - section}, {"dp": peer_x}, {"dp": peer_y}
    cells, latents = noise.shape
    half_rows = part.shape[1]
    comp_count = centers.shape[0]

    barrier = pltpu.get_barrier_semaphore()
    for device in (partner, to_x, to_y):
        pl.semaphore_signal(barrier, inc=1, device_id=device)
    for step in range(1, count_z):
        pl.semaphore_signal(barrier, inc=1, device_id={"mp": (z + step) % count_z})
    pl.semaphore_wait(barrier, 3 + count_z - 1)

    used = [0, 0]

    def remote(src, dst, device):
        index = used[0]
        used[0] += 1
        return pltpu.make_async_remote_copy(
            src_ref=src, dst_ref=dst, send_sem=sent.at[index], recv_sem=got.at[index], device_id=device
        )

    def within(src, dst):
        index = used[1]
        used[1] += 1
        return pltpu.make_async_copy(src, dst, local_sem.at[index])

    around = (section, dp, peers, partner, to_x, to_y)
    spreads_of = [
        spread(remote, src, dst, axis, size, *around)
        for src, dst, (axis, size) in zip(shards, gathered, plan)
    ]
    steps_of = [spread_steps(copies) for copies in spreads_of]
    loads = [within(src, room) for src, room in zip(shards, held)]
    keeps = [
        within(room, block_of(dst, axis, section * count_dp + dp, size))
        for room, dst, (axis, size) in zip(held, gathered, plan)
    ]
    fetches = [
        within(src, dst) for src, dst in zip(gathered, (up_in, down_in, latent_in, dec_in))
    ]
    density_sends = [
        remote(density, density_all.at[z], {"mp": (z + step) % count_z})
        for step in range(1, count_z)
    ]
    density_keep = within(density, density_all.at[z])

    def run_steps(items, number):
        def run():
            for item in items:
                steps_of[item][number]()

        return run

    def keep():
        for load in loads:
            load.wait()
        for copy in keeps:
            copy.start()

    near, far = list(range(count - 1)), [count - 1]

    def fetch():
        for item in near:
            for name in ("own", "relay_x", "relay_y", "relay_upper", "relay_lower"):
                spreads_of[item][name].wait_recv()
            keeps[item].wait()
        for copy in fetches:
            copy.start()
        for copy in fetches:
            copy.wait()

    def share():
        for copy in density_sends + [density_keep]:
            copy.start()

    for load in loads:
        load.start()

    def rows_of(half):
        return pl.ds(pl.multiple_of(half * (cells - half_rows), 16), half_rows)

    def out_product(half):
        part[half] = mat_nn(attended[rows_of(half), :], out_w[...])

    def feed_forward(half):
        rows = rows_of(half)
        values = start[rows, :] + total[half]
        kept_rows[half] = values
        normed, scale = normalize(values)
        second = (normed * gain[...] + bias[...]).astype(BF16)
        upper = mat_nn(second, up_in[...])
        active = gelu(upper).astype(BF16)
        part[half] = mat_nn(active, down_in[...])
        normed_out[rows, :] = normed
        scale_out[rows, :] = scale
        second_out[rows, :] = second
        upper_out[rows, :] = upper
        active_out[rows, :] = active

    def latents_of(half):
        rows = rows_of(half)
        hidden = (kept_rows[half] + total[half]).astype(BF16)
        hidden_out[rows, :] = hidden
        stats = mat_nn(hidden, latent_in[...])
        means, log_vars = stats[:, :latents], stats[:, latents:]
        own_noise = noise[rows, :]
        scaled = jnp.exp(0.5 * log_vars) * own_noise
        latent = means + scaled
        low = latent.astype(BF16)
        part[half] = mat_nn(low, dec_in[...])
        log_vars_out[rows, :] = log_vars
        spread_out[rows, :] = scaled
        latent_out[rows, :] = latent
        latent_low_out[rows, :] = low
        lane = lax.broadcasted_iota(jnp.int32, (half_rows, 128), 1)
        columns = jnp.sum(
            -0.5 * LOG_TWO_PI - 0.5 * log_vars - 0.5 * own_noise * own_noise, axis=1, keepdims=True
        )
        table = jnp.where(lane == comp_count, columns, 0.0)
        for index in range(comp_count):
            log_spread = spreads[index : index + 1, :]
            offset = latent - centers[index : index + 1, :]
            columns = jnp.sum(
                -0.5 * LOG_TWO_PI - 0.5 * log_spread - 0.5 * offset * offset * jnp.exp(-log_spread),
                axis=1,
                keepdims=True,
            )
            table = jnp.where(lane == index, columns, table)
        density[:, pl.ds(pl.multiple_of(half * half_rows, 128), half_rows)] = table.T[
            : density.shape[0], :
        ]

    def conclude(half):
        decoder_out[rows_of(half), :] = total[half]

    def produce(moment):
        item = lax.div(moment, spacing)
        half, stage = lax.rem(item, 2), lax.div(item, 2)
        begins = lax.rem(moment, spacing) == 0
        for number, work in enumerate((out_product, feed_forward, latents_of, conclude)):
            pl.when(begins & (stage == number))(functools.partial(work, half))

    hooks = [
        (0, run_steps(near, 0)),
        (1, keep),
        (7, run_steps(near, 1)),
        (13, run_steps(near, 2)),
        (16, run_steps(near, 3)),
        (2 * spacing, fetch),
        (2 * spacing + 1, run_steps(far, 0)),
        (2 * spacing + 10, run_steps(far, 1)),
        (2 * spacing + 18, run_steps(far, 2)),
        (2 * spacing + 26, run_steps(far, 3)),
        (5 * spacing + 1, share),
    ]
    line_pipe(produce, hooks, 6, spacing, part, total, *line)
    conclude(1)
    for item in far:
        for name in ("own", "relay_x", "relay_y", "relay_upper", "relay_lower"):
            spreads_of[item][name].wait_recv()
        keeps[item].wait()
    for copies in spreads_of:
        for copy in copies.values():
            copy.wait_send()
    for copy in density_sends:
        copy.wait()
    density_keep.wait()


def middle(number, attended, start, gain, bias, out_w, noise, centers, spreads, gathers):
    sections, count_dp, count_z = (lax.axis_size(name) for name in ("section", "dp", "mp"))
    cells, features = start.shape
    latents = noise.shape[1]
    total_parts = sections * count_dp
    pieces = features // 128
    spacing = pipe_spacing(pieces, count_z)
    half_rows = 256
    plan = tuple((axis, shard.shape[axis]) for shard, axis in gathers)
    shapes = [
        shard.shape[:axis] + (shard.shape[axis] * total_parts,) + shard.shape[axis + 1 :]
        for shard, axis in gathers
    ]
    units = shapes[0][1]
    vmem, anywhere = pl.BlockSpec(memory_space=pltpu.VMEM), pl.BlockSpec(memory_space=pl.ANY)
    outputs = [
        ((cells, features), F32),
        ((cells, 1), F32),
        ((cells, features), BF16),
        ((cells, units), F32),
        ((cells, units), BF16),
        ((cells, features), BF16),
        ((cells, latents), F32),
        ((cells, latents), F32),
        ((cells, latents), F32),
        ((cells, latents), BF16),
        ((cells, features), F32),
        ((count_z, 24, 2 * half_rows), F32),
    ] + [(shape, BF16) for shape in shapes]
    rooms = 2 * spacing
    buffer = pltpu.VMEM((rooms, half_rows, 128), BF16)
    copies = 11 * len(gathers) + count_z - 1
    halves = pltpu.VMEM((2, half_rows, features), F32)
    results = pl.pallas_call(
        functools.partial(middle_kernel, plan, spacing),
        out_shape=[jax.ShapeDtypeStruct(*item) for item in outputs],
        in_specs=[vmem] * 8 + [anywhere] * len(gathers),
        out_specs=[vmem] * 11 + [anywhere] * (1 + len(gathers)),
        scratch_shapes=[halves, halves, halves, pltpu.VMEM((24, 2 * half_rows), F32)]
        + [pltpu.VMEM(shape, BF16) for shape in shapes[:-1]]
        + [pltpu.VMEM(shard.shape, BF16) for shard, _ in gathers]
        + [buffer] * 4
        + [pltpu.SemaphoreType.DMA((rooms,))] * 4
        + [
            pltpu.SemaphoreType.DMA((copies,)),
            pltpu.SemaphoreType.DMA((copies,)),
            pltpu.SemaphoreType.DMA((3 * len(gathers),)),
        ],
        compiler_params=pltpu.CompilerParams(
            collective_id=number, has_side_effects=True, vmem_limit_bytes=60 * 2**20
        ),
        name="middle",
    )(attended, start, gain, bias, out_w, noise, centers, spreads, *[shard for shard, _ in gathers])
    return results[:12], results[12:]


def back_kernel(
    spacing, latent_total, ramp_step, counts, grad_rebuilt, decoder_pre, latent, spread_latent, respons, alive, centers,
    spreads, upper, normed, scale, gain, genes_w, dec_w, latent_w, down_w, up_w, grad_genes,
    pre_out, stats_out, weighted_out, hidden_out, upper_out, middle_out, low_out, sums_out,
    genes_sum, genes_other, part, total, hidden_rows, counts_all, kl_scale, genes_in, dec_in, latent_in, down_in,
    up_in, mine, theirs, from_x, from_y, inbound, *refs
):
    line, (sent, got, local_sem) = refs[:8], refs[8:]
    section, z, dp = (lax.axis_index(name) for name in ("section", "mp", "dp"))
    count_z, count_dp = lax.axis_size("mp"), lax.axis_size("dp")
    row, col = dp // 2, dp % 2
    peer_x, peer_y = row * 2 + (1 - col), (1 - row) * 2 + col
    peers = (peer_x, peer_y, (1 - row) * 2 + (1 - col))
    partner, to_x, to_y = {"section": 1 - section}, {"dp": peer_x}, {"dp": peer_y}
    cells = upper.shape[0]
    half_rows = part.shape[1]
    comp_count = centers.shape[0]

    barrier = pltpu.get_barrier_semaphore()
    for device in (partner, to_x, to_y):
        pl.semaphore_signal(barrier, inc=1, device_id=device)
    for exists, neighbour in ((z > 0, z - 1), (z < count_z - 1, z + 1)):

        @pl.when(exists)
        def _(neighbour=neighbour):
            pl.semaphore_signal(barrier, inc=1, device_id={"mp": neighbour})

    at_end = (z == 0) | (z == count_z - 1)

    @pl.when(at_end)
    def _():
        pl.semaphore_wait(barrier, 4)

    @pl.when(jnp.logical_not(at_end))
    def _():
        pl.semaphore_wait(barrier, 5)

    used = [0, 0]

    def remote(src, dst, device):
        index = used[0]
        used[0] += 1
        return pltpu.make_async_remote_copy(
            src_ref=src, dst_ref=dst, send_sem=sent.at[index], recv_sem=got.at[index], device_id=device
        )

    def within(src, dst):
        index = used[1]
        used[1] += 1
        return pltpu.make_async_copy(src, dst, local_sem.at[index])

    count_rows = counts.shape[0]
    around = (section, dp, peers, partner, to_x, to_y)
    counting = spread(remote, counts, counts_all, 0, count_rows, *around)
    count_steps = spread_steps(counting)
    size = from_x.shape[0]
    swap = remote(part_of(grad_genes, 0, 1 - section, size * count_dp), genes_other, partner)
    indices = (peers[2], peer_x, peer_y, dp)
    load_mine = [
        within(block_of(grad_genes, 0, section * count_dp + index, size), mine.at[index])
        for index in range(count_dp)
    ]
    load_theirs = [
        within(block_of(genes_other, 0, index, size), theirs.at[index]) for index in range(count_dp)
    ]
    first, second, pass_on, conclude_genes = trade(
        remote, mine, indices, from_x, from_y, inbound, to_x, to_y
    )
    load_genes = within(genes_w, genes_in)
    fetches = [
        within(src, dst)
        for src, dst in ((dec_w, dec_in), (latent_w, latent_in), (down_w, down_in), (up_w, up_in))
    ]

    load_genes.start()
    counts_all[pl.ds(pl.multiple_of((section * count_dp + dp) * count_rows, 8), count_rows), :] = (
        counts[...]
    )

    def begin():
        count_steps[0]()
        swap.start()
        for copy in fetches + load_mine:
            copy.start()
        load_genes.wait()

    def count_cells():
        for name in ("own", "relay_x", "relay_y", "relay_upper", "relay_lower"):
            counting[name].wait_recv()
        for copy in fetches:
            copy.wait()
        sums = sum(
            counts_all[index * count_rows : index * count_rows + 8, :]
            for index in range(counts_all.shape[0] // count_rows)
        )
        mean_kl = sums[0:1, :] / (latent_total * sums[1:2, :])
        excess = mean_kl - FREE_BITS
        small = jnp.exp(-jnp.abs(excess))
        above = 1.0 + small
        log_above = jnp.where(above == 1.0, small, jnp.log(above) * (small / (above - 1.0)))
        softplus = jnp.maximum(excess, 0.0) + log_above
        sigmoid = jnp.where(excess >= 0.0, 1.0, small) / above
        kl_scale[0:1, :] = ramp_step[0:1, :] * softplus * sigmoid

    def open_theirs():
        swap.wait_recv()
        for copy in load_theirs:
            copy.start()

    def trade_begins():
        for copy in load_mine + load_theirs:
            copy.wait()
        mine[...] = (mine[...].astype(F32) + theirs[...].astype(F32)).astype(BF16)
        for copy in first + second:
            copy.start()

    def rows_of(half):
        return pl.ds(pl.multiple_of(half * (cells - half_rows), 16), half_rows)

    def genes_product(half):
        part[half] = mat_nt(grad_rebuilt[rows_of(half), :], genes_in[...])

    def latents_back(half):
        rows = rows_of(half)
        pre = (total[half] * gelu_slope(decoder_pre[rows, :])).astype(BF16)
        pre_out[rows, :] = pre
        weight = kl_scale[0:1, 0:1] * alive[rows, :]
        weighted = respons[rows, :] * weight
        weighted_out[rows, :] = weighted
        own_latent = latent[rows, :]
        grad_latent = mat_nt(pre, dec_in[...])
        for index in range(comp_count):
            pulled = (own_latent - centers[index : index + 1, :]) * jnp.exp(
                -spreads[index : index + 1, :]
            )
            grad_latent = grad_latent + weighted[:, index : index + 1] * pulled
        grad_logs = grad_latent * (0.5 * spread_latent[rows, :]) - 0.5 * weight
        stats = jnp.concatenate([grad_latent.astype(BF16), grad_logs.astype(BF16)], axis=1)
        stats_out[rows, :] = stats
        part[half] = mat_nt(stats, latent_in[...])

    def feed_back(half):
        rows = rows_of(half)
        hidden = total[half].astype(BF16)
        hidden_rows[half] = hidden
        hidden_out[rows, :] = hidden
        grad_upper = (mat_nt(hidden, down_in[...]) * gelu_slope(upper[rows, :])).astype(BF16)
        upper_out[rows, :] = grad_upper
        part[half] = mat_nt(grad_upper, up_in[...])

    def conclude(half):
        rows = rows_of(half)
        grad_norm, own_normed = total[half], normed[rows, :]
        grad_middle = hidden_rows[half].astype(F32) + norm_back(
            grad_norm, own_normed, scale[rows, :], gain[...]
        )
        middle_out[rows, :] = grad_middle
        low_out[rows, :] = grad_middle.astype(BF16)
        return grad_norm * own_normed, grad_norm

    def conclude_first(half):
        scaled, plain = conclude(half)
        sums_out[0:1, :] = jnp.sum(scaled, axis=0, keepdims=True)
        sums_out[1:2, :] = jnp.sum(plain, axis=0, keepdims=True)

    def produce(moment):
        item = lax.div(moment, spacing)
        half, stage = lax.rem(item, 2), lax.div(item, 2)
        begins = lax.rem(moment, spacing) == 0
        for number, work in enumerate((genes_product, latents_back, feed_back, conclude_first)):
            pl.when(begins & (stage == number))(functools.partial(work, half))

    hooks = [
        (0, begin),
        (4, count_steps[1]),
        (6, count_steps[2]),
        (8, count_steps[3]),
        (10, open_theirs),
        (13, trade_begins),
        (2 * spacing, count_cells),
        (2 * spacing + 6, pass_on),
    ]
    line_pipe(produce, hooks, 6, spacing, part, total, *line)
    scaled, plain = conclude(1)
    repeated = 2 * half_rows - cells
    sums_out[0:1, :] += jnp.sum(scaled[repeated:, :], axis=0, keepdims=True)
    sums_out[1:2, :] += jnp.sum(plain[repeated:, :], axis=0, keepdims=True)
    genes_sum[...] = conclude_genes()
    for copy in counting.values():
        copy.wait_send()
    swap.wait_send()


def back(number, latent_total, ramp, counts, grad_rebuilt, decoder_pre, latent, spread_latent, respons, alive, centers,
         spreads, upper, normed, scale, gain, genes_w, dec_w, latent_w, down_w, up_w, grad_genes):
    sections, count_dp, count_z = (lax.axis_size(name) for name in ("section", "dp", "mp"))
    cells, features = decoder_pre.shape
    units, latents = upper.shape[1], latent.shape[1]
    spacing = pipe_spacing(features // 128, count_z)
    rooms, half_rows = 2 * spacing, 256
    vmem, anywhere = pl.BlockSpec(memory_space=pltpu.VMEM), pl.BlockSpec(memory_space=pl.ANY)
    piece = (grad_genes.shape[0] // (sections * count_dp), grad_genes.shape[1])
    roles, one = pltpu.VMEM((count_dp,) + piece, BF16), pltpu.VMEM(piece, BF16)
    buffer = pltpu.VMEM((rooms, half_rows, 128), BF16)
    halves = pltpu.VMEM((2, half_rows, features), F32)
    outputs = [
        ((cells, features), BF16),
        ((cells, 2 * latents), BF16),
        (respons.shape, F32),
        ((cells, features), BF16),
        ((cells, units), BF16),
        ((cells, features), F32),
        ((cells, features), BF16),
        ((8, features), F32),
        (piece, F32),
        ((piece[0] * count_dp, piece[1]), BF16),
    ]
    copies = 11 + 1 + 6
    results = pl.pallas_call(
        functools.partial(back_kernel, spacing, float(latent_total)),
        out_shape=[jax.ShapeDtypeStruct(*item) for item in outputs],
        in_specs=[vmem] * 14 + [anywhere] * 6,
        out_specs=[vmem] * 9 + [anywhere],
        scratch_shapes=[
            halves,
            halves,
            pltpu.VMEM((2, half_rows, features), BF16),
            pltpu.VMEM((sections * count_dp * counts.shape[0], 128), F32),
            pltpu.VMEM((8, 128), F32),
        ]
        + [pltpu.VMEM(array.shape, BF16) for array in (genes_w, dec_w, latent_w, down_w, up_w)]
        + [roles, roles, one, one, one]
        + [buffer] * 4
        + [pltpu.SemaphoreType.DMA((rooms,))] * 4
        + [
            pltpu.SemaphoreType.DMA((copies,)),
            pltpu.SemaphoreType.DMA((copies,)),
            pltpu.SemaphoreType.DMA((2 * count_dp + 5,)),
        ],
        compiler_params=pltpu.CompilerParams(
            collective_id=number, has_side_effects=True, vmem_limit_bytes=62 * 2**20
        ),
        name="back",
    )(ramp, counts, grad_rebuilt, decoder_pre, latent, spread_latent, respons, alive, centers, spreads, upper,
      normed, scale, gain, genes_w, dec_w, latent_w, down_w, up_w, grad_genes)
    return results[:9]


def meet(tiled, number, reduce=None, gathers=(), swaps=(), exchanges=(), shares=(), pairs=()):
    if tiled:
        return comm(number, reduce, gathers, swaps, exchanges, shares, pairs)
    partner = [(i, 1 - i) for i in range(2)]
    section, count_dp = lax.axis_index("section"), lax.axis_size("dp")
    swapped = []
    for array, axis in swaps:
        size = array.shape[axis] // 2
        half = lax.dynamic_slice_in_dim(array, (1 - section) * size, size, axis)
        swapped.append(lax.ppermute(half, "section", partner))
    exchanged = []
    for array, other, axis in exchanges:
        if other is not None:
            array = half_sum(array, other, axis)
        parts = lax.all_to_all(jnp.stack(jnp.split(array, count_dp, axis)), "dp", 0, 0)
        exchanged.append(total(parts))
    return [
        [] if reduce is None else comm(number, reduce)[0][0:1],
        [lax.all_gather(shard, ("section", "dp"), axis=axis, tiled=True) for shard, axis in gathers],
        swapped,
        exchanged,
        [lax.all_gather(array, "mp") for array in shares],
        [lax.ppermute(array, "section", partner) for array in pairs],
    ]


def half_sum(array, received, axis):
    size = received.shape[axis]
    own = lax.dynamic_slice_in_dim(array, lax.axis_index("section") * size, size, axis)
    return (own.astype(F32) + received.astype(F32)).astype(array.dtype)


def total(parts):
    return jnp.sum(parts.astype(F32), axis=0)


def local(
    expression,
    cell_xy,
    live_mask,
    lengths,
    ramp_step,
    latent_noise,
    gene_embed,
    ln1_gain,
    ln1_bias,
    w_query,
    w_key,
    w_value,
    w_out,
    ln2_gain,
    ln2_bias,
    w_up,
    w_down,
    w_mean,
    w_logvar,
    comp_mean,
    comp_logvar,
    w_dec,
    w_genes,
):
    micro_count = lengths.shape[0]
    cells = expression.shape[0] // micro_count
    micro = lax.axis_index("section")
    latent_cols = w_mean.shape[1]
    comp_count, comp_width = comp_mean.shape
    width = ln1_gain.shape[0]
    shards = 2 * lax.axis_size("dp")
    features = shards * width
    tiled = width % 128 == 0 and lax.axis_size("dp") == 4
    meeting = functools.partial(meet, tiled)

    def own(array, axis=0):
        return lax.dynamic_slice_in_dim(array, micro * cells, cells, axis)

    alive = own(live_mask)
    alive_float = alive.astype(F32)
    noise = own(latent_noise)
    slide = slide_ids(lax.dynamic_index_in_dim(lengths, micro, 0, False), cells)

    norm_block = jnp.pad(jnp.stack([ln1_gain, ln1_bias, ln2_gain, ln2_bias]), ((0, 12), (0, 0)))
    comp_block = jnp.pad(
        jnp.concatenate([comp_mean, comp_logvar], axis=0), ((0, 0), (0, width - comp_width))
    )
    small = jnp.concatenate([norm_block, comp_block], axis=0)
    small_rows = small.shape[0]
    qkv_shard = jnp.concatenate([w_query, w_key, w_value], axis=1)
    places = own(cell_xy, 1)
    weights = ((small, 0), (qkv_shard, 0), (w_out, 1))
    if tiled:
        start, embed, (small_all, qkv, out_w) = head(
            0, places.T, expression, gene_embed, weights
        )
    else:
        _, (embed, small_all, qkv, out_w), _, _, _, _ = meeting(
            0, gathers=((gene_embed, 1),) + weights
        )
        (summed,), _, _, _, _, _ = meeting(1, (expression, embed, False, True))
        start = summed + position_code(places, features)
    small_all = small_all.reshape(shards, small_rows, width).astype(F32)
    norm_params = small_all[:, :4].transpose(1, 0, 2).reshape(4, features)
    gain_one, bias_one, gain_two, bias_two = (norm_params[i : i + 1] for i in range(4))
    comps = small_all[:, 16:, :comp_width].transpose(1, 0, 2).reshape(2 * comp_count, -1)
    centers, spreads = comps[:comp_count], comps[comp_count:]

    normed_one, scale_one, first_low, projected, attended, log_totals = attend(
        start, gain_one, bias_one, qkv, slide, alive
    )
    latent_shard = jnp.concatenate([w_mean, w_logvar], axis=1)
    precision = jnp.exp(-spreads)
    if tiled:
        states, (up_w, down_w, latent_w, dec_w, genes_w) = middle(
            1,
            attended,
            start,
            gain_two,
            bias_two,
            out_w,
            noise,
            centers,
            spreads,
            ((w_up, 0), (w_down, 1), (latent_shard, 0), (w_dec, 1), (w_genes, 0)),
        )
        (normed_two, scale_two, second_low, upper, activated, hidden, log_vars, latent, spread_latent,
         latent_low, decoder_pre, density_parts) = states
        density = jnp.sum(density_parts, axis=0)
        rows = density.shape[1] // 2
        densities = jnp.concatenate([density[:, :rows], density[:, 3 * rows - cells :]], axis=1)
    else:
        (summed,), (up_w, down_w, latent_w, dec_w), _, _, _, _ = meeting(
            2, (attended, out_w, False, False), gathers=((w_up, 0), (w_down, 1), (latent_shard, 0), (w_dec, 1))
        )
        after_attn = start + summed
        normed_two, scale_two = normalize(after_attn)
        second_low = (normed_two * gain_two + bias_two).astype(BF16)
        upper = mat_nn(second_low, up_w)
        activated = gelu(upper).astype(BF16)
        (summed,), (genes_w,), _, _, _, _ = meeting(
            3, (activated, down_w, False, False), gathers=((w_genes, 0),)
        )
        hidden = (after_attn + summed).astype(BF16)

        stats = mat_nn(hidden, latent_w)
        means, log_vars = stats[:, :latent_cols], stats[:, latent_cols:]
        spread_latent = jnp.exp(0.5 * log_vars) * noise
        latent = means + spread_latent
        latent_low = latent.astype(BF16)
        post_part = jnp.sum(-0.5 * LOG_TWO_PI - 0.5 * log_vars - 0.5 * noise * noise, axis=1)
        offsets = latent[None] - centers[:, None, :]
        pulled = offsets * precision[:, None, :]
        comp_part = jnp.sum(
            -0.5 * LOG_TWO_PI - 0.5 * spreads[:, None, :] - 0.5 * offsets * pulled, axis=2
        )
        density_part = jnp.pad(
            jnp.concatenate([comp_part, post_part[None]], axis=0), ((0, 7), (0, -cells % 128))
        )
        (decoder_pre,), _, _, _, (density_parts,), _ = meeting(
            4, (latent_low, dec_w, False, False), shares=(density_part,)
        )
        densities = jnp.sum(density_parts, axis=0)[:, :cells]
    logits = densities[:comp_count] - math.log(comp_count)
    log_post = densities[comp_count]
    largest = jnp.max(logits, axis=0, keepdims=True)
    log_prior = largest[0] + jnp.log(jnp.sum(jnp.exp(logits - largest), axis=0))
    respons = jnp.exp(logits - log_prior[None, :])
    divergence = jnp.sum((log_post - log_prior) * alive_float)
    grad_rebuilt, grad_genes = decode(micro, decoder_pre, genes_w, expression, alive_float)

    counts = jnp.concatenate(
        [jnp.full((1, 128), divergence), jnp.full((31, 128), jnp.sum(alive_float))], axis=0
    )
    ramp_weight = jnp.minimum(1.0, (ramp_step[0] + 1).astype(F32) / RAMP)
    offsets = latent[None] - centers[:, None, :]
    pulled = offsets * precision[:, None, :]
    if tiled:
        (grad_pre, grad_stats, weighted, grad_hidden, grad_upper, grad_middle, middle_low, norm_sums,
         genes_parts) = back(
            2,
            LATENT,
            jnp.full((8, 128), ramp_weight),
            counts,
            grad_rebuilt,
            decoder_pre,
            latent,
            spread_latent,
            jnp.pad(respons.T, ((0, 0), (0, 128 - comp_count))),
            alive_float[:, None],
            centers,
            spreads,
            upper,
            normed_two,
            scale_two,
            gain_two,
            genes_w,
            dec_w,
            latent_w,
            down_w,
            up_w,
            grad_genes,
        )
        weighted = weighted[:, :comp_count].T[:, :, None]
        grad_dec = mat_tn(latent_low, grad_pre).astype(BF16)
        grad_latent_w = mat_tn(hidden, grad_stats).astype(BF16)
        grad_down = mat_tn(activated, grad_hidden).astype(BF16)
        grad_up = mat_tn(second_low, grad_upper).astype(BF16)
    else:
        (grad_act,), (count_parts,), (genes_other,), _, _, _ = meeting(
            5, (grad_rebuilt, genes_w, True, False), gathers=((counts, 0),), swaps=((grad_genes, 0),)
        )
        count_parts = jnp.sum(count_parts.reshape(shards, 32, 128)[:, :, 0], axis=0)
        mean_kl = count_parts[0] / (LATENT * count_parts[1])
        kl_scale = (
            ramp_weight * jax.nn.softplus(mean_kl - FREE_BITS) * jax.nn.sigmoid(mean_kl - FREE_BITS)
        )
        grad_pre = (grad_act * gelu_slope(decoder_pre)).astype(BF16)
        grad_dec = mat_tn(latent_low, grad_pre).astype(BF16)
        cell_weight = kl_scale * alive_float
        weighted = (respons * cell_weight[None, :])[:, :, None]
        grad_latent = mat_nt(grad_pre, dec_w) + jnp.sum(weighted * pulled, axis=0)
        grad_means = grad_latent.astype(BF16)
        grad_logs = (grad_latent * (0.5 * spread_latent) - 0.5 * cell_weight[:, None]).astype(BF16)
        grad_stats = jnp.concatenate([grad_means, grad_logs], axis=1)
        grad_latent_w = mat_tn(hidden, grad_stats).astype(BF16)
        (summed,), _, (latent_other, dec_other), (genes_parts,), _, _ = meeting(
            6,
            (grad_stats, latent_w, True, False),
            swaps=((grad_latent_w, 0), (grad_dec, 1)),
            exchanges=((grad_genes, genes_other, 0),),
        )
        grad_hidden = summed.astype(BF16)

        grad_down = mat_tn(activated, grad_hidden).astype(BF16)
        grad_upper = (mat_nt(grad_hidden, down_w) * gelu_slope(upper)).astype(BF16)
        grad_up = mat_tn(second_low, grad_upper).astype(BF16)
        (grad_norm_two,), _, (down_other, up_other), _, _, _ = (
            meeting(
                7,
                (grad_upper, up_w, True, False),
                swaps=((grad_down, 1), (grad_up, 0)),
            )
        )
        grad_middle = grad_hidden.astype(F32) + norm_back(
            grad_norm_two, normed_two, scale_two, gain_two
        )
        middle_low = grad_middle.astype(BF16)
        norm_sums = [jnp.sum(grad_norm_two * normed_two, axis=0), jnp.sum(grad_norm_two, axis=0)]
    grad_comps = jnp.concatenate(
        [
            -jnp.sum(weighted * pulled, axis=1),
            -jnp.sum(weighted * (0.5 * offsets * pulled - 0.5), axis=1),
        ],
        axis=0,
    )
    grad_out = mat_tn(attended, middle_low).astype(BF16)
    if tiled:
        grad_qkv_act, (down_other, up_other, latent_other, dec_other) = attend_back(
            3,
            middle_low,
            out_w,
            projected,
            log_totals,
            slide,
            alive,
            ((grad_down, 1), (grad_up, 0), (grad_latent_w, 0), (grad_dec, 1)),
        )
    else:
        grad_qkv_act, _ = attend_back(
            11, middle_low, out_w, projected, log_totals, slide, alive, ()
        )
    grad_qkv = mat_tn(first_low, grad_qkv_act).astype(BF16)
    (grad_norm_one,), _, (qkv_other, out_other), (down_parts, up_parts, latent_parts, dec_parts), _, _ = meeting(
        8,
        (grad_qkv_act, qkv, True, False),
        swaps=((grad_qkv, 0), (grad_out, 1)),
        exchanges=(
            (grad_down, down_other, 1),
            (grad_up, up_other, 0),
            (grad_latent_w, latent_other, 0),
            (grad_dec, dec_other, 1),
        ),
    )
    grad_start = grad_middle + norm_back(grad_norm_one, normed_one, scale_one, gain_one)
    start_low = grad_start.astype(BF16)

    norm_grads = jnp.stack(
        [
            jnp.sum(grad_norm_one * normed_one, axis=0),
            jnp.sum(grad_norm_one, axis=0),
            norm_sums[0],
            norm_sums[1],
        ]
    )
    norm_grads = norm_grads.reshape(4, shards, width).transpose(1, 0, 2)
    comp_grads = grad_comps.reshape(2 * comp_count, shards, comp_width).transpose(1, 0, 2)
    small_grads = jnp.concatenate(
        [
            jnp.pad(norm_grads, ((0, 0), (0, 12), (0, 0))),
            jnp.pad(comp_grads, ((0, 0), (0, 0), (0, width - comp_width))),
        ],
        axis=1,
    ).reshape(shards * small_rows, width)
    if tiled:
        embed_parts, qkv_parts, out_parts, small_sum, grad_expression = tail(
            9,
            start_low,
            expression,
            embed,
            grad_rebuilt,
            grad_qkv,
            qkv_other,
            grad_out,
            out_other,
            small_grads.reshape(2, shards // 2, small_rows, width),
        )
    else:
        start_all = lax.all_gather(start_low, "section", axis=0, tiled=True)
        start_half = lax.dynamic_slice_in_dim(start_all, micro * (features // 2), features // 2, 1)
        grad_embed = mat_tn(expression, start_half).astype(BF16)
        grad_cells = (
            mat_nt(start_low, embed).astype(BF16).astype(F32) - grad_rebuilt.astype(F32)
        ).astype(BF16)
        grad_expression = lax.all_gather(grad_cells, "section", axis=0, tiled=True)
        small_other = lax.ppermute(
            lax.dynamic_slice_in_dim(
                small_grads, (1 - micro) * (shards // 2 * small_rows), shards // 2 * small_rows, 0
            ),
            "section",
            [(0, 1), (1, 0)],
        )
        _, _, _, (embed_parts, qkv_parts, out_parts, small_sum), _, _ = meeting(
            9,
            exchanges=(
                (grad_embed, None, 1),
                (grad_qkv, qkv_other, 0),
                (grad_out, out_other, 1),
                (small_grads, small_other, 0),
            ),
        )
    grad_query, grad_key, grad_value = jnp.split(qkv_parts, 3, axis=1)
    grad_mean, grad_logvar = jnp.split(latent_parts, 2, axis=1)
    return (
        embed_parts,
        small_sum[0],
        small_sum[1],
        grad_query,
        grad_key,
        grad_value,
        out_parts,
        small_sum[2],
        small_sum[3],
        up_parts,
        down_parts,
        grad_mean,
        grad_logvar,
        small_sum[16 : 16 + comp_count, :comp_width],
        small_sum[16 + comp_count :, :comp_width],
        dec_parts,
        genes_parts,
        grad_expression,
    )


def solution(mesh):
    weight_rows = P(("section", "dp"), "mp")
    weight_cols = P("mp", ("section", "dp"))
    vector = P(("section", "dp"))
    comps = P(None, ("mp", "section", "dp"))
    weights = (
        weight_cols, vector, vector, weight_rows, weight_rows, weight_rows, weight_cols,
        vector, vector, weight_rows, weight_cols, weight_rows, weight_rows, comps, comps,
        weight_cols, weight_rows,
    )
    return jax.shard_map(
        local,
        mesh=mesh,
        in_specs=(P("dp", "mp"), P(None, "dp"), P("dp"), P("dp", None), P(), P("dp", "mp"))
        + weights,
        out_specs=weights + (P("dp", "mp"),),
        check_vma=False,
    )
```

```python
import functools
import math

import jax
import jax.numpy as jnp
from jax import lax
from jax.experimental import pallas as pl
from jax.experimental.pallas import tpu as pltpu
from jax.sharding import PartitionSpec as P

HEAD = 64
LATENT = 512
RAMP = 1000
LOG_TWO_PI = 1.8378770664093453
NEG_LARGE = -1e30
FREE_BITS = 1.0
HOP_LAG = 3
WINDOW = 3
BLOCK_STEP = 4
TILE = 256
PARTS = 4
PART_ROWS = 128
PIECE_COLUMNS = 256
TILES_FROM = 15
LINK_BYTES_PER_US = 92000.0
MOMENT_US = 1.3
SPREAD = 1
SPREAD_FROM = 0
SPREAD_STEP = 1
F32 = jnp.float32
BF16 = jnp.bfloat16


def mat_nn(left, right):
    return jnp.dot(left, right, preferred_element_type=F32)


def mat_tn(left, right):
    return lax.dot_general(left, right, (((0,), (0,)), ((), ())), preferred_element_type=F32)


def mat_nt(left, right):
    return lax.dot_general(left, right, (((1,), (1,)), ((), ())), preferred_element_type=F32)


def gelu(values):
    return 0.5 * values * (1.0 + lax.erf(values * 0.7071067811865476))


def gelu_slope(values):
    return (
        0.5 * (1.0 + lax.erf(values * 0.7071067811865476))
        + values * jnp.exp(-0.5 * values * values) * 0.3989422804014327
    )


def normalize(values):
    center = values - jnp.mean(values, axis=-1, keepdims=True)
    scale = lax.rsqrt(jnp.mean(center * center, axis=-1, keepdims=True) + 1e-05)
    return center * scale, scale


def norm_back(grad_in, normed, scale, gain):
    scaled = grad_in * gain
    return scale * (
        scaled
        - jnp.mean(scaled, axis=-1, keepdims=True)
        - normed * jnp.mean(scaled * normed, axis=-1, keepdims=True)
    )


def position_code(places, feature_count):
    quarter = feature_count // 4
    frequency = jnp.exp(jnp.arange(quarter, dtype=F32) * (-math.log(10000.0) / quarter))
    along_x = places[0][:, None] * frequency[None, :]
    along_y = places[1][:, None] * frequency[None, :]
    return jnp.concatenate(
        [jnp.sin(along_x), jnp.cos(along_x), jnp.sin(along_y), jnp.cos(along_y)], axis=1
    )


def slide_ids(length_row, cell_count):
    bounds = jnp.cumsum(length_row)[:-1]
    index = jnp.arange(cell_count, dtype=jnp.int32)
    return jnp.sum((index[:, None] >= bounds[None, :]).astype(jnp.int32), axis=1)


def allowed_pairs(info):
    columns = info[...].T
    cells = columns.shape[0]
    shape = (cells, cells)
    own_key = lax.broadcasted_iota(jnp.int32, shape, 0) == lax.broadcasted_iota(jnp.int32, shape, 1)
    return (columns[:, 0:1] == info[0:1, :]) & ((columns[:, 1:2] == 1.0) | own_key)


def attend_kernel(start, gain, bias, weights, info, *outs):
    normed_out, scale_out, low_out, projected_out, attended_out, totals_out = outs
    cells, width = attended_out.shape
    factor = HEAD ** (-0.5)
    normed, scale = normalize(start[...])
    normed_out[...] = normed
    scale_out[...] = scale
    low = (normed * gain[...] + bias[...]).astype(BF16)
    low_out[...] = low
    projected = mat_nn(low, weights[...]).astype(BF16)
    projected_out[...] = projected
    allowed = allowed_pairs(info)
    for head_index in range(width // HEAD):
        first = head_index * HEAD
        q = projected[:, first : first + HEAD]
        k = projected[:, width + first : width + first + HEAD]
        v = projected[:, 2 * width + first : 2 * width + first + HEAD]
        scores = jnp.where(allowed, mat_nt(k, q) * factor, NEG_LARGE)
        largest = jnp.max(scores, axis=0, keepdims=True)
        exponents = jnp.exp(scores - largest)
        sums = jnp.sum(exponents, axis=0, keepdims=True)
        probs = (exponents / sums).astype(BF16)
        attended_out[:, first : first + HEAD] = mat_tn(probs, v).astype(BF16)
        totals_out[head_index : head_index + 1, :] = largest + jnp.log(sums)


def attend(start, gain, bias, weights, info):
    cells, features = start.shape
    width = weights.shape[1] // 3
    return pl.pallas_call(
        attend_kernel,
        out_shape=[
            jax.ShapeDtypeStruct((cells, features), F32),
            jax.ShapeDtypeStruct((cells, 1), F32),
            jax.ShapeDtypeStruct((cells, features), BF16),
            jax.ShapeDtypeStruct((cells, 3 * width), BF16),
            jax.ShapeDtypeStruct((cells, width), BF16),
            jax.ShapeDtypeStruct((width // HEAD, cells), F32),
        ],
        compiler_params=pltpu.CompilerParams(vmem_limit_bytes=48 * 2**20),
        name="attend",
    )(start, gain, bias, weights, info)


def decode_kernel(section, pre, weights, cells, alive, residual, grad, act, act_turned):
    @pl.when(pl.program_id(0) == 0)
    def _():
        value = gelu(pre[...]).astype(BF16)
        act[...] = value
        act_turned[...] = value.T

    rebuilt = mat_nn(act[...], weights[...])
    difference = ((rebuilt - cells[...].astype(F32)) * alive[...]).astype(BF16)
    residual[...] = difference
    grad[...] = mat_nn(act_turned[...], difference).astype(BF16)


def decode(micro, pre, weights, expression, alive):
    rows, features = pre.shape
    genes = weights.shape[1]
    block = 512
    return pl.pallas_call(
        decode_kernel,
        grid_spec=pltpu.PrefetchScalarGridSpec(
            num_scalar_prefetch=1,
            grid=(pl.cdiv(genes, block),),
            in_specs=[
                pl.BlockSpec((rows, features), lambda step, section: (0, 0)),
                pl.BlockSpec((features, block), lambda step, section: (0, step)),
                pl.BlockSpec((rows, block), lambda step, section: (section[0], step)),
                pl.BlockSpec((rows, 1), lambda step, section: (0, 0)),
            ],
            out_specs=[
                pl.BlockSpec((rows, block), lambda step, section: (0, step)),
                pl.BlockSpec((features, block), lambda step, section: (0, step)),
            ],
            scratch_shapes=[pltpu.VMEM((rows, features), BF16), pltpu.VMEM((features, rows), BF16)],
        ),
        out_shape=[
            jax.ShapeDtypeStruct((rows, genes), BF16),
            jax.ShapeDtypeStruct((features, genes), BF16),
        ],
        compiler_params=pltpu.CompilerParams(vmem_limit_bytes=48 * 2**20),
        name="decode",
    )(micro.astype(jnp.int32).reshape(1), pre, weights, expression, alive[:, None])


def attend_back_kernel(plan, middle, out_w, projected, log_totals, info, *refs):
    swapped, out, received = refs[: len(plan)], refs[len(plan)], refs[len(plan) + 1 : 2 * len(plan) + 1]
    sent, got = refs[2 * len(plan) + 1 :]
    section = lax.axis_index("section")
    partner = {"section": 1 - section}
    barrier = pltpu.get_barrier_semaphore()
    pl.semaphore_signal(barrier, inc=1, device_id=partner)
    pl.semaphore_wait(barrier, 1)
    copies = [
        pltpu.make_async_remote_copy(
            src_ref=part_of(src, axis, 1 - section, size),
            dst_ref=dst,
            send_sem=sent.at[item],
            recv_sem=got.at[item],
            device_id=partner,
        )
        for item, (src, dst, (axis, size)) in enumerate(zip(swapped, received, plan))
    ]
    for copy in copies:
        copy.start()
    cells, width = out.shape[0], out.shape[1] // 3
    factor = HEAD ** (-0.5)
    allowed = allowed_pairs(info)
    grad_out = mat_nt(middle[...], out_w[...]).astype(BF16)
    for head in range(width // HEAD):
        first = head * HEAD
        q = projected[:, first : first + HEAD]
        k = projected[:, width + first : width + first + HEAD]
        v = projected[:, 2 * width + first : 2 * width + first + HEAD]
        g = grad_out[:, first : first + HEAD]
        scores = mat_nt(k, q) * factor - log_totals[head : head + 1, :]
        probs = jnp.where(allowed, jnp.exp(jnp.minimum(scores, 0.0)), 0.0)
        grad_probs = mat_nt(v, g)
        inner = jnp.sum(probs * grad_probs, axis=0, keepdims=True)
        grad_scores = (probs * (grad_probs - inner)).astype(BF16)
        out[:, first : first + HEAD] = (mat_tn(grad_scores, k) * factor).astype(BF16)
        out[:, width + first : width + first + HEAD] = (mat_nn(grad_scores, q) * factor).astype(BF16)
        out[:, 2 * width + first : 2 * width + first + HEAD] = mat_nn(
            probs.astype(BF16), g
        ).astype(BF16)
    for copy in copies:
        copy.wait()


def attend_back(number, middle, out_w, projected, log_totals, info, swaps):
    plan = tuple((axis, array.shape[axis] // 2) for array, axis in swaps)
    halves = [
        array.shape[:axis] + (array.shape[axis] // 2,) + array.shape[axis + 1 :]
        for array, axis in swaps
    ]
    vmem, anywhere = pl.BlockSpec(memory_space=pltpu.VMEM), pl.BlockSpec(memory_space=pl.ANY)
    count = len(swaps)
    results = pl.pallas_call(
        functools.partial(attend_back_kernel, plan),
        out_shape=[jax.ShapeDtypeStruct(projected.shape, BF16)]
        + [jax.ShapeDtypeStruct(half, BF16) for half in halves],
        in_specs=[vmem] * 5 + [anywhere] * count,
        out_specs=[vmem] + [anywhere] * count,
        scratch_shapes=[pltpu.SemaphoreType.DMA((max(count, 1),))] * 2,
        compiler_params=pltpu.CompilerParams(
            collective_id=number, has_side_effects=True, vmem_limit_bytes=48 * 2**20
        ),
        name="attend_back",
    )(
        middle,
        out_w,
        projected,
        log_totals,
        info,
        *[array for array, _ in swaps],
    )
    return results[0], results[1:]


def part_of(ref, axis, index, size):
    span = pl.ds(index * size, size)
    if axis == 0:
        return ref.at[span, :]
    return ref.at[:, pl.ds(pl.multiple_of(index * size, 128), size)]


def settle_plain(out, place, value):
    out[place] = value


def line_sum(produce, hooks, settle, part, out, from_left, from_right, to_right, to_left, got_left, got_right, sent_right, sent_left):
    me, count = lax.axis_index("mp"), lax.axis_size("mp")
    pieces, height, width = from_left.shape
    splits = pieces * width // part.shape[1]
    stride = (part.shape[0] - height) // (splits - 1)
    has_right, has_left = me < count - 1, me > 0

    def place(piece):
        return (
            pl.ds(pl.multiple_of(lax.rem(piece, splits) * stride, 16), height),
            pl.ds(pl.multiple_of(lax.div(piece, splits) * width, width), width),
        )

    def rightward(piece):
        return pltpu.make_async_remote_copy(
            src_ref=to_right.at[piece],
            dst_ref=from_left.at[piece],
            send_sem=sent_right.at[piece],
            recv_sem=got_left.at[piece],
            device_id={"mp": me + 1},
        )

    def leftward(piece):
        return pltpu.make_async_remote_copy(
            src_ref=to_left.at[piece],
            dst_ref=from_right.at[piece],
            send_sem=sent_left.at[piece],
            recv_sem=got_right.at[piece],
            device_id={"mp": me - 1},
        )

    def flow(piece, copy, has_source, has_target, source, target):
        @pl.when((piece >= 0) & (piece < pieces))
        def _():
            @pl.when(has_source)
            def _():
                copy(piece).wait_recv()

            @pl.when(has_target & has_source)
            def _():
                target[piece] = (part[place(piece)] + source[piece].astype(F32)).astype(BF16)

            @pl.when(has_target & jnp.logical_not(has_source))
            def _():
                target[piece] = part[place(piece)].astype(BF16)

            @pl.when(has_target & (piece >= WINDOW))
            def _():
                copy(piece - WINDOW).wait_send()

            @pl.when(has_target)
            def _():
                copy(piece).start()

    moments = pieces + HOP_LAG * (count - 1)
    right_half = lax.div(2 * me + 1, count)
    trail = HOP_LAG * (right_half * me + (1 - right_half) * (count - 1 - me))

    def step(moment, carry):
        produce(moment)
        flow(moment - HOP_LAG * me, rightward, has_left, has_right, from_left, to_right)
        flow(
            moment - HOP_LAG * (count - 1 - me), leftward, has_right, has_left, from_right, to_left
        )
        done = moment - trail
        finished = (done >= 0) & (done < pieces)

        @pl.when(finished & has_left & has_right)
        def _():
            settle(
                out,
                place(done),
                part[place(done)] + from_left[done].astype(F32) + from_right[done].astype(F32),
            )

        @pl.when(finished & jnp.logical_not(has_left))
        def _():
            settle(out, place(done), part[place(done)] + from_right[done].astype(F32))

        @pl.when(finished & jnp.logical_not(has_right))
        def _():
            settle(out, place(done), part[place(done)] + from_left[done].astype(F32))

        return carry

    def finish():
        def step(piece, carry):
            @pl.when(has_right)
            def _():
                rightward(piece).wait_send()

            @pl.when(has_left)
            def _():
                leftward(piece).wait_send()

            return carry

        lax.fori_loop(pieces - WINDOW, pieces, step, 0)

    reached = 0
    for when, hook in hooks:
        if when > reached:
            lax.fori_loop(reached, when, step, 0)
            reached = when
        hook()
    lax.fori_loop(reached, moments, step, 0)
    finish()


PRODUCT_SCRATCH = 5


def start_product(form, left, right, part, left_in, right_in, left_sem, right_sem):
    transposed, sliced = form
    blocks = right_in.shape[0]
    width = part.shape[1] // blocks
    if sliced:
        rows = left_in.shape[0]
        first = pl.multiple_of(lax.axis_index("section") * rows, 16)
        left_copy = pltpu.make_async_copy(left.at[pl.ds(first, rows), :], left_in, left_sem)
        left_copy.start()

    def right_copy(block):
        span = pl.ds(pl.multiple_of(block * width, width), width)
        view = right.at[span, :] if transposed else right.at[:, span]
        return pltpu.make_async_copy(view, right_in.at[block], right_sem.at[block])

    for block in range(blocks):
        right_copy(block).start()
    if sliced:
        left_copy.wait()

    def produce(moment):
        @pl.when((lax.rem(moment, BLOCK_STEP) == 0) & (moment < blocks * BLOCK_STEP))
        def _():
            block = lax.div(moment, BLOCK_STEP)
            right_copy(block).wait()
            contract = (((1,), (1 if transposed else 0,)), ((), ()))
            part[:, pl.ds(pl.multiple_of(block * width, width), width)] = lax.dot_general(
                (left_in if sliced else left)[...],
                right_in[block],
                contract,
                preferred_element_type=F32,
            )

    return produce


def halfway(rows):
    return rows // 32 * 16


def block_of(ref, axis, index, size, start=0, stop=None):
    if axis == 0:
        stop = size if stop is None else stop
        return ref.at[pl.ds(pl.multiple_of(index * size + start, 16), stop - start), :]
    stop = ref.shape[0] if stop is None else stop
    return ref.at[pl.ds(start, stop - start), pl.ds(pl.multiple_of(index * size, 128), size)]


def reaction_moments(travelling):
    third = travelling / LINK_BYTES_PER_US
    last = 2 * len(range(8)) + 3 * HOP_LAG - 1
    return [
        min(last, math.ceil((parts * third + 2.0 + 0.5 * parts) / MOMENT_US)) for parts in (1, 2)
    ]


def comm_kernel(plan, *refs):
    refs = list(refs)

    def take(number):
        taken = refs[:number]
        del refs[:number]
        return taken

    reduces, gathers, swaps, exchanges, shares, pairs, travelling = plan
    groups = (len(gathers), len(swaps), len(exchanges), shares, pairs)
    sources = [take(n) for n in (2 if reduces else 0,) + groups]
    others = [take(1)[0] if paired else None for _, _, paired in exchanges]
    results = [take(n) for n in (1 if reduces else 0,) + groups]
    product = take(PRODUCT_SCRATCH) if reduces else None
    line = take(8) if reduces else None
    staging = [take(4 + paired) for _, _, paired in exchanges]
    sent, got, local_sem = refs

    section, z, dp = (lax.axis_index(name) for name in ("section", "mp", "dp"))
    count_z, count_dp = lax.axis_size("mp"), lax.axis_size("dp")
    row, col = dp // 2, dp % 2
    peer_x, peer_y = row * 2 + (1 - col), (1 - row) * 2 + col
    peer_d = (1 - row) * 2 + (1 - col)
    partner, to_x, to_y = {"section": 1 - section}, {"dp": peer_x}, {"dp": peer_y}

    barrier = pltpu.get_barrier_semaphore()
    fixed = 0
    if gathers or swaps or pairs:
        pl.semaphore_signal(barrier, inc=1, device_id=partner)
        fixed += 1
    if gathers or exchanges:
        pl.semaphore_signal(barrier, inc=1, device_id=to_x)
        pl.semaphore_signal(barrier, inc=1, device_id=to_y)
        fixed += 2
    if shares:
        for step in range(1, count_z):
            pl.semaphore_signal(barrier, inc=1, device_id={"mp": (z + step) % count_z})
        fixed += count_z - 1
    elif reduces:
        for exists, neighbour in ((z > 0, z - 1), (z < count_z - 1, z + 1)):

            @pl.when(exists)
            def _(neighbour=neighbour):
                pl.semaphore_signal(barrier, inc=1, device_id={"mp": neighbour})

        at_end = (z == 0) | (z == count_z - 1)

        @pl.when(at_end)
        def _():
            pl.semaphore_wait(barrier, fixed + 1)

        @pl.when(jnp.logical_not(at_end))
        def _():
            pl.semaphore_wait(barrier, fixed + 2)

    if fixed and (shares or not reduces):
        pl.semaphore_wait(barrier, fixed)

    used = [0, 0]

    def remote(src, dst, device):
        index = used[0]
        used[0] += 1
        return pltpu.make_async_remote_copy(
            src_ref=src, dst_ref=dst, send_sem=sent.at[index], recv_sem=got.at[index], device_id=device
        )

    def within(src, dst):
        index = used[1]
        used[1] += 1
        return pltpu.make_async_copy(src, dst, local_sem.at[index])

    locals_, early, first, second = [], [], [], []
    after_one, after_two, after_three = [], [], []
    receives, loads = [], []
    starts_d, starts_xy, conclusions = [], [], []
    for item, (axis, size) in enumerate(swaps):
        src, dst = sources[2][item], results[2][item]
        copy = remote(part_of(src, axis, 1 - section, size), dst, partner)
        early.append(copy)
        receives.append(copy)
    for item in range(pairs):
        copy = remote(sources[5][item], results[5][item], partner)
        early.append(copy)
        receives.append(copy)
    for item in range(shares):
        src, dst = sources[4][item], results[4][item]
        locals_.append(within(src, dst.at[z]))
        for step in range(1, count_z):
            copy = remote(src, dst.at[z], {"mp": (z + step) % count_z})
            early.append(copy)
            receives.append(copy)
    for item, (axis, size) in enumerate(gathers):
        src, dst = sources[1][item], results[1][item]
        rows = src.shape[0]
        cut = halfway(rows)

        def shard_of(index, start=0, stop=rows, dst=dst, axis=axis, size=size):
            return block_of(dst, axis, section * count_dp + index, size, start, stop)

        upper, lower = src.at[pl.ds(0, cut), :], src.at[pl.ds(cut, rows - cut), :]
        locals_.append(within(src, shard_of(dp)))
        own = remote(src, shard_of(dp), partner)
        x_upper = remote(upper, shard_of(dp, 0, cut), to_x)
        y_lower = remote(lower, shard_of(dp, cut), to_y)
        x_lower = remote(lower, shard_of(dp, cut), to_x)
        y_upper = remote(upper, shard_of(dp, 0, cut), to_y)
        pass_y = remote(shard_of(peer_x, 0, cut), shard_of(peer_x, 0, cut), to_y)
        pass_x = remote(shard_of(peer_y, cut), shard_of(peer_y, cut), to_x)
        relay_x = remote(shard_of(peer_x), shard_of(peer_x), partner)
        relay_y = remote(shard_of(peer_y), shard_of(peer_y), partner)
        relay_upper = remote(shard_of(peer_d, 0, cut), shard_of(peer_d, 0, cut), partner)
        relay_lower = remote(shard_of(peer_d, cut), shard_of(peer_d, cut), partner)
        early.append(own)
        first += [x_upper, y_lower]
        second += [x_lower, y_upper]
        after_one += [([x_upper], None, pass_y), ([y_lower], None, pass_x)]
        after_two += [([x_lower], None, relay_x), ([y_upper], None, relay_y)]
        after_three += [([pass_y], None, relay_upper), ([pass_x], None, relay_lower)]
        receives += [own, relay_x, relay_y, relay_upper, relay_lower]
    for item, (axis, size, paired) in enumerate(exchanges):
        src, dst = sources[3][item], results[3][item]
        mine, from_x, from_y, inbound = staging[item][:4]
        rows, dtype = from_x.shape[0], from_x.dtype
        cut = halfway(rows)
        rest = rows - cut
        half = section * count_dp if paired else 0
        fetched = []
        for role, index in enumerate((peer_d, peer_x, peer_y, dp)):
            copies = [within(block_of(src, axis, half + index, size), mine.at[role])]
            if paired:
                copies.append(
                    within(block_of(others[item], axis, index, size), staging[item][4].at[role])
                )
            fetched.append(copies)
            loads += copies

        def merge(role, mine=mine, other=staging[item][-1] if paired else None):
            def run():
                if other is not None:
                    mine[role] = (mine[role].astype(F32) + other[role].astype(F32)).astype(mine.dtype)

            return run

        top, bottom = pl.ds(0, cut), pl.ds(cut, rest)
        d_upper = remote(mine.at[0, top, :], inbound.at[top, :], to_x)
        d_lower = remote(mine.at[0, bottom, :], inbound.at[bottom, :], to_y)
        x_upper = remote(mine.at[1, top, :], from_x.at[top, :], to_x)
        y_lower = remote(mine.at[2, bottom, :], from_y.at[bottom, :], to_y)
        y_upper = remote(mine.at[2, top, :], from_y.at[top, :], to_y)
        x_lower = remote(mine.at[1, bottom, :], from_x.at[bottom, :], to_x)

        def add(role, span, mine=mine, term=inbound):
            def run():
                mine[role, span, :] = (
                    mine[role, span, :].astype(F32) + term[span, :].astype(F32)
                ).astype(mine.dtype)

            return run

        def conclude(mine=mine, from_x=from_x, from_y=from_y, dst=dst):
            dst[...] = mine[3].astype(F32) + from_x[...].astype(F32) + from_y[...].astype(F32)

        starts_d += [(fetched[0], merge(0), [d_upper, d_lower])]
        starts_xy += [
            (fetched[1], merge(1), [x_upper]),
            (fetched[2], merge(2), [y_lower]),
            (fetched[3], merge(3), []),
        ]
        after_one += [
            ([d_upper], add(2, top), y_upper),
            ([d_lower], add(1, bottom), x_lower),
        ]
        receives += [x_upper, y_lower, y_upper, x_lower]
        conclusions.append(conclude)

    remotes = early + first + second

    def begin():
        for copy in loads + remotes + locals_:
            copy.start()

    def send_parts():
        for copies, compute, targets in starts_d + starts_xy:
            for copy in copies:
                copy.wait()
            compute()
            for copy in targets:
                copy.start()

    def react(items):
        def run():
            for waits, compute, copy in items:
                for wait in waits:
                    wait.wait_recv()
                if compute is not None:
                    compute()
                copy.start()

        return run

    if reduces:
        produce = start_product(reduces, *sources[0], *product)
        moments = reaction_moments(travelling)
        hooks = [(0, begin), (2, send_parts), (moments[0], react(after_one)), (moments[1], react(after_two))]
        line_sum(produce, hooks, settle_plain, product[0], results[0][0], *line)
    else:
        begin()
        send_parts()
        react(after_one)()
        react(after_two)()
    react(after_three)()
    for copy in receives:
        copy.wait_recv()
    for conclude in conclusions:
        conclude()
    started = remotes + [copy for _, _, copies in starts_d + starts_xy for copy in copies]
    started += [copy for _, _, copy in after_one + after_two + after_three]
    for copy in started:
        copy.wait_send()
    for copy in locals_:
        copy.wait()


def comm(number, reduce=None, gathers=(), swaps=(), exchanges=(), shares=(), pairs=(), name="meet"):
    count_dp, count_z = lax.axis_size("dp"), lax.axis_size("mp")
    sections = lax.axis_size("section")

    def resized(shape, axis, size):
        return shape[:axis] + (size,) + shape[axis + 1 :]

    inputs, outputs, scratch = [], [], []
    plan_gathers, plan_swaps, plan_exchanges = [], [], []
    remote_count = local_count = travelling = 0
    reduces = None
    if reduce is not None:
        left, right, transposed, sliced = reduce
        reduces = (transposed, sliced)
        rows, depth = left.shape[0] // (sections if sliced else 1), left.shape[1]
        width = right.shape[0 if transposed else 1]
        blocks = width // 256
        inputs += [left, right]
        outputs.append(jax.ShapeDtypeStruct((rows, width), F32))
        scratch += [
            pltpu.VMEM((rows, width), F32),
            pltpu.VMEM((rows, depth) if sliced else (16, 128), BF16),
            pltpu.VMEM((blocks, 256, depth) if transposed else (blocks, depth, 256), BF16),
            pltpu.SemaphoreType.DMA,
            pltpu.SemaphoreType.DMA((blocks,)),
        ]
        buffer = pltpu.VMEM((width // 64, 256, 128), BF16)
        scratch += [buffer] * 4 + [pltpu.SemaphoreType.DMA((width // 64,))] * 4
    for shard, axis in gathers:
        size = shard.shape[axis]
        inputs.append(shard)
        outputs.append(
            jax.ShapeDtypeStruct(resized(shard.shape, axis, size * sections * count_dp), shard.dtype)
        )
        plan_gathers.append((axis, size))
        travelling += shard.size * shard.dtype.itemsize
        remote_count += 11
        local_count += 1
    for array, axis in swaps:
        size = array.shape[axis] // sections
        inputs.append(array)
        outputs.append(jax.ShapeDtypeStruct(resized(array.shape, axis, size), array.dtype))
        plan_swaps.append((axis, size))
        remote_count += 1
    other_inputs = []
    for array, other, axis in exchanges:
        paired = other is not None
        size = array.shape[axis] // (count_dp * (sections if paired else 1))
        piece = resized(array.shape, axis, size)
        inputs.append(array)
        outputs.append(jax.ShapeDtypeStruct(piece, F32))
        plan_exchanges.append((axis, size, paired))
        roles, one = pltpu.VMEM((4,) + piece, array.dtype), pltpu.VMEM(piece, array.dtype)
        scratch += [roles, one, one, one]
        if paired:
            other_inputs.append(other)
            scratch.append(roles)
        travelling += piece[0] * piece[1] * array.dtype.itemsize
        remote_count += 6
        local_count += 8
    for array in shares:
        inputs.append(array)
        outputs.append(jax.ShapeDtypeStruct((count_z,) + array.shape, array.dtype))
        remote_count += count_z - 1
        local_count += 1
    for array in pairs:
        inputs.append(array)
        outputs.append(jax.ShapeDtypeStruct(array.shape, array.dtype))
        remote_count += 1
    inputs += other_inputs
    scratch += [
        pltpu.SemaphoreType.DMA((max(remote_count, 1),)),
        pltpu.SemaphoreType.DMA((max(remote_count, 1),)),
        pltpu.SemaphoreType.DMA((max(local_count, 1),)),
    ]
    plan = (reduces, tuple(plan_gathers), tuple(plan_swaps), tuple(plan_exchanges), len(shares), len(pairs), travelling)
    placed = [True] * (reduces is not None) + [False] * (len(gathers) + len(swaps))
    placed += [True] * len(exchanges) + [False] * (len(shares) + len(pairs))
    vmem, anywhere = pl.BlockSpec(memory_space=pltpu.VMEM), pl.BlockSpec(memory_space=pl.ANY)
    outs = pl.pallas_call(
        functools.partial(comm_kernel, plan),
        out_shape=outputs,
        in_specs=([] if reduces is None else [anywhere if reduces[1] else vmem])
        + [anywhere] * (len(inputs) - (0 if reduces is None else 1)),
        out_specs=[vmem if in_vmem else anywhere for in_vmem in placed],
        scratch_shapes=scratch,
        compiler_params=pltpu.CompilerParams(
            collective_id=number, has_side_effects=True, vmem_limit_bytes=48 * 2**20
        ),
        cost_estimate=pl.CostEstimate(flops=1000000, bytes_accessed=90000000, transcendentals=0),
        name=name,
    )(*inputs)
    outs = list(outs)
    split = []
    for number_of in (1 if reduces else 0, len(gathers), len(swaps), len(exchanges), len(shares), len(pairs)):
        split.append(outs[:number_of])
        outs = outs[number_of:]
    return split


def spread(remote, src, dst, axis, size, section, dp, peers, partner, to_x, to_y):
    count_dp = lax.axis_size("dp")
    rows = src.shape[0]
    cut = halfway(rows)
    peer_x, peer_y, peer_d = peers

    def shard_of(index, start=0, stop=rows):
        return block_of(dst, axis, section * count_dp + index, size, start, stop)

    def still(*place):
        return (shard_of(*place), shard_of(*place))

    upper, lower = src.at[pl.ds(0, cut), :], src.at[pl.ds(cut, rows - cut), :]
    return {
        "own": remote(src, shard_of(dp), partner),
        "x_upper": remote(upper, shard_of(dp, 0, cut), to_x),
        "y_lower": remote(lower, shard_of(dp, cut), to_y),
        "x_lower": remote(lower, shard_of(dp, cut), to_x),
        "y_upper": remote(upper, shard_of(dp, 0, cut), to_y),
        "pass_y": remote(*still(peer_x, 0, cut), to_y),
        "pass_x": remote(*still(peer_y, cut), to_x),
        "relay_x": remote(*still(peer_x), partner),
        "relay_y": remote(*still(peer_y), partner),
        "relay_upper": remote(*still(peer_d, 0, cut), partner),
        "relay_lower": remote(*still(peer_d, cut), partner),
    }


def spread_steps(copies):
    def begin():
        for name in ("own", "x_upper", "y_lower", "x_lower", "y_upper"):
            copies[name].start()

    def follow(pairs):
        def run():
            for arrived, onward in pairs:
                copies[arrived].wait_recv()
                copies[onward].start()

        return run

    one = follow((("x_upper", "pass_y"), ("y_lower", "pass_x")))
    two = follow((("x_lower", "relay_x"), ("y_upper", "relay_y")))
    three = follow((("pass_y", "relay_upper"), ("pass_x", "relay_lower")))
    return begin, one, two, three


def head_kernel(plan, *refs):
    refs = list(refs)

    def take(number):
        taken = refs[:number]
        del refs[:number]
        return taken

    count = len(plan)
    places, frequency, expression, embed = take(4)
    shards = take(count)
    start, embed_all = take(2)
    gathered = take(count)
    part, codes, cells_in, columns_in, cells_sem, columns_sem = take(6)
    held = take(count)
    line = take(8)
    sent, got, local_sem = refs

    section, z, dp = (lax.axis_index(name) for name in ("section", "mp", "dp"))
    count_z, count_dp = lax.axis_size("mp"), lax.axis_size("dp")
    row, col = dp // 2, dp % 2
    peer_x, peer_y = row * 2 + (1 - col), (1 - row) * 2 + col
    peer_d = (1 - row) * 2 + (1 - col)
    peers = (peer_x, peer_y, peer_d)
    partner, to_x, to_y = {"section": 1 - section}, {"dp": peer_x}, {"dp": peer_y}
    rows, width = cells_in.shape[0], embed.shape[1]

    barrier = pltpu.get_barrier_semaphore()
    for device in (partner, to_x, to_y):
        pl.semaphore_signal(barrier, inc=1, device_id=device)
    for exists, neighbour in ((z > 0, z - 1), (z < count_z - 1, z + 1)):

        @pl.when(exists)
        def _(neighbour=neighbour):
            pl.semaphore_signal(barrier, inc=1, device_id={"mp": neighbour})

    at_end = (z == 0) | (z == count_z - 1)

    @pl.when(at_end)
    def _():
        pl.semaphore_wait(barrier, 4)

    @pl.when(jnp.logical_not(at_end))
    def _():
        pl.semaphore_wait(barrier, 5)

    used = [0, 0]

    def remote(src, dst, device):
        index = used[0]
        used[0] += 1
        return pltpu.make_async_remote_copy(
            src_ref=src, dst_ref=dst, send_sem=sent.at[index], recv_sem=got.at[index], device_id=device
        )

    def within(src, dst):
        index = used[1]
        used[1] += 1
        return pltpu.make_async_copy(src, dst, local_sem.at[index])

    place = (section, dp, peers, partner, to_x, to_y)
    main = spread(remote, embed, embed_all, 1, width, *place)
    begin, one, two, three = spread_steps(main)
    rest = [
        spread(remote, src, dst, axis, size, *place)
        for src, dst, (axis, size) in zip(shards, gathered, plan)
    ]
    rest_steps = [spread_steps(copies) for copies in rest]
    loads = [within(src, room) for src, room in zip(shards, held)]
    kept = [within(columns_in.at[0], block_of(embed_all, 1, section * count_dp + dp, width))]
    kept += [
        within(room, block_of(dst, axis, section * count_dp + dp, size))
        for room, dst, (axis, size) in zip(held, gathered, plan)
    ]

    order = [
        section * count_dp + dp,
        (1 - section) * count_dp + dp,
        section * count_dp + peer_x,
        section * count_dp + peer_y,
        (1 - section) * count_dp + peer_x,
        (1 - section) * count_dp + peer_y,
        section * count_dp + peer_d,
        (1 - section) * count_dp + peer_d,
    ]

    first = pl.multiple_of(section * rows, 16)
    cells_copy = pltpu.make_async_copy(expression.at[pl.ds(first, rows), :], cells_in, cells_sem)

    def fetch(turn):
        src = embed if turn == 0 else block_of(embed_all, 1, order[turn], width)
        return pltpu.make_async_copy(src, columns_in.at[turn], columns_sem.at[turn])

    begin()
    cells_copy.start()
    fetch(0).start()
    for copy in loads:
        copy.start()

    quarter = frequency.shape[1]
    for axis in range(2):
        along = places[:, axis : axis + 1] * frequency[...]
        codes[:, 2 * axis * quarter : (2 * axis + 1) * quarter] = jnp.sin(along)
        codes[:, (2 * axis + 1) * quarter : (2 * axis + 2) * quarter] = jnp.cos(along)
    cells_copy.wait()

    def keep():
        for copy in loads:
            copy.wait()
        for copy in kept:
            copy.start()

    def produce(moment):
        turn = lax.div(moment, 2)

        @pl.when((lax.rem(moment, 2) == 0) & (turn < len(order)))
        def _():
            pltpu.make_async_copy(embed, columns_in.at[turn], columns_sem.at[turn]).wait()
            part[:, pl.ds(pl.multiple_of(turn * width, width), width)] = mat_nn(
                cells_in[...], columns_in[turn]
            )

    def settle(out, where, value):
        span, columns = where
        turn = lax.div(columns.start, width)
        block = sum(jnp.where(turn == index, target, 0) for index, target in enumerate(order))
        columns = pl.ds(pl.multiple_of(block * width, width), width)
        out[span, columns] = value + codes[span, columns]

    def arrived(names, turns):
        def run():
            for name in names:
                main[name].wait_recv()
            for turn in turns:
                fetch(turn).start()

        return run

    def neighbours():
        one()
        for steps in rest_steps:
            steps[0]()
        two()
        for turn in (2, 3):
            fetch(turn).start()

    def diagonal():
        three()
        fetch(6).start()

    def later(number):
        def run():
            for steps in rest_steps:
                steps[number]()

        return run

    hooks = [
        (1, keep),
        (2, arrived(("own",), (1,))),
        (4, neighbours),
        (8, arrived(("relay_x", "relay_y"), (4, 5))),
        (12, diagonal),
        (14, arrived(("relay_upper", "relay_lower"), (7,))),
        (17, later(1)),
        (21, later(2)),
    ]
    line_sum(produce, hooks, settle, part, start, *line)
    for steps in rest_steps:
        steps[3]()
    for copies in rest:
        for name in ("own", "relay_x", "relay_y", "relay_upper", "relay_lower"):
            copies[name].wait_recv()
    for copies in [main] + rest:
        for copy in copies.values():
            copy.wait_send()
    for copy in kept:
        copy.wait()


def head(number, places, expression, embed, gathers):
    sections, count_dp = lax.axis_size("section"), lax.axis_size("dp")
    rows, genes = places.shape[0], expression.shape[1]
    width = embed.shape[1]
    total_parts = sections * count_dp
    features = total_parts * width
    quarter = features // 4
    frequency = jnp.exp(jnp.arange(quarter, dtype=F32) * (-math.log(10000.0) / quarter))[None, :]
    vmem, anywhere = pl.BlockSpec(memory_space=pltpu.VMEM), pl.BlockSpec(memory_space=pl.ANY)
    plan = tuple((axis, shard.shape[axis]) for shard, axis in gathers)
    shapes = [
        shard.shape[:axis] + (shard.shape[axis] * total_parts,) + shard.shape[axis + 1 :]
        for shard, axis in gathers
    ]
    pieces = features // 64
    buffer = pltpu.VMEM((pieces, 256, 128), BF16)
    copies = 11 * (1 + len(gathers))
    results = pl.pallas_call(
        functools.partial(head_kernel, plan),
        out_shape=[
            jax.ShapeDtypeStruct((rows, features), F32),
            jax.ShapeDtypeStruct((genes, features), BF16),
        ]
        + [jax.ShapeDtypeStruct(shape, shard.dtype) for shape, (shard, _) in zip(shapes, gathers)],
        in_specs=[vmem] * 2 + [anywhere] * (2 + len(gathers)),
        out_specs=[vmem] + [anywhere] * (1 + len(gathers)),
        scratch_shapes=[
            pltpu.VMEM((rows, features), F32),
            pltpu.VMEM((rows, features), F32),
            pltpu.VMEM((rows, genes), BF16),
            pltpu.VMEM((total_parts, genes, width), BF16),
            pltpu.SemaphoreType.DMA,
            pltpu.SemaphoreType.DMA((total_parts,)),
        ]
        + [pltpu.VMEM(shard.shape, shard.dtype) for shard, _ in gathers]
        + [buffer] * 4
        + [pltpu.SemaphoreType.DMA((pieces,))] * 4
        + [
            pltpu.SemaphoreType.DMA((copies,)),
            pltpu.SemaphoreType.DMA((copies,)),
            pltpu.SemaphoreType.DMA((1 + 2 * len(gathers),)),
        ],
        compiler_params=pltpu.CompilerParams(
            collective_id=number, has_side_effects=True, vmem_limit_bytes=48 * 2**20
        ),
        name="head",
    )(places, frequency, expression, embed, *[shard for shard, _ in gathers])
    return results[0], results[1], results[2:]


def trade(remote, mine, indices, from_x, from_y, inbound, to_x, to_y):
    rows = from_x.shape[0]
    cut = halfway(rows)
    top, bottom = pl.ds(0, cut), pl.ds(cut, rows - cut)
    d, x, y, own = indices
    d_upper = remote(mine.at[d, top, :], inbound.at[top, :], to_x)
    d_lower = remote(mine.at[d, bottom, :], inbound.at[bottom, :], to_y)
    x_upper = remote(mine.at[x, top, :], from_x.at[top, :], to_x)
    y_lower = remote(mine.at[y, bottom, :], from_y.at[bottom, :], to_y)
    y_upper = remote(mine.at[y, top, :], from_y.at[top, :], to_y)
    x_lower = remote(mine.at[x, bottom, :], from_x.at[bottom, :], to_x)

    def pass_on():
        for copy, index, span, onward in (
            (d_upper, y, top, y_upper),
            (d_lower, x, bottom, x_lower),
        ):
            copy.wait_recv()
            mine[index, span, :] = (
                mine[index, span, :].astype(F32) + inbound[span, :].astype(F32)
            ).astype(mine.dtype)
            onward.start()

    def conclude():
        for copy in (x_upper, y_lower, y_upper, x_lower):
            copy.wait_recv()
        for copy in (d_upper, d_lower, x_upper, y_lower, y_upper, x_lower):
            copy.wait_send()
        return mine[own].astype(F32) + from_x[...].astype(F32) + from_y[...].astype(F32)

    return (d_upper, d_lower), (x_upper, y_lower), pass_on, conclude


def tail_kernel(
    start, expression, embed, grad_rebuilt, qkv, out, small, qkv_other, out_other,
    embed_sum, qkv_sum, out_sum, small_sum, cells_own, cells_other,
    start_other, start_turned, x_own, x_other, embed_in, cells, embed_parts, embed_x, embed_y, embed_in_d,
    qkv_parts, qkv_x, qkv_y, qkv_in_d, qkv_partner, out_parts, out_x, out_y, out_in_d, out_partner,
    small_parts, small_x, small_y, small_in_d, small_partner, sent, got, local_sem,
):
    section, dp = lax.axis_index("section"), lax.axis_index("dp")
    count_dp = lax.axis_size("dp")
    row, col = dp // 2, dp % 2
    peer_x, peer_y = row * 2 + (1 - col), (1 - row) * 2 + col
    peer_d = (1 - row) * 2 + (1 - col)
    partner, to_x, to_y = {"section": 1 - section}, {"dp": peer_x}, {"dp": peer_y}
    rows, genes = cells.shape
    half = start_other.shape[1]
    width = half // count_dp

    barrier = pltpu.get_barrier_semaphore()
    for device in (partner, to_x, to_y):
        pl.semaphore_signal(barrier, inc=1, device_id=device)
    pl.semaphore_wait(barrier, 3)

    used = [0, 0]

    def remote(src, dst, device):
        index = used[0]
        used[0] += 1
        return pltpu.make_async_remote_copy(
            src_ref=src, dst_ref=dst, send_sem=sent.at[index], recv_sem=got.at[index], device_id=device
        )

    def within(src, dst):
        index = used[1]
        used[1] += 1
        return pltpu.make_async_copy(src, dst, local_sem.at[index])

    def half_of(index):
        return pl.ds(pl.multiple_of(index * half, 128), half)

    def rows_of(index):
        return pl.ds(pl.multiple_of(index * rows, 16), rows)

    swaps = [
        remote(start.at[:, half_of(1 - section)], start_other, partner),
        remote(small.at[1 - section], small_partner, partner),
    ]
    for copy in swaps:
        copy.start()
    roles = (peer_d, peer_x, peer_y, dp)
    fetches = []
    for src, other, axis, parts, parts_other in (
        (qkv, qkv_other, 0, qkv_parts, qkv_partner),
        (out, out_other, 1, out_parts, out_partner),
    ):
        size = src.shape[axis] // (2 * count_dp)
        for role, index in enumerate(roles):
            fetches.append(
                within(block_of(src, axis, section * count_dp + index, size), parts.at[role])
            )
            fetches.append(within(block_of(other, axis, index, size), parts_other.at[role]))
    fetches.append(within(small.at[section], small_parts))
    load_own = within(expression.at[rows_of(section), :], x_own)
    load_other = within(expression.at[rows_of(1 - section), :], x_other)
    load_embed = within(embed, embed_in)
    load_cells = within(grad_rebuilt, cells)
    for copy in fetches + [load_own, load_other, load_embed, load_cells]:
        copy.start()

    trades = [
        trade(remote, parts, indices, *buffers, to_x, to_y)
        for parts, indices, buffers in (
            (qkv_parts, (0, 1, 2, 3), (qkv_x, qkv_y, qkv_in_d)),
            (out_parts, (0, 1, 2, 3), (out_x, out_y, out_in_d)),
            (small_parts, roles, (small_x, small_y, small_in_d)),
            (embed_parts, roles, (embed_x, embed_y, embed_in_d)),
        )
    ]

    for copy in fetches:
        copy.wait()
    swaps[1].wait_recv()
    for parts, other in (
        (qkv_parts, qkv_partner),
        (out_parts, out_partner),
        (small_parts, small_partner),
    ):
        parts[...] = (parts[...].astype(F32) + other[...].astype(F32)).astype(parts.dtype)
    for first, second, _, _ in trades[:3]:
        for copy in first + second:
            copy.start()

    load_own.wait()
    load_other.wait()
    swaps[0].wait_recv()
    start_turned[0] = start[:, half_of(section)].T
    start_turned[1] = start_other[...].T

    def embed_tile(span, size):
        tile = mat_nn(start_turned[0], x_own[:, span]) + mat_nn(start_turned[1], x_other[:, span])
        embed_parts[:, :, span] = tile.reshape(count_dp, width, size).astype(BF16)

    whole = genes // TILE

    def embed_step(index, carry):
        embed_tile(pl.ds(pl.multiple_of(index * TILE, TILE), TILE), TILE)
        return carry

    lax.fori_loop(0, whole, embed_step, 0)
    if genes % TILE:
        embed_tile(pl.ds(whole * TILE, genes % TILE), genes % TILE)
    for copy in trades[3][0] + trades[3][1]:
        copy.start()

    load_embed.wait()
    load_cells.wait()

    def cells_tile(span):
        tile = mat_nt(start[...], embed_in[span, :]).astype(BF16)
        cells[:, span] = (tile.astype(F32) - cells[:, span].astype(F32)).astype(BF16)

    def cells_step(index, carry):
        cells_tile(pl.ds(pl.multiple_of(index * TILE, TILE), TILE))
        return carry

    lax.fori_loop(0, whole, cells_step, 0)
    if genes % TILE:
        cells_tile(pl.ds(whole * TILE, genes % TILE))
    give = remote(cells, cells_other, partner)
    give.start()
    keep = within(cells, cells_own)
    keep.start()

    for _, _, pass_on, _ in trades:
        pass_on()
    qkv_sum[...] = trades[0][3]()
    out_sum[...] = trades[1][3]()
    small_sum[...] = trades[2][3]()
    embed_sum[...] = trades[3][3]().T
    for copy in swaps:
        copy.wait_send()
    give.wait()
    keep.wait()


def assemble_kernel(own, other, whole, held, arrived, left):
    section = lax.axis_index("section")
    rows = own.shape[0]
    spans = [(start, min(128, rows - start)) for start in range(0, rows, 128)]
    loads, stores = [], []
    for place, (src, index) in enumerate(((own, section), (other, 1 - section))):
        for part, (start, size) in enumerate(spans):
            span = pl.ds(start, size)
            target = pl.ds(pl.multiple_of(index * rows + start, 16), size)
            number = place * len(spans) + part
            loads.append(
                pltpu.make_async_copy(src.at[span, :], held.at[place, span, :], arrived.at[number])
            )
            stores.append(
                pltpu.make_async_copy(held.at[place, span, :], whole.at[target, :], left.at[number])
            )
    for load in loads:
        load.start()
    for load, store in zip(loads, stores):
        load.wait()
        store.start()
    for store in stores:
        store.wait()


def tail(number, start, expression, embed, grad_rebuilt, qkv, qkv_other, out, out_other, small):
    rows, features = start.shape
    genes, count_dp = embed.shape[0], lax.axis_size("dp")
    half = features // 2
    width = half // count_dp
    vmem, anywhere = pl.BlockSpec(memory_space=pltpu.VMEM), pl.BlockSpec(memory_space=pl.ANY)

    def buffers(shape, dtype, paired):
        parts, one = pltpu.VMEM((count_dp,) + shape, dtype), pltpu.VMEM(shape, dtype)
        return [parts, one, one, one] + ([parts] if paired else [])

    qkv_piece = (qkv.shape[0] // (2 * count_dp), qkv.shape[1])
    out_piece = (out.shape[0], out.shape[1] // (2 * count_dp))
    small_piece = small.shape[2:]
    cells = jax.ShapeDtypeStruct((rows, genes), BF16)
    results = pl.pallas_call(
        tail_kernel,
        out_shape=[
            jax.ShapeDtypeStruct((genes, width), F32),
            jax.ShapeDtypeStruct(qkv_piece, F32),
            jax.ShapeDtypeStruct(out_piece, F32),
            jax.ShapeDtypeStruct(small_piece, F32),
            cells,
            cells,
        ],
        in_specs=[vmem] + [anywhere] * 8,
        out_specs=[vmem] * 4 + [anywhere] * 2,
        scratch_shapes=[
            pltpu.VMEM((rows, half), BF16),
            pltpu.VMEM((2, half, rows), BF16),
            pltpu.VMEM((rows, genes), BF16),
            pltpu.VMEM((rows, genes), BF16),
            pltpu.VMEM((genes, features), BF16),
            pltpu.VMEM((rows, genes), BF16),
        ]
        + buffers((width, genes), BF16, False)
        + buffers(qkv_piece, BF16, True)
        + buffers(out_piece, BF16, True)
        + buffers(small_piece, F32, True)
        + [
            pltpu.SemaphoreType.DMA((27,)),
            pltpu.SemaphoreType.DMA((27,)),
            pltpu.SemaphoreType.DMA((22,)),
        ],
        compiler_params=pltpu.CompilerParams(
            collective_id=number, has_side_effects=True, vmem_limit_bytes=62 * 2**20
        ),
        name="tail",
    )(start, expression, embed, grad_rebuilt, qkv, out, small, qkv_other, out_other)
    whole = pl.pallas_call(
        assemble_kernel,
        out_shape=jax.ShapeDtypeStruct((2 * rows, genes), BF16),
        in_specs=[anywhere] * 2,
        out_specs=anywhere,
        scratch_shapes=[pltpu.VMEM((2, rows, genes), BF16)]
        + [pltpu.SemaphoreType.DMA((2 * (-(-rows // 128)),))] * 2,
        compiler_params=pltpu.CompilerParams(vmem_limit_bytes=62 * 2**20),
        name="assemble",
    )(results[4], results[5])
    return list(results[:4]) + [whole]


def line_pipe(produce, hooks, items, spacing, part, total, from_left, from_right, to_right, to_left, got_left, got_right, sent_right, sent_left):
    me, count = lax.axis_index("mp"), lax.axis_size("mp")
    columns = from_left.shape[2]
    pieces = part.shape[2] // columns
    has_right, has_left = me < count - 1, me > 0

    def place(slot):
        first = pl.multiple_of(lax.rem(slot, spacing) * columns, columns)
        return (lax.rem(lax.div(slot, spacing), PARTS), slice(None), pl.ds(first, columns))

    rooms = from_left.shape[0]

    def room_of(slot):
        return lax.rem(slot, rooms)

    def rightward(slot):
        room = room_of(slot)
        return pltpu.make_async_remote_copy(
            src_ref=to_right.at[room],
            dst_ref=from_left.at[room],
            send_sem=sent_right.at[room],
            recv_sem=got_left.at[room],
            device_id={"mp": me + 1},
        )

    def leftward(slot):
        room = room_of(slot)
        return pltpu.make_async_remote_copy(
            src_ref=to_left.at[room],
            dst_ref=from_right.at[room],
            send_sem=sent_left.at[room],
            recv_sem=got_right.at[room],
            device_id={"mp": me - 1},
        )

    def used(slot):
        return (slot >= 0) & (slot < items * spacing) & (lax.rem(slot, spacing) < pieces)

    def flow(slot, copy, has_source, has_target, source, target):
        @pl.when(used(slot))
        def _():
            room = room_of(slot)

            @pl.when(has_source)
            def _():
                copy(slot).wait_recv()

            @pl.when(has_target & (slot >= rooms))
            def _():
                copy(slot).wait_send()

            @pl.when(has_target & has_source)
            def _():
                target[room] = (part[place(slot)] + source[room].astype(F32)).astype(BF16)

            @pl.when(has_target & jnp.logical_not(has_source))
            def _():
                target[room] = part[place(slot)].astype(BF16)

            @pl.when(has_target)
            def _():
                copy(slot).start()

    right_half = lax.div(2 * me + 1, count)
    trail = HOP_LAG * (right_half * me + (1 - right_half) * (count - 1 - me))

    def step(moment, carry):
        for when, hook in hooks:
            pl.when(moment == when)(hook)
        produce(moment)
        flow(moment - HOP_LAG * me, rightward, has_left, has_right, from_left, to_right)
        flow(
            moment - HOP_LAG * (count - 1 - me), leftward, has_right, has_left, from_right, to_left
        )
        done = moment - trail

        room = room_of(done)

        @pl.when(used(done) & has_left & has_right)
        def _():
            total[place(done)] = (
                part[place(done)] + from_left[room].astype(F32) + from_right[room].astype(F32)
            )

        @pl.when(used(done) & jnp.logical_not(has_left))
        def _():
            total[place(done)] = part[place(done)] + from_right[room].astype(F32)

        @pl.when(used(done) & jnp.logical_not(has_right))
        def _():
            total[place(done)] = part[place(done)] + from_left[room].astype(F32)

        return carry

    lax.fori_loop(0, (items + PARTS - 1) * spacing, step, 0)

    def finish(slot, carry):
        @pl.when(used(slot) & has_right)
        def _():
            rightward(slot).wait_send()

        @pl.when(used(slot) & has_left)
        def _():
            leftward(slot).wait_send()

        return carry

    lax.fori_loop(items * spacing - rooms, items * spacing, finish, 0)


def pipe_spacing(pieces, count):
    return max(pieces, (pieces - 1 + HOP_LAG * (count - 1)) // PARTS + 1)


def part_rows(part, cells):
    last = lax.div(part, PARTS - 1) * (PARTS * PART_ROWS - cells)
    return pl.ds(pl.multiple_of(part * PART_ROWS - last, 16), PART_ROWS)


def middle_kernel(
    plan, spacing, start, gain_one, bias_one, qkv_w, info, gain, bias, out_w, noise,
    centers, spreads, *refs
):
    refs = list(refs)

    def take(number):
        taken = refs[:number]
        del refs[:number]
        return taken

    count = len(plan)
    shards = take(count)
    (normed_out, scale_out, second_out, upper_out, active_out, hidden_out, log_vars_out,
     latent_out, spread_out, latent_low_out, decoder_out, density_all) = take(12)
    gathered = take(count)
    attend_outs = take(6)
    attended = attend_outs[4]
    part, total, kept_rows, density = take(4)
    up_in, down_in, latent_in, dec_in = take(4)
    held = take(count)
    line = take(8)
    sent, got, local_sem = refs

    section, z, dp = (lax.axis_index(name) for name in ("section", "mp", "dp"))
    count_z, count_dp = lax.axis_size("mp"), lax.axis_size("dp")
    row, col = dp // 2, dp % 2
    peer_x, peer_y = row * 2 + (1 - col), (1 - row) * 2 + col
    peers = (peer_x, peer_y, (1 - row) * 2 + (1 - col))
    partner, to_x, to_y = {"section": 1 - section}, {"dp": peer_x}, {"dp": peer_y}
    cells, latents = noise.shape
    half_rows = part.shape[1]
    comp_count = centers.shape[0]

    barrier = pltpu.get_barrier_semaphore()
    for device in (partner, to_x, to_y):
        pl.semaphore_signal(barrier, inc=1, device_id=device)
    for step in range(1, count_z):
        pl.semaphore_signal(barrier, inc=1, device_id={"mp": (z + step) % count_z})
    pl.semaphore_wait(barrier, 3 + count_z - 1)

    used = [0, 0]

    def remote(src, dst, device):
        index = used[0]
        used[0] += 1
        return pltpu.make_async_remote_copy(
            src_ref=src, dst_ref=dst, send_sem=sent.at[index], recv_sem=got.at[index], device_id=device
        )

    def within(src, dst):
        index = used[1]
        used[1] += 1
        return pltpu.make_async_copy(src, dst, local_sem.at[index])

    around = (section, dp, peers, partner, to_x, to_y)
    spreads_of = [
        spread(remote, src, dst, axis, size, *around)
        for src, dst, (axis, size) in zip(shards, gathered, plan)
    ]
    steps_of = [spread_steps(copies) for copies in spreads_of]
    loads = [within(src, room) for src, room in zip(shards, held)]
    keeps = [
        within(room, block_of(dst, axis, section * count_dp + dp, size))
        for room, dst, (axis, size) in zip(held, gathered, plan)
    ]
    fetches = [
        within(src, dst) for src, dst in zip(gathered, (up_in, down_in, latent_in, dec_in))
    ]
    density_sends = [
        remote(density, density_all.at[z], {"mp": (z + step) % count_z})
        for step in range(1, count_z)
    ]
    density_keep = within(density, density_all.at[z])

    def run_steps(items, number):
        def run():
            for item in items:
                steps_of[item][number]()

        return run

    def keep():
        for load in loads:
            load.wait()
        for copy in keeps:
            copy.start()

    near, mid, far = [0, 1], [2, 3], [4]

    def fetch(items):
        def run():
            for item in items:
                for name in ("own", "relay_x", "relay_y", "relay_upper", "relay_lower"):
                    spreads_of[item][name].wait_recv()
                keeps[item].wait()
                fetches[item].start()
            for item in items:
                fetches[item].wait()

        return run

    def share():
        for copy in density_sends + [density_keep]:
            copy.start()

    for load in loads:
        load.start()
    run_steps(near, 0)()
    attend_kernel(start, gain_one, bias_one, qkv_w, info, *attend_outs)

    def rows_of(half):
        return part_rows(half, cells)

    def out_product(half):
        part[half] = mat_nn(attended[rows_of(half), :], out_w[...])

    def feed_forward(half):
        rows = rows_of(half)
        values = start[rows, :] + total[half]
        kept_rows[half] = values
        normed, scale = normalize(values)
        second = (normed * gain[...] + bias[...]).astype(BF16)
        upper = mat_nn(second, up_in[...])
        active = gelu(upper).astype(BF16)
        part[half] = mat_nn(active, down_in[...])
        normed_out[rows, :] = normed
        scale_out[rows, :] = scale
        second_out[rows, :] = second
        upper_out[rows, :] = upper
        active_out[rows, :] = active

    def latents_of(half):
        rows = rows_of(half)
        hidden = (kept_rows[half] + total[half]).astype(BF16)
        hidden_out[rows, :] = hidden
        stats = mat_nn(hidden, latent_in[...])
        means, log_vars = stats[:, :latents], stats[:, latents:]
        own_noise = noise[rows, :]
        scaled = jnp.exp(0.5 * log_vars) * own_noise
        latent = means + scaled
        low = latent.astype(BF16)
        part[half] = mat_nn(low, dec_in[...])
        log_vars_out[rows, :] = log_vars
        spread_out[rows, :] = scaled
        latent_out[rows, :] = latent
        latent_low_out[rows, :] = low
        lane = lax.broadcasted_iota(jnp.int32, (half_rows, 128), 1)
        columns = jnp.sum(
            -0.5 * LOG_TWO_PI - 0.5 * log_vars - 0.5 * own_noise * own_noise, axis=1, keepdims=True
        )
        table = jnp.where(lane == comp_count, columns, 0.0)
        for index in range(comp_count):
            log_spread = spreads[index : index + 1, :]
            offset = latent - centers[index : index + 1, :]
            columns = jnp.sum(
                -0.5 * LOG_TWO_PI - 0.5 * log_spread - 0.5 * offset * offset * jnp.exp(-log_spread),
                axis=1,
                keepdims=True,
            )
            table = jnp.where(lane == index, columns, table)
        density[:, pl.ds(pl.multiple_of(half * half_rows, 128), half_rows)] = table.T[
            : density.shape[0], :
        ]

    def conclude(half):
        decoder_out[rows_of(half), :] = total[half]

    def produce(moment):
        item = lax.div(moment, spacing)
        half, stage = lax.rem(item, PARTS), lax.div(item, PARTS)
        begins = lax.rem(moment, spacing) == 0
        for number, work in enumerate((out_product, feed_forward, latents_of, conclude)):
            pl.when(begins & (stage == number))(functools.partial(work, half))

    hooks = [
        (1, keep),
        (3, run_steps(near, 1)),
        (7, run_steps(near, 2)),
        (11, run_steps(near, 3)),
        (12, run_steps(mid + far, 0)),
        (PARTS * spacing, fetch(near)),
        (PARTS * spacing + 3, run_steps(mid, 1)),
        (PARTS * spacing + 5, run_steps(mid, 2)),
        (PARTS * spacing + 7, run_steps(mid, 3)),
        (PARTS * spacing + 10, run_steps(far, 1)),
        (2 * PARTS * spacing - 1, fetch(mid)),
        (2 * PARTS * spacing + 2, run_steps(far, 2)),
        (2 * PARTS * spacing + 10, run_steps(far, 3)),
        (3 * PARTS * spacing - spacing + 1, share),
    ]
    line_pipe(produce, hooks, 3 * PARTS, spacing, part, total, *line)
    conclude(PARTS - 1)
    for item in far:
        for name in ("own", "relay_x", "relay_y", "relay_upper", "relay_lower"):
            spreads_of[item][name].wait_recv()
        keeps[item].wait()
    for copies in spreads_of:
        for copy in copies.values():
            copy.wait_send()
    for copy in density_sends:
        copy.wait()
    density_keep.wait()


def middle(number, start, norm_one, qkv_w, info, gain, bias, out_w, noise, centers, spreads, gathers):
    sections, count_dp, count_z = (lax.axis_size(name) for name in ("section", "dp", "mp"))
    cells, features = start.shape
    latents = noise.shape[1]
    total_parts = sections * count_dp
    spacing = pipe_spacing(features // PIECE_COLUMNS, count_z)
    plan = tuple((axis, shard.shape[axis]) for shard, axis in gathers)
    shapes = [
        shard.shape[:axis] + (shard.shape[axis] * total_parts,) + shard.shape[axis + 1 :]
        for shard, axis in gathers
    ]
    units = shapes[0][1]
    vmem, anywhere = pl.BlockSpec(memory_space=pltpu.VMEM), pl.BlockSpec(memory_space=pl.ANY)
    outputs = [
        ((cells, features), F32),
        ((cells, 1), F32),
        ((cells, features), BF16),
        ((cells, units), F32),
        ((cells, units), BF16),
        ((cells, features), BF16),
        ((cells, latents), F32),
        ((cells, latents), F32),
        ((cells, latents), F32),
        ((cells, latents), BF16),
        ((cells, features), F32),
        ((count_z, 24, PARTS * PART_ROWS), F32),
    ] + [(shape, BF16) for shape in shapes]
    width = qkv_w.shape[1] // 3
    outputs += [
        ((cells, features), F32),
        ((cells, 1), F32),
        ((cells, features), BF16),
        ((cells, 3 * width), BF16),
        ((cells, width), BF16),
        ((width // HEAD, cells), F32),
    ]
    rooms = PARTS * spacing
    buffer = pltpu.VMEM((rooms, PART_ROWS, PIECE_COLUMNS), BF16)
    copies = 11 * len(gathers) + count_z - 1
    halves = pltpu.VMEM((PARTS, PART_ROWS, features), F32)
    results = pl.pallas_call(
        functools.partial(middle_kernel, plan, spacing),
        out_shape=[jax.ShapeDtypeStruct(*item) for item in outputs],
        in_specs=[vmem] * 11 + [anywhere] * len(gathers),
        out_specs=[vmem] * 11 + [anywhere] * (1 + len(gathers)) + [vmem] * 6,
        scratch_shapes=[halves, halves, halves, pltpu.VMEM((24, PARTS * PART_ROWS), F32)]
        + [pltpu.VMEM(shape, BF16) for shape in shapes[:-1]]
        + [pltpu.VMEM(shard.shape, BF16) for shard, _ in gathers]
        + [buffer] * 4
        + [pltpu.SemaphoreType.DMA((rooms,))] * 4
        + [
            pltpu.SemaphoreType.DMA((copies,)),
            pltpu.SemaphoreType.DMA((copies,)),
            pltpu.SemaphoreType.DMA((3 * len(gathers),)),
        ],
        compiler_params=pltpu.CompilerParams(
            collective_id=number, has_side_effects=True, vmem_limit_bytes=62 * 2**20
        ),
        name="middle",
    )(
        start, *norm_one, qkv_w, info, gain, bias, out_w, noise, centers,
        spreads, *[shard for shard, _ in gathers],
    )
    return results[:12], results[12:-6], results[-6:]


def back_kernel(
    spacing, latent_total, ramp_step, density_parts, info, latent, spread_latent, centers,
    spreads, upper, scale, gain, decoder_pre, normed, genes_w, dec_w, latent_w, down_w, up_w, expression,
    pre_out, stats_out, comps_out, hidden_out, upper_out, middle_out, low_out, sums_out,
    genes_sum, rebuilt_out, part, total, wide, counts, respons, info_columns, counts_all, kl_scale, genes_in, dec_in, latent_in, down_in,
    up_in, cells_in, residual, act_turned, grad, cells_sem, free, *refs
):
    line, (sent, got, local_sem) = refs[:8], refs[8:]
    section, z, dp = (lax.axis_index(name) for name in ("section", "mp", "dp"))
    count_z, count_dp = lax.axis_size("mp"), lax.axis_size("dp")
    row, col = dp // 2, dp % 2
    peer_x, peer_y = row * 2 + (1 - col), (1 - row) * 2 + col
    peers = (peer_x, peer_y, (1 - row) * 2 + (1 - col))
    partner, to_x, to_y = {"section": 1 - section}, {"dp": peer_x}, {"dp": peer_y}
    cells = upper.shape[0]
    half_rows = part.shape[1]
    comp_count = centers.shape[0]

    barrier = pltpu.get_barrier_semaphore()
    for device in (partner, to_x, to_y):
        pl.semaphore_signal(barrier, inc=1, device_id=device)
    for exists, neighbour in ((z > 0, z - 1), (z < count_z - 1, z + 1)):

        @pl.when(exists)
        def _(neighbour=neighbour):
            pl.semaphore_signal(barrier, inc=1, device_id={"mp": neighbour})

    at_end = (z == 0) | (z == count_z - 1)

    @pl.when(at_end)
    def _():
        pl.semaphore_wait(barrier, 4)

    @pl.when(jnp.logical_not(at_end))
    def _():
        pl.semaphore_wait(barrier, 5)

    used = [0, 0]

    def remote(src, dst, device):
        index = used[0]
        used[0] += 1
        return pltpu.make_async_remote_copy(
            src_ref=src, dst_ref=dst, send_sem=sent.at[index], recv_sem=got.at[index], device_id=device
        )

    def within(src, dst):
        index = used[1]
        used[1] += 1
        return pltpu.make_async_copy(src, dst, local_sem.at[index])

    count_rows = counts.shape[0]
    around = (section, dp, peers, partner, to_x, to_y)
    counting = spread(remote, counts, counts_all, 0, count_rows, *around)
    count_steps = spread_steps(counting)
    size = genes_sum.shape[0]
    act = pre_out
    theirs = genes_in.at[pl.ds(0, count_dp)]
    from_x, from_y, inbound = (genes_in.at[count_dp + room] for room in range(3))
    swap = remote(grad.at[pl.ds((1 - section) * count_dp, count_dp)], theirs, partner)
    indices = tuple(section * count_dp + index for index in (peers[2], peer_x, peer_y, dp))
    first, second, pass_on, conclude_genes = trade(
        remote, grad, indices, from_x, from_y, inbound, to_x, to_y
    )
    load_genes = [
        within(genes_w.at[pl.ds(index * size, size), :], genes_in.at[index])
        for index in range(genes_in.shape[0])
    ]
    keep_residual = within(residual, rebuilt_out)
    load_pre, load_normed = within(decoder_pre, wide), within(normed, wide)

    def load_cells(part_index, room):
        rows = part_rows(part_index, cells)
        first_row = pl.multiple_of(section * cells + rows.start, 16)
        return pltpu.make_async_copy(
            expression.at[pl.ds(first_row, PART_ROWS), :], cells_in.at[room], cells_sem.at[room]
        )
    fetches = [
        within(src, dst)
        for src, dst in ((dec_w, dec_in), (latent_w, latent_in), (down_w, down_in), (up_w, up_in))
    ]

    load_pre.start()
    for copy in load_genes:
        copy.start()
    for room in range(2):
        load_cells(room, room).start()
    sums_out[...] = jnp.zeros_like(sums_out)
    comps_out[...] = jnp.zeros_like(comps_out)
    def mixture():
        density = sum(density_parts[index] for index in range(count_z))
        logits = density[:comp_count, :] - math.log(comp_count)
        largest = jnp.max(logits, axis=0, keepdims=True)
        log_prior = largest + jnp.log(jnp.sum(jnp.exp(logits - largest), axis=0, keepdims=True))
        respons[...] = jnp.exp(logits - log_prior).T
        info_columns[...] = info[...].T
        kept = info[1:2, :]
        early = (PARTS - 1) * PART_ROWS
        by_part = jnp.concatenate([kept[:, :early], kept[:, cells - PART_ROWS :]], axis=1)
        lane = lax.broadcasted_iota(jnp.int32, by_part.shape, 1)
        repeated = (lane >= early) & (lane < PARTS * PART_ROWS - (cells - early))
        by_part = jnp.where(repeated, 0.0, by_part)
        difference = density[comp_count : comp_count + 1, :] - log_prior
        divergence = jnp.sum(difference * by_part, axis=1, keepdims=True)
        live = jnp.sum(kept, axis=1, keepdims=True)
        line_of = lax.broadcasted_iota(jnp.int32, counts.shape, 0)
        counts[...] = jnp.where(line_of == 0, divergence, live)
        mine = pl.ds(pl.multiple_of((section * count_dp + dp) * count_rows, 8), count_rows)
        counts_all[mine, :] = counts[...]

    def begin():
        mixture()
        count_steps[0]()
        for copy in fetches:
            copy.start()
        load_pre.wait()
        for copy in load_genes:
            copy.wait()

    def count_cells():
        for name in ("own", "relay_x", "relay_y", "relay_upper", "relay_lower"):
            counting[name].wait_recv()
        for copy in fetches:
            copy.wait()
        sums = sum(
            counts_all[index * count_rows : index * count_rows + 8, :]
            for index in range(counts_all.shape[0] // count_rows)
        )
        mean_kl = sums[0:1, :] / (latent_total * sums[1:2, :])
        excess = mean_kl - FREE_BITS
        small = jnp.exp(-jnp.abs(excess))
        above = 1.0 + small
        log_above = jnp.where(above == 1.0, small, jnp.log(above) * (small / (above - 1.0)))
        softplus = jnp.maximum(excess, 0.0) + log_above
        sigmoid = jnp.where(excess >= 0.0, 1.0, small) / above
        kl_scale[0:1, :] = ramp_step[0:1, :] * softplus * sigmoid

    def residual_done():
        for device in (partner, to_x, to_y):
            pl.semaphore_signal(free, inc=1, device_id=device)
        keep_residual.start()
        act_turned[...] = act[...].T

    genes = residual.shape[1]
    whole = genes // TILE

    def grad_tile(span, width):
        tile = mat_nn(act_turned[...], residual[:, span])
        grad[:, :, span] = tile.reshape(grad.shape[0], size, width).astype(BF16)

    def swap_halves():
        if genes % TILE:
            grad_tile(pl.ds(whole * TILE, genes % TILE), genes % TILE)
        pl.semaphore_wait(free, 3)
        swap.start()

    def trade_begins():
        swap.wait_recv()
        mine = pl.ds(section * count_dp, count_dp)
        grad[mine] = (grad[mine].astype(F32) + genes_in[0:count_dp].astype(F32)).astype(BF16)
        for copy in first + second:
            copy.start()

    def rows_of(half):
        return part_rows(half, cells)

    def genes_product(half):
        rows, room = rows_of(half), lax.rem(half, 2)
        weights = genes_in[...].reshape(genes_in.shape[0] * size, genes)
        own_act = gelu(wide[rows, :]).astype(BF16)
        act[rows, :] = own_act
        load_cells(half, room).wait()
        rebuilt = mat_nn(own_act, weights)
        difference = ((rebuilt - cells_in[room].astype(F32)) * info_columns[rows, 1:2]).astype(BF16)
        residual[rows, :] = difference
        part[half] = mat_nt(difference, weights)

        @pl.when(half + 2 < PARTS)
        def _():
            load_cells(half + 2, room).start()

    def latents_back(half):
        rows = rows_of(half)
        pre = (total[half] * gelu_slope(wide[rows, :])).astype(BF16)
        pre_out[rows, :] = pre
        weight = kl_scale[0:1, 0:1] * info_columns[rows, 1:2]
        by_part = pl.ds(pl.multiple_of(half * PART_ROWS, PART_ROWS), PART_ROWS)
        weighted = respons[by_part, :] * weight
        own_latent = latent[rows, :]
        grad_latent = mat_nt(pre, dec_in[...])
        line_of = lax.broadcasted_iota(jnp.int32, weighted.shape, 0)
        repeated = jnp.where(half < PARTS - 1, 0, PARTS * PART_ROWS - cells)
        counted = jnp.where(line_of >= repeated, weighted, 0.0)
        for index in range(comp_count):
            offset = own_latent - centers[index : index + 1, :]
            pulled = offset * jnp.exp(-spreads[index : index + 1, :])
            grad_latent = grad_latent + weighted[:, index : index + 1] * pulled
            share = counted[:, index : index + 1]
            comps_out[index : index + 1, :] -= jnp.sum(share * pulled, axis=0, keepdims=True)
            comps_out[comp_count + index : comp_count + index + 1, :] -= jnp.sum(
                share * (0.5 * offset * pulled - 0.5), axis=0, keepdims=True
            )
        grad_logs = grad_latent * (0.5 * spread_latent[rows, :]) - 0.5 * weight
        stats = jnp.concatenate([grad_latent.astype(BF16), grad_logs.astype(BF16)], axis=1)
        stats_out[rows, :] = stats
        part[half] = mat_nt(stats, latent_in[...])

    def feed_back(half):
        rows = rows_of(half)
        hidden = total[half].astype(BF16)
        hidden_out[rows, :] = hidden
        grad_upper = (mat_nt(hidden, down_in[...]) * gelu_slope(upper[rows, :])).astype(BF16)
        upper_out[rows, :] = grad_upper
        part[half] = mat_nt(grad_upper, up_in[...])

    def conclude(half):
        rows = rows_of(half)
        grad_norm, own_normed = total[half], wide[rows, :]
        grad_middle = hidden_out[rows, :].astype(F32) + norm_back(
            grad_norm, own_normed, scale[rows, :], gain[...]
        )
        middle_out[rows, :] = grad_middle
        low_out[rows, :] = grad_middle.astype(BF16)
        return grad_norm * own_normed, grad_norm

    def conclude_early(half):
        scaled, plain = conclude(half)
        sums_out[0:1, :] += jnp.sum(scaled, axis=0, keepdims=True)
        sums_out[1:2, :] += jnp.sum(plain, axis=0, keepdims=True)

    def produce(moment):
        item = lax.div(moment, spacing)
        half, stage = lax.rem(item, PARTS), lax.div(item, PARTS)
        begins = lax.rem(moment, spacing) == 0
        for number, work in enumerate((genes_product, latents_back, feed_back, conclude_early)):
            pl.when(begins & (stage == number))(functools.partial(work, half))

        tile = moment - TILES_FROM

        @pl.when((tile >= 0) & (tile < whole))
        def _():
            grad_tile(pl.ds(pl.multiple_of(tile * TILE, TILE), TILE), TILE)

    hooks = [
        (0, begin),
        (4, count_steps[1]),
        (6, count_steps[2]),
        (8, count_steps[3]),
        (PARTS * spacing - 3, residual_done),
        (PARTS * spacing, count_cells),
        (TILES_FROM + whole, swap_halves),
        (TILES_FROM + whole + 6, trade_begins),
        (TILES_FROM + whole + 15, pass_on),
        (2 * PARTS * spacing - 1, load_normed.start),
        (3 * PARTS * spacing - 1, load_normed.wait),
    ]
    line_pipe(produce, hooks, 3 * PARTS, spacing, part, total, *line)
    scaled, plain = conclude(PARTS - 1)
    repeated = PARTS * PART_ROWS - cells
    sums_out[0:1, :] += jnp.sum(scaled[repeated:, :], axis=0, keepdims=True)
    sums_out[1:2, :] += jnp.sum(plain[repeated:, :], axis=0, keepdims=True)
    genes_sum[...] = conclude_genes()
    for copy in counting.values():
        copy.wait_send()
    swap.wait_send()
    keep_residual.wait()


def back(number, latent_total, ramp, density_parts, info, decoder_pre, latent, spread_latent, centers,
         spreads, upper, normed, scale, gain, genes_w, dec_w, latent_w, down_w, up_w, expression):
    sections, count_dp, count_z = (lax.axis_size(name) for name in ("section", "dp", "mp"))
    cells, features = decoder_pre.shape
    units, latents = upper.shape[1], latent.shape[1]
    comp_count, count_rows = centers.shape[0], 32
    spacing = pipe_spacing(features // PIECE_COLUMNS, count_z)
    rooms = PARTS * spacing
    vmem, anywhere = pl.BlockSpec(memory_space=pltpu.VMEM), pl.BlockSpec(memory_space=pl.ANY)
    piece = (genes_w.shape[0] // (sections * count_dp), genes_w.shape[1])
    parts = pltpu.VMEM((sections * count_dp,) + piece, BF16)
    buffer = pltpu.VMEM((rooms, PART_ROWS, PIECE_COLUMNS), BF16)
    halves = pltpu.VMEM((PARTS, PART_ROWS, features), F32)
    outputs = [
        ((cells, features), BF16),
        ((cells, 2 * latents), BF16),
        ((2 * comp_count, latents), F32),
        ((cells, features), BF16),
        ((cells, units), BF16),
        ((cells, features), F32),
        ((cells, features), BF16),
        ((8, features), F32),
        (piece, F32),
        ((cells, piece[1]), BF16),
    ]
    copies = 11 + 1 + 6
    results = pl.pallas_call(
        functools.partial(back_kernel, spacing, float(latent_total)),
        out_shape=[jax.ShapeDtypeStruct(*item) for item in outputs],
        in_specs=[vmem] * 10 + [anywhere] * 8,
        out_specs=[vmem] * 9 + [anywhere],
        scratch_shapes=[
            halves,
            halves,
            pltpu.VMEM((cells, features), F32),
            pltpu.VMEM((count_rows, 128), F32),
            pltpu.VMEM((PARTS * PART_ROWS, comp_count), F32),
            pltpu.VMEM((cells, info.shape[0]), F32),
            pltpu.VMEM((sections * count_dp * count_rows, 128), F32),
            pltpu.VMEM((8, 128), F32),
        ]
        + [parts]
        + [pltpu.VMEM(array.shape, BF16) for array in (dec_w, latent_w, down_w, up_w)]
        + [
            pltpu.VMEM((2, PART_ROWS, piece[1]), BF16),
            pltpu.VMEM((cells, piece[1]), BF16),
            pltpu.VMEM((features, cells), BF16),
            parts,
            pltpu.SemaphoreType.DMA((2,)),
            pltpu.SemaphoreType.REGULAR,
        ]
        + [buffer] * 4
        + [pltpu.SemaphoreType.DMA((rooms,))] * 4
        + [
            pltpu.SemaphoreType.DMA((copies,)),
            pltpu.SemaphoreType.DMA((copies,)),
            pltpu.SemaphoreType.DMA((sections * count_dp + 7,)),
        ],
        compiler_params=pltpu.CompilerParams(
            collective_id=number, has_side_effects=True, vmem_limit_bytes=62 * 2**20
        ),
        name="back",
    )(ramp, density_parts, info, latent, spread_latent, centers, spreads, upper, scale, gain, decoder_pre, normed,
      genes_w, dec_w, latent_w, down_w, up_w, expression)
    return results


def meet(tiled, number, reduce=None, gathers=(), swaps=(), exchanges=(), shares=(), pairs=()):
    if tiled:
        return comm(number, reduce, gathers, swaps, exchanges, shares, pairs)
    partner = [(i, 1 - i) for i in range(2)]
    section, count_dp = lax.axis_index("section"), lax.axis_size("dp")
    swapped = []
    for array, axis in swaps:
        size = array.shape[axis] // 2
        half = lax.dynamic_slice_in_dim(array, (1 - section) * size, size, axis)
        swapped.append(lax.ppermute(half, "section", partner))
    exchanged = []
    for array, other, axis in exchanges:
        if other is not None:
            array = half_sum(array, other, axis)
        parts = lax.all_to_all(jnp.stack(jnp.split(array, count_dp, axis)), "dp", 0, 0)
        exchanged.append(total(parts))
    return [
        [] if reduce is None else comm(number, reduce)[0][0:1],
        [lax.all_gather(shard, ("section", "dp"), axis=axis, tiled=True) for shard, axis in gathers],
        swapped,
        exchanged,
        [lax.all_gather(array, "mp") for array in shares],
        [lax.ppermute(array, "section", partner) for array in pairs],
    ]


def half_sum(array, received, axis):
    size = received.shape[axis]
    own = lax.dynamic_slice_in_dim(array, lax.axis_index("section") * size, size, axis)
    return (own.astype(F32) + received.astype(F32)).astype(array.dtype)


def total(parts):
    return jnp.sum(parts.astype(F32), axis=0)


def local(
    expression,
    cell_xy,
    live_mask,
    lengths,
    ramp_step,
    latent_noise,
    gene_embed,
    ln1_gain,
    ln1_bias,
    w_query,
    w_key,
    w_value,
    w_out,
    ln2_gain,
    ln2_bias,
    w_up,
    w_down,
    w_mean,
    w_logvar,
    comp_mean,
    comp_logvar,
    w_dec,
    w_genes,
):
    micro_count = lengths.shape[0]
    cells = expression.shape[0] // micro_count
    micro = lax.axis_index("section")
    latent_cols = w_mean.shape[1]
    comp_count, comp_width = comp_mean.shape
    width = ln1_gain.shape[0]
    shards = 2 * lax.axis_size("dp")
    features = shards * width
    tiled = width % 128 == 0 and lax.axis_size("dp") == 4
    meeting = functools.partial(meet, tiled)

    def own(array, axis=0):
        return lax.dynamic_slice_in_dim(array, micro * cells, cells, axis)

    alive = own(live_mask)
    alive_float = alive.astype(F32)
    noise = own(latent_noise)
    slide = slide_ids(lax.dynamic_index_in_dim(lengths, micro, 0, False), cells)
    info = jnp.pad(jnp.stack([slide.astype(F32), alive_float]), ((0, 6), (0, 0)))

    norm_block = jnp.pad(jnp.stack([ln1_gain, ln1_bias, ln2_gain, ln2_bias]), ((0, 12), (0, 0)))
    comp_block = jnp.pad(
        jnp.concatenate([comp_mean, comp_logvar], axis=0), ((0, 0), (0, width - comp_width))
    )
    small = jnp.concatenate([norm_block, comp_block], axis=0)
    small_rows = small.shape[0]
    qkv_shard = jnp.concatenate([w_query, w_key, w_value], axis=1)
    places = own(cell_xy, 1)
    weights = ((small, 0), (qkv_shard, 0), (w_out, 1))
    if tiled:
        start, embed, (small_all, qkv, out_w) = head(
            0, places.T, expression, gene_embed, weights
        )
    else:
        _, (embed, small_all, qkv, out_w), _, _, _, _ = meeting(
            0, gathers=((gene_embed, 1),) + weights
        )
        (summed,), _, _, _, _, _ = meeting(1, (expression, embed, False, True))
        start = summed + position_code(places, features)
    small_all = small_all.reshape(shards, small_rows, width).astype(F32)
    norm_params = small_all[:, :4].transpose(1, 0, 2).reshape(4, features)
    gain_one, bias_one, gain_two, bias_two = (norm_params[i : i + 1] for i in range(4))
    comps = small_all[:, 16:, :comp_width].transpose(1, 0, 2).reshape(2 * comp_count, -1)
    centers, spreads = comps[:comp_count], comps[comp_count:]

    latent_shard = jnp.concatenate([w_mean, w_logvar], axis=1)
    precision = jnp.exp(-spreads)
    if tiled:
        states, (up_w, down_w, latent_w, dec_w, genes_w), attention = middle(
            1,
            start,
            (gain_one, bias_one),
            qkv,
            info,
            gain_two,
            bias_two,
            out_w,
            noise,
            centers,
            spreads,
            ((w_up, 0), (w_down, 1), (latent_shard, 0), (w_dec, 1), (w_genes, 0)),
        )
        (normed_two, scale_two, second_low, upper, activated, hidden, log_vars, latent, spread_latent,
         latent_low, decoder_pre, density_parts) = states
        normed_one, scale_one, first_low, projected, attended, log_totals = attention
    else:
        normed_one, scale_one, first_low, projected, attended, log_totals = attend(
            start, gain_one, bias_one, qkv, info
        )
        (summed,), (up_w, down_w, latent_w, dec_w), _, _, _, _ = meeting(
            2, (attended, out_w, False, False), gathers=((w_up, 0), (w_down, 1), (latent_shard, 0), (w_dec, 1))
        )
        after_attn = start + summed
        normed_two, scale_two = normalize(after_attn)
        second_low = (normed_two * gain_two + bias_two).astype(BF16)
        upper = mat_nn(second_low, up_w)
        activated = gelu(upper).astype(BF16)
        (summed,), (genes_w,), _, _, _, _ = meeting(
            3, (activated, down_w, False, False), gathers=((w_genes, 0),)
        )
        hidden = (after_attn + summed).astype(BF16)

        stats = mat_nn(hidden, latent_w)
        means, log_vars = stats[:, :latent_cols], stats[:, latent_cols:]
        spread_latent = jnp.exp(0.5 * log_vars) * noise
        latent = means + spread_latent
        latent_low = latent.astype(BF16)
        post_part = jnp.sum(-0.5 * LOG_TWO_PI - 0.5 * log_vars - 0.5 * noise * noise, axis=1)
        offsets = latent[None] - centers[:, None, :]
        pulled = offsets * precision[:, None, :]
        comp_part = jnp.sum(
            -0.5 * LOG_TWO_PI - 0.5 * spreads[:, None, :] - 0.5 * offsets * pulled, axis=2
        )
        density_part = jnp.pad(
            jnp.concatenate([comp_part, post_part[None]], axis=0), ((0, 7), (0, -cells % 128))
        )
        (decoder_pre,), _, _, _, (density_parts,), _ = meeting(
            4, (latent_low, dec_w, False, False), shares=(density_part,)
        )
        densities = jnp.sum(density_parts, axis=0)[:, :cells]
        logits = densities[:comp_count] - math.log(comp_count)
        log_post = densities[comp_count]
        largest = jnp.max(logits, axis=0, keepdims=True)
        log_prior = largest[0] + jnp.log(jnp.sum(jnp.exp(logits - largest), axis=0))
        respons = jnp.exp(logits - log_prior[None, :])
        divergence = jnp.sum((log_post - log_prior) * alive_float)
        counts = jnp.concatenate(
            [jnp.full((1, 128), divergence), jnp.full((31, 128), jnp.sum(alive_float))], axis=0
        )

    ramp_weight = jnp.minimum(1.0, (ramp_step[0] + 1).astype(F32) / RAMP)
    if tiled:
        (grad_pre, grad_stats, grad_comps, grad_hidden, grad_upper, grad_middle, middle_low, norm_sums,
         genes_parts, grad_rebuilt) = back(
            2,
            LATENT,
            jnp.full((8, 128), ramp_weight),
            density_parts,
            info,
            decoder_pre,
            latent,
            spread_latent,
            centers,
            spreads,
            upper,
            normed_two,
            scale_two,
            gain_two,
            genes_w,
            dec_w,
            latent_w,
            down_w,
            up_w,
            expression,
        )
        grad_dec = mat_tn(latent_low, grad_pre).astype(BF16)
        grad_latent_w = mat_tn(hidden, grad_stats).astype(BF16)
        grad_down = mat_tn(activated, grad_hidden).astype(BF16)
        grad_up = mat_tn(second_low, grad_upper).astype(BF16)
    else:
        grad_rebuilt, grad_genes = decode(micro, decoder_pre, genes_w, expression, alive_float)
        (grad_act,), (count_parts,), (genes_other,), _, _, _ = meeting(
            5, (grad_rebuilt, genes_w, True, False), gathers=((counts, 0),), swaps=((grad_genes, 0),)
        )
        count_parts = jnp.sum(count_parts.reshape(shards, 32, 128)[:, :, 0], axis=0)
        mean_kl = count_parts[0] / (LATENT * count_parts[1])
        kl_scale = (
            ramp_weight * jax.nn.softplus(mean_kl - FREE_BITS) * jax.nn.sigmoid(mean_kl - FREE_BITS)
        )
        grad_pre = (grad_act * gelu_slope(decoder_pre)).astype(BF16)
        grad_dec = mat_tn(latent_low, grad_pre).astype(BF16)
        cell_weight = kl_scale * alive_float
        weighted = (respons * cell_weight[None, :])[:, :, None]
        grad_latent = mat_nt(grad_pre, dec_w) + jnp.sum(weighted * pulled, axis=0)
        grad_means = grad_latent.astype(BF16)
        grad_logs = (grad_latent * (0.5 * spread_latent) - 0.5 * cell_weight[:, None]).astype(BF16)
        grad_stats = jnp.concatenate([grad_means, grad_logs], axis=1)
        grad_latent_w = mat_tn(hidden, grad_stats).astype(BF16)
        (summed,), _, (latent_other, dec_other), (genes_parts,), _, _ = meeting(
            6,
            (grad_stats, latent_w, True, False),
            swaps=((grad_latent_w, 0), (grad_dec, 1)),
            exchanges=((grad_genes, genes_other, 0),),
        )
        grad_hidden = summed.astype(BF16)

        grad_down = mat_tn(activated, grad_hidden).astype(BF16)
        grad_upper = (mat_nt(grad_hidden, down_w) * gelu_slope(upper)).astype(BF16)
        grad_up = mat_tn(second_low, grad_upper).astype(BF16)
        (grad_norm_two,), _, (down_other, up_other), _, _, _ = (
            meeting(
                7,
                (grad_upper, up_w, True, False),
                swaps=((grad_down, 1), (grad_up, 0)),
            )
        )
        grad_middle = grad_hidden.astype(F32) + norm_back(
            grad_norm_two, normed_two, scale_two, gain_two
        )
        middle_low = grad_middle.astype(BF16)
        norm_sums = [jnp.sum(grad_norm_two * normed_two, axis=0), jnp.sum(grad_norm_two, axis=0)]
        grad_comps = jnp.concatenate(
            [
                -jnp.sum(weighted * pulled, axis=1),
                -jnp.sum(weighted * (0.5 * offsets * pulled - 0.5), axis=1),
            ],
            axis=0,
        )
    grad_out = mat_tn(attended, middle_low).astype(BF16)
    if tiled:
        grad_qkv_act, (down_other, up_other, latent_other, dec_other) = attend_back(
            3,
            middle_low,
            out_w,
            projected,
            log_totals,
            info,
            ((grad_down, 1), (grad_up, 0), (grad_latent_w, 0), (grad_dec, 1)),
        )
    else:
        grad_qkv_act, _ = attend_back(
            11, middle_low, out_w, projected, log_totals, info, ()
        )
    grad_qkv = mat_tn(first_low, grad_qkv_act).astype(BF16)
    (grad_norm_one,), _, (qkv_other, out_other), (down_parts, up_parts, latent_parts, dec_parts), _, _ = meeting(
        8,
        (grad_qkv_act, qkv, True, False),
        swaps=((grad_qkv, 0), (grad_out, 1)),
        exchanges=(
            (grad_down, down_other, 1),
            (grad_up, up_other, 0),
            (grad_latent_w, latent_other, 0),
            (grad_dec, dec_other, 1),
        ),
    )
    grad_start = grad_middle + norm_back(grad_norm_one, normed_one, scale_one, gain_one)
    start_low = grad_start.astype(BF16)

    norm_grads = jnp.stack(
        [
            jnp.sum(grad_norm_one * normed_one, axis=0),
            jnp.sum(grad_norm_one, axis=0),
            norm_sums[0],
            norm_sums[1],
        ]
    )
    norm_grads = norm_grads.reshape(4, shards, width).transpose(1, 0, 2)
    comp_grads = grad_comps.reshape(2 * comp_count, shards, comp_width).transpose(1, 0, 2)
    small_grads = jnp.concatenate(
        [
            jnp.pad(norm_grads, ((0, 0), (0, 12), (0, 0))),
            jnp.pad(comp_grads, ((0, 0), (0, 0), (0, width - comp_width))),
        ],
        axis=1,
    ).reshape(shards * small_rows, width)
    if tiled:
        embed_parts, qkv_parts, out_parts, small_sum, grad_expression = tail(
            9,
            start_low,
            expression,
            embed,
            grad_rebuilt,
            grad_qkv,
            qkv_other,
            grad_out,
            out_other,
            small_grads.reshape(2, shards // 2, small_rows, width),
        )
    else:
        start_all = lax.all_gather(start_low, "section", axis=0, tiled=True)
        start_half = lax.dynamic_slice_in_dim(start_all, micro * (features // 2), features // 2, 1)
        grad_embed = mat_tn(expression, start_half).astype(BF16)
        grad_cells = (
            mat_nt(start_low, embed).astype(BF16).astype(F32) - grad_rebuilt.astype(F32)
        ).astype(BF16)
        grad_expression = lax.all_gather(grad_cells, "section", axis=0, tiled=True)
        small_other = lax.ppermute(
            lax.dynamic_slice_in_dim(
                small_grads, (1 - micro) * (shards // 2 * small_rows), shards // 2 * small_rows, 0
            ),
            "section",
            [(0, 1), (1, 0)],
        )
        _, _, _, (embed_parts, qkv_parts, out_parts, small_sum), _, _ = meeting(
            9,
            exchanges=(
                (grad_embed, None, 1),
                (grad_qkv, qkv_other, 0),
                (grad_out, out_other, 1),
                (small_grads, small_other, 0),
            ),
        )
    grad_query, grad_key, grad_value = jnp.split(qkv_parts, 3, axis=1)
    grad_mean, grad_logvar = jnp.split(latent_parts, 2, axis=1)
    return (
        embed_parts,
        small_sum[0],
        small_sum[1],
        grad_query,
        grad_key,
        grad_value,
        out_parts,
        small_sum[2],
        small_sum[3],
        up_parts,
        down_parts,
        grad_mean,
        grad_logvar,
        small_sum[16 : 16 + comp_count, :comp_width],
        small_sum[16 + comp_count :, :comp_width],
        dec_parts,
        genes_parts,
        grad_expression,
    )


def solution(mesh):
    weight_rows = P(("section", "dp"), "mp")
    weight_cols = P("mp", ("section", "dp"))
    vector = P(("section", "dp"))
    comps = P(None, ("mp", "section", "dp"))
    weights = (
        weight_cols, vector, vector, weight_rows, weight_rows, weight_rows, weight_cols,
        vector, vector, weight_rows, weight_cols, weight_rows, weight_rows, comps, comps,
        weight_cols, weight_rows,
    )
    return jax.shard_map(
        local,
        mesh=mesh,
        in_specs=(P("dp", "mp"), P(None, "dp"), P("dp"), P("dp", None), P(), P("dp", "mp"))
        + weights,
        out_specs=weights + (P("dp", "mp"),),
        check_vma=False,
    )
```
